128 devices in a mesh: branch: 32 (over z, x, core), tensor: 4 (over y).
Axes of the slice: x: 4, y: 4, z: 4, core: 2. Of those that a mesh axis runs over, the one named last changes fastest.
Arguments:
- inputs: bfloat16 [4, 512, 2048], P(None, 'branch'), may hold values from -6 to 6
- w_query: bfloat16 [2048, 2048], P(None, 'tensor'), may hold values from -0.125 to 0.125
- w_key: bfloat16 [2048, 2048], P(None, 'tensor'), may hold values from -0.125 to 0.125
- w_value: bfloat16 [2048, 4096], P(None, 'tensor'), may hold values from -0.125 to 0.125
- w_gate_z: bfloat16 [2048, 4096], P(None, 'tensor'), may hold values from -0.125 to 0.125
- w_beta: bfloat16 [2048, 32], P(None, 'tensor'), may hold values from -0.125 to 0.125
- w_decay: bfloat16 [2048, 32], P(None, 'tensor'), may hold values from -0.125 to 0.125
- conv_query: bfloat16 [4, 2048], P(None, 'tensor'), may hold values from -3 to 3
- conv_key: bfloat16 [4, 2048], P(None, 'tensor'), may hold values from -3 to 3
- conv_value: bfloat16 [4, 4096], P(None, 'tensor'), may hold values from -3 to 3
- decay_log: float32 [32], P('tensor'), may hold values from -3 to 1
- dt_bias: float32 [32], P('tensor'), may hold values from -1 to 1
- norm_gain: float32 [128], replicated, may hold values from 0.1 to 1.9
- w_out: bfloat16 [4096, 2048], P('tensor'), may hold values from -0.09375 to 0.09375
- state: bfloat16 [512, 32, 128, 128], P('branch', 'tensor'), may hold values from -4 to 4
- tail_query: bfloat16 [512, 3, 2048], P('branch', None, 'tensor'), may hold values from -6 to 6
- tail_key: bfloat16 [512, 3, 2048], P('branch', None, 'tensor'), may hold values from -6 to 6
- tail_value: bfloat16 [512, 3, 4096], P('branch', None, 'tensor'), may hold values from -6 to 6
- parents: int32 [512], P('branch'), may hold values from 0 to 511, as said below
Outputs:
- out_rows: bfloat16 [4, 512, 2048], P(None, 'branch', 'tensor')
- final_state: bfloat16 [512, 32, 128, 128], P('branch', 'tensor')
- final_tail_query: bfloat16 [512, 3, 2048], P('branch', None, 'tensor')
- final_tail_key: bfloat16 [512, 3, 2048], P('branch', None, 'tensor')
- final_tail_value: bfloat16 [512, 3, 4096], P('branch', None, 'tensor')
The draws below stay inside these ranges and needn't reach their ends.
Inputs may be any that keep to these rules, and one draw needn't show every extreme that they name: `parents`: for every aligned block of 16 branches and every block of 16 branches, either none or exactly 1 of the first block's branches have their parent in the second block.
All inputs are finite; a program needn't handle non-finite values.
Results may differ from the reference program's by a relative error of at most 0.0059.
Values may be sent and summed in bfloat16 or wider, within the bound.
No kernel may reach another device: no remote copies, remote signals or barrier semaphores. Data moves between devices by JAX's collectives and lax.ppermute only.
A program may use at most 128 MiB of HBM per device.

```python
import math
import jax
import jax.numpy as jnp
from jax import lax

D = 2048
KH = 16
VH = 32
DK = 128
DV = 128
KSIZE = 4
STEPS = 4
B_DEV = 16
BRANCHES = 512


def draw_parents(key, part):
    key = jax.random.fold_in(key, 7)
    blocks = BRANCHES // B_DEV
    per_pair = max(1, 2 * B_DEV // blocks)
    sources = B_DEV // per_pair
    key_hot, key_score, key_local, key_shuffle = jax.random.split(key, 4)
    hotness = jax.random.randint(key_hot, (blocks,), 1, 9)
    scores = jax.random.randint(key_score, (blocks, blocks), 0, 4096) * hotness[None, :]
    scores = scores * blocks + jnp.arange(blocks, dtype=jnp.int32)[None, :]
    ignored, chosen = lax.top_k(scores, sources)
    source_rows = jnp.repeat(chosen, per_pair, axis=1)
    local_rows = jax.random.randint(key_local, (blocks, B_DEV), 0, B_DEV)
    shuffle_keys = jax.random.randint(key_shuffle, (blocks, B_DEV), 0, 1 << 20) * B_DEV + jnp.arange(B_DEV, dtype=jnp.int32)[None, :]
    shuffle = jnp.argsort(shuffle_keys, axis=1)
    source_rows = jnp.take_along_axis(source_rows, shuffle, axis=1)
    return (source_rows * B_DEV + local_rows).reshape(-1).astype(jnp.int32)


def level_of(key, shape, cuts, low, high):
    loudness = 1.0
    for dim, blocks in cuts:
        steps = jax.random.uniform(jax.random.fold_in(jax.random.fold_in(key, 6), dim), (blocks,), jnp.float32, low / len(cuts), high / len(cuts))
        loudness = loudness * jnp.repeat(jnp.exp(steps), shape[dim] // blocks).reshape((-1,) + (1,) * (len(shape) - 1 - dim))
    return loudness


def bell_draw(stream_key, dims, scale, bound, cuts=(), kind=jnp.bfloat16):
    level = level_of(stream_key, dims, cuts, -0.22, 0.18) if cuts else 1.0
    result = jax.random.normal(stream_key, dims, jnp.float32) * scale * level
    return jnp.minimum(jnp.maximum(result, -bound), bound).astype(kind)


def setup_inputs(seed: int = 0) -> dict:
    splits = jax.random.split(jax.random.key(seed), 20)
    return {
        "inputs": bell_draw(splits[0], (STEPS, BRANCHES, D), 1.0, 6.0, ((1, 32),)),
        "w_query": bell_draw(splits[1], (D, KH * DK), D ** -0.5, 0.125, ((1, 4),)),
        "w_key": bell_draw(splits[2], (D, KH * DK), D ** -0.5, 0.125, ((1, 4),)),
        "w_value": bell_draw(splits[3], (D, VH * DV), D ** -0.5, 0.125, ((1, 4),)),
        "w_gate_z": bell_draw(splits[4], (D, VH * DV), D ** -0.5, 0.125, ((1, 4),)),
        "w_beta": bell_draw(splits[5], (D, VH), D ** -0.5, 0.125, ((1, 4),)),
        "w_decay": bell_draw(splits[6], (D, VH), D ** -0.5, 0.125, ((1, 4),)),
        "conv_query": bell_draw(splits[7], (KSIZE, KH * DK), 0.5, 3.0, ((1, 4),)),
        "conv_key": bell_draw(splits[8], (KSIZE, KH * DK), 0.5, 3.0, ((1, 4),)),
        "conv_value": bell_draw(splits[9], (KSIZE, VH * DV), 0.5, 3.0, ((1, 4),)),
        "decay_log": jnp.clip(-3.0 + 4.0 * jax.random.uniform(splits[10], (VH,), jnp.float32) ** level_of(splits[10], (VH,), ((0, 4),), -0.2, 0.2), -3.0, 1.0),
        "dt_bias": jnp.clip(jax.random.uniform(splits[11], (VH,), jnp.float32, -1.0, 1.0) * level_of(splits[11], (VH,), ((0, 4),), -0.4, 0.0), -1.0, 1.0),
        "norm_gain": jnp.clip(1.0 + 0.18 * jax.random.normal(splits[12], (DV,), jnp.float32), 0.1, 1.9),
        "w_out": bell_draw(splits[13], (VH * DV, D), (VH * DV) ** -0.5, 0.09375, ((0, 4),)),
        "state": bell_draw(splits[14], (BRANCHES, VH, DK, DV), 0.5, 4.0, ((0, 32), (1, 4))),
        "tail_query": bell_draw(splits[15], (BRANCHES, KSIZE - 1, KH * DK), 1.0, 6.0, ((0, 32), (2, 4))),
        "tail_key": bell_draw(splits[16], (BRANCHES, KSIZE - 1, KH * DK), 1.0, 6.0, ((0, 32), (2, 4))),
        "tail_value": bell_draw(splits[17], (BRANCHES, KSIZE - 1, VH * DV), 1.0, 6.0, ((0, 32), (2, 4))),
        "parents": draw_parents(jax.random.fold_in(splits[19], 71), 0),
    }


def unit_rows(head_block):
    return head_block * lax.rsqrt(lax.optimization_barrier(jnp.sum(head_block * head_block, axis=-1, keepdims=True)) + 1e-06)

def convolve(history, new_entry, weights):
    kernel = weights.astype(jnp.float32)
    window = jnp.concatenate([history, new_entry[:, None, :]], axis=1)
    blended = lax.optimization_barrier(jnp.sum(window.astype(jnp.float32) * kernel[None], axis=1))
    return (jax.nn.silu(blended), window[:, 1:])

def advance(token_rows, state_carry, params):
    memory, tail_q, tail_k, tail_v = state_carry
    w_query, w_key, w_value, w_gate_z, w_beta, w_decay, conv_query, conv_key, conv_value, decay_log, dt_bias, norm_gain, w_out = params
    row_count = token_rows.shape[0]
    key_heads = w_query.shape[1] // DK
    value_heads = w_value.shape[1] // DV
    new_query = jnp.dot(token_rows, w_query, preferred_element_type=jnp.float32).astype(jnp.bfloat16)
    new_key = jnp.dot(token_rows, w_key, preferred_element_type=jnp.float32).astype(jnp.bfloat16)
    new_value = jnp.dot(token_rows, w_value, preferred_element_type=jnp.float32).astype(jnp.bfloat16)
    gate_z = jnp.dot(token_rows, w_gate_z, preferred_element_type=jnp.float32)
    beta_raw = jnp.dot(token_rows, w_beta, preferred_element_type=jnp.float32)
    decay_raw = jnp.dot(token_rows, w_decay, preferred_element_type=jnp.float32)
    query_conv, tail_q = convolve(tail_q, new_query, conv_query)
    key_conv, tail_k = convolve(tail_k, new_key, conv_key)
    value_conv, tail_v = convolve(tail_v, new_value, conv_value)
    query_full = jnp.repeat(unit_rows(query_conv.reshape(row_count, key_heads, DK)) * DK ** (-0.5), 2, axis=1)
    key_full = jnp.repeat(unit_rows(key_conv.reshape(row_count, key_heads, DK)), 2, axis=1)
    values = value_conv.reshape(row_count, value_heads, DV)
    strength = jax.nn.sigmoid(beta_raw)
    forget_log = -jnp.exp(decay_log) * jax.nn.softplus(decay_raw + dt_bias)
    memory = memory * jnp.exp(forget_log)[:, :, None, None]
    recalled = jnp.einsum('rhk,rhkv->rhv', key_full, memory, precision=lax.Precision.HIGHEST)
    correction = (values - recalled) * strength[:, :, None]
    memory = memory + key_full[:, :, :, None] * correction[:, :, None, :]
    readout = jnp.einsum('rhk,rhkv->rhv', query_full, memory, precision=lax.Precision.HIGHEST)
    scale_inv = lax.rsqrt(lax.optimization_barrier(jnp.mean(readout * readout, axis=-1, keepdims=True)) + 1e-06)
    normed = readout * scale_inv * norm_gain * jax.nn.silu(gate_z.reshape(row_count, value_heads, DV))
    flat_heads = normed.reshape(row_count, value_heads * DV).astype(jnp.bfloat16)
    partial_sum = jnp.dot(flat_heads, w_out, preferred_element_type=jnp.float32)
    return (partial_sum, (memory, tail_q, tail_k, tail_v))

def run_steps(step_inputs, state_carry, params):
    results = []
    for index in range(step_inputs.shape[0]):
        partial_sum, state_carry = advance(step_inputs[index], state_carry, params)
        results.append(partial_sum)
    return (jnp.stack(results).astype(jnp.bfloat16), state_carry)

def reference(inputs, w_query, w_key, w_value, w_gate_z, w_beta, w_decay, conv_query, conv_key, conv_value, decay_log, dt_bias, norm_gain, w_out, state, tail_query, tail_key, tail_value, parents):
    params = (w_query, w_key, w_value, w_gate_z, w_beta, w_decay, conv_query, conv_key, conv_value, decay_log, dt_bias, norm_gain, w_out)
    width = math.gcd(BRANCHES, 64)
    blocks = BRANCHES // width

    def split_rows(array):
        return array.reshape((blocks, width) + array.shape[1:])

    def split_steps(array):
        return array.reshape(array.shape[0], blocks, width, D).transpose(1, 0, 2, 3)

    def join_steps(array):
        return array.transpose(1, 0, 2, 3).reshape(array.shape[1], BRANCHES, D)

    def first_half(pieces):
        rows_in, memory_in, tail_q, tail_k, tail_v = pieces
        sums, carried = run_steps(rows_in, (memory_in.astype(jnp.float32), tail_q, tail_k, tail_v), params)
        return (sums, carried[0].astype(jnp.bfloat16), carried[1], carried[2], carried[3])
    first_sums, mid_memory, mid_q, mid_k, mid_v = lax.map(first_half, (split_steps(inputs[:2]), split_rows(state), split_rows(tail_query), split_rows(tail_key), split_rows(tail_value)))
    mid_memory = lax.optimization_barrier(mid_memory.reshape((BRANCHES,) + mid_memory.shape[2:]))
    chosen = parents.astype(jnp.int32)
    picked_memory = jnp.take(mid_memory, chosen, axis=0)
    picked_q = jnp.take(mid_q.reshape((BRANCHES,) + mid_q.shape[2:]), chosen, axis=0)
    picked_k = jnp.take(mid_k.reshape((BRANCHES,) + mid_k.shape[2:]), chosen, axis=0)
    picked_v = jnp.take(mid_v.reshape((BRANCHES,) + mid_v.shape[2:]), chosen, axis=0)
    picked_memory = lax.optimization_barrier(picked_memory)

    def second_half(pieces):
        rows_in, memory_in, tail_q, tail_k, tail_v = pieces
        sums, carried = run_steps(rows_in, (memory_in.astype(jnp.float32), tail_q, tail_k, tail_v), params)
        return (sums, carried[0].astype(jnp.bfloat16), carried[1], carried[2], carried[3])
    second_sums, last_memory, last_q, last_k, last_v = lax.map(second_half, (split_steps(inputs[2:]), split_rows(picked_memory), split_rows(picked_q), split_rows(picked_k), split_rows(picked_v)))
    out_rows = jnp.concatenate([join_steps(first_sums), join_steps(second_sums)], axis=0)
    return (out_rows, last_memory.reshape((BRANCHES,) + last_memory.shape[2:]), last_q.reshape((BRANCHES,) + last_q.shape[2:]), last_k.reshape((BRANCHES,) + last_k.shape[2:]), last_v.reshape((BRANCHES,) + last_v.shape[2:]))
```

```python
import functools

import jax
import jax.numpy as jnp
from jax import lax
from jax.experimental import pallas as pl
from jax.experimental.pallas import tpu as pltpu
from jax.sharding import PartitionSpec as P

DK = 128
DV = 128
HEADS = 8
KEYS = 4
ROWS = 16
TAPS = 4
WIDE = 3 * HEADS
SLIM = 2 * KEYS + HEADS
BODY = HEADS * DK
SLOT = BODY + (TAPS - 1) * SLIM
VMEM_BYTES = 48 * 1024 * 1024
f32 = jnp.float32
bf16 = jnp.bfloat16


def split(value):
    high = value.astype(bf16).astype(f32)
    return high, value - high


def dot(left, right):
    return jnp.dot(left, right, preferred_element_type=f32)


def widening():
    row = lax.broadcasted_iota(jnp.int32, ((TAPS - 1) * WIDE, (TAPS - 1) * SLIM), 0)
    column = lax.broadcasted_iota(jnp.int32, ((TAPS - 1) * WIDE, (TAPS - 1) * SLIM), 1)
    tap, place = row // WIDE, row % WIDE
    origin = tap * SLIM + jnp.where(place < 2 * HEADS, place // 2, place - HEADS)
    return jnp.where(origin == column, 1.0, 0.0).astype(bf16)


def recall_row(tails, new_rows, conv, strengths, decays, gates, memory):
    window = [tails[i * WIDE : (i + 1) * WIDE] for i in range(TAPS - 1)] + list(new_rows)
    queries, keys, values = [], [], []
    for step in range(2):
        mixed = window[step] * conv[0:WIDE]
        for tap in range(1, TAPS):
            mixed = mixed + window[step + tap] * conv[tap * WIDE : (tap + 1) * WIDE]
        mixed = mixed * jax.nn.sigmoid(mixed)
        units = mixed[: 2 * HEADS]
        units = units * lax.rsqrt(jnp.sum(units * units, axis=-1, keepdims=True) + 1e-06)
        queries.append(units[:HEADS] * DK ** (-0.5))
        keys.append(units[HEADS:])
        values.append(mixed[2 * HEADS :])
    vectors = jnp.concatenate([keys[0], queries[0], keys[1], queries[1]], axis=0)
    high, low = split(vectors)
    high, low = high.astype(bf16), low.astype(bf16)
    head = lax.broadcasted_iota(jnp.int32, (HEADS, DV), 0)
    found = [jnp.zeros((HEADS, DV), f32)] * 4
    for h in range(HEADS):
        product = dot(high, memory(h)) + dot(low, memory(h))
        found = [
            jnp.where(head == h, product[i * HEADS : (i + 1) * HEADS], found[i]) for i in range(4)
        ]

    def inner(left, right):
        return jnp.sum(left * right, axis=-1, keepdims=True)

    decay0, decay1 = decays
    change0 = (values[0] - decay0 * found[0]) * strengths[0]
    read0 = decay0 * found[1] + inner(queries[0], keys[0]) * change0
    change1 = (
        values[1] - decay1 * (decay0 * found[2] + inner(keys[1], keys[0]) * change0)
    ) * strengths[1]
    read1 = (
        decay1 * (decay0 * found[3] + inner(queries[1], keys[0]) * change0)
        + inner(queries[1], keys[1]) * change1
    )
    normed = [
        read * lax.rsqrt(jnp.mean(read * read, axis=-1, keepdims=True) + 1e-06) * gate
        for read, gate in zip((read0, read1), gates)
    ]
    update = jnp.concatenate(
        [keys[0], keys[1], decay1 * change0, change1, decay0 * decay1], axis=0
    )
    return normed, update


def write_row(update, memory, store):
    key0, key1, change0, change1, decay = [
        update[i * HEADS : (i + 1) * HEADS] for i in range(5)
    ]
    (key0h, key0l), (key1h, key1l) = split(key0), split(key1)
    (change0h, change0l), (change1h, change1l) = split(change0), split(change1)
    left = jnp.concatenate([key0h, key0l, key0h, key1h, key1l, key1h], axis=0)
    left = left.T.astype(bf16)
    right = jnp.concatenate([change0h, change0h, change0l, change1h, change1h, change1l], axis=0)
    head = lax.broadcasted_iota(jnp.int32, right.shape, 0) % HEADS
    for h in range(HEADS):
        added = dot(left, jnp.where(head == h, right, 0.0).astype(bf16))
        store(h, (memory(h).astype(f32) * decay[h : h + 1] + added).astype(bf16))


def rows_at(ref, start, count):
    return ref[pl.ds(pl.multiple_of(start, 8), count), :]


def first_kernel(
    x_ref, tails_ref, conv_ref, decay_ref, bias_ref, gain_ref,
    w_query, w_key, w_value, w_gate, w_beta, w_decay, state,
    new_ref, gate_ref, strength_ref, forget_ref, raw_ref, normed_ref, update_ref,
    query_buf, key_buf, value_buf, gate_buf, beta_buf, decay_buf, state_buf,
    new_all, gate_all, strength_all, forget_all, normed_all,
    weight_sem, state_sem,
):
    steps = x_ref.shape[0] // ROWS
    rows = steps * ROWS
    copies = []
    small = [
        pltpu.make_async_copy(w_beta, beta_buf, weight_sem.at[4 * KEYS]),
        pltpu.make_async_copy(w_decay, decay_buf, weight_sem.at[4 * KEYS + 1]),
    ]
    for copy in small:
        copy.start()
    for j in range(KEYS):
        for i, (hbm, buf, width) in enumerate(
            (
                (w_query, query_buf, DK),
                (w_key, key_buf, DK),
                (w_value, value_buf, 2 * DV),
                (w_gate, gate_buf, 2 * DV),
            )
        ):
            part = pl.ds(j * width, width)
            copy = pltpu.make_async_copy(hbm.at[:, part], buf.at[:, part], weight_sem.at[4 * j + i])
            copy.start()
            copies.append(copy)
    states = [
        pltpu.make_async_copy(state.at[row], state_buf.at[row], state_sem.at[row])
        for row in range(ROWS)
    ]
    for copy in states:
        copy.start()

    x = x_ref[...]
    for copy in small:
        copy.wait()
    beta, decay = dot(x, beta_buf[...]), dot(x, decay_buf[...])
    for h in range(HEADS):
        strength_all[pl.ds(h, rows, stride=HEADS), :] = jnp.broadcast_to(beta[:, h : h + 1], (rows, DV))
        forget_all[pl.ds(h, rows, stride=HEADS), :] = jnp.broadcast_to(decay[:, h : h + 1], (rows, DV))
    strength_all[...] = jax.nn.sigmoid(strength_all[...])
    raised = forget_all[...].reshape(rows, HEADS, DV) + bias_ref[...][None]
    forget = -jnp.exp(decay_ref[...])[None] * jax.nn.softplus(raised)
    forget_all[...] = jnp.exp(forget).reshape(rows * HEADS, DV)

    for j in range(KEYS):
        for copy in copies[4 * j : 4 * j + 4]:
            copy.wait()
        query = dot(x, query_buf[:, j * DK : (j + 1) * DK]).astype(bf16)
        key = dot(x, key_buf[:, j * DK : (j + 1) * DK]).astype(bf16)
        value = dot(x, value_buf[:, 2 * j * DV : 2 * (j + 1) * DV]).astype(bf16)
        gate = dot(x, gate_buf[:, 2 * j * DV : 2 * (j + 1) * DV])
        raw_ref[:, j * DK : (j + 1) * DK] = query
        raw_ref[:, (KEYS + j) * DK : (KEYS + j + 1) * DK] = key
        raw_ref[:, 2 * (KEYS + j) * DK : 2 * (KEYS + j + 1) * DK] = value
        query, key, value = query.astype(f32), key.astype(f32), value.astype(f32)
        gate = gate * jax.nn.sigmoid(gate)
        for i in range(2):
            h = 2 * j + i
            new_all[pl.ds(h, rows, stride=WIDE), :] = query
            new_all[pl.ds(HEADS + h, rows, stride=WIDE), :] = key
            new_all[pl.ds(2 * HEADS + h, rows, stride=WIDE), :] = value[:, i * DV : (i + 1) * DV]
            gate_all[pl.ds(h, rows, stride=HEADS), :] = gate[:, i * DV : (i + 1) * DV] * gain_ref[...]

    half = 2 * ROWS
    new_ref[...] = new_all[half * WIDE :, :]
    gate_ref[...] = gate_all[half * HEADS :, :]
    strength_ref[...] = strength_all[half * HEADS :, :]
    forget_ref[...] = forget_all[half * HEADS :, :]
    wide = widening()
    conv = conv_ref[...]

    def one(row, carry):
        pltpu.make_async_copy(state.at[row], state_buf.at[row], state_sem.at[row]).wait()
        normed, update = recall_row(
            dot(wide, tails_ref[row]),
            [rows_at(new_all, (step * ROWS + row) * WIDE, WIDE) for step in range(2)],
            conv,
            [rows_at(strength_all, (step * ROWS + row) * HEADS, HEADS) for step in range(2)],
            [rows_at(forget_all, (step * ROWS + row) * HEADS, HEADS) for step in range(2)],
            [rows_at(gate_all, (step * ROWS + row) * HEADS, HEADS) for step in range(2)],
            lambda h: state_buf[row, h * DK : (h + 1) * DK, :],
        )
        for step in range(2):
            normed_all[pl.ds(pl.multiple_of((step * ROWS + row) * HEADS, 8), HEADS), :] = normed[step]
        update_ref[row] = update
        return carry

    lax.fori_loop(0, ROWS, one, 0)
    for h in range(HEADS):
        normed_ref[:, h * DV : (h + 1) * DV] = normed_all[pl.ds(h, half, stride=HEADS), :].astype(bf16)


def send_kernel(
    wanted_ref, update_ref, tails_ref, state, slots, state_buf, stored_buf, done_ref, state_sem, slot_sem
):
    def load(row):
        return pltpu.make_async_copy(state.at[row], state_buf.at[row], state_sem.at[row])

    def ship(slot, row):
        return (
            pltpu.make_async_copy(
                stored_buf.at[row], slots.at[slot, pl.ds(0, BODY)], slot_sem.at[0, slot]
            ),
            pltpu.make_async_copy(
                tails_ref.at[row], slots.at[slot, pl.ds(BODY, SLOT - BODY)], slot_sem.at[1, slot]
            ),
        )

    for row in range(ROWS):
        load(row).start()
        done_ref[row] = 0

    def one(slot, carry):
        row = jnp.clip(wanted_ref[slot], 0, ROWS - 1)

        @pl.when(wanted_ref[slot] >= 0)
        def _():
            @pl.when(done_ref[row] == 0)
            def _():
                load(row).wait()

                def store(h, value):
                    stored_buf[row, h * DK : (h + 1) * DK, :] = value

                write_row(
                    update_ref[row], lambda h: state_buf[row, h * DK : (h + 1) * DK, :], store
                )
                done_ref[row] = 1

            for copy in ship(slot, row):
                copy.start()

        return carry

    lax.fori_loop(0, slots.shape[0], one, 0)

    def end_slot(slot, carry):
        @pl.when(wanted_ref[slot] >= 0)
        def _():
            for copy in ship(slot, 0):
                copy.wait()

        return carry

    lax.fori_loop(0, slots.shape[0], end_slot, 0)

    def end_row(row, carry):
        @pl.when(done_ref[row] == 0)
        def _():
            load(row).wait()

        return carry

    lax.fori_loop(0, ROWS, end_row, 0)


def second_kernel(
    slot_ref, new_ref, gate_ref, strength_ref, forget_ref, conv_ref, slots,
    normed_ref, update_ref, last_ref,
    slot_buf, normed_all, slot_sem,
):
    def load(row):
        return pltpu.make_async_copy(slots.at[slot_ref[row]], slot_buf.at[row], slot_sem.at[row])

    for row in range(ROWS):
        load(row).start()
    wide = widening()
    conv = conv_ref[...]

    def one(row, carry):
        load(row).wait()
        tails = slot_buf[row, BODY:, :]
        last_ref[row] = tails[2 * SLIM :]
        normed, update = recall_row(
            dot(wide, tails),
            [rows_at(new_ref, (step * ROWS + row) * WIDE, WIDE) for step in range(2)],
            conv,
            [rows_at(strength_ref, (step * ROWS + row) * HEADS, HEADS) for step in range(2)],
            [rows_at(forget_ref, (step * ROWS + row) * HEADS, HEADS) for step in range(2)],
            [rows_at(gate_ref, (step * ROWS + row) * HEADS, HEADS) for step in range(2)],
            lambda h: slot_buf[row, h * DK : (h + 1) * DK, :],
        )
        for step in range(2):
            normed_all[pl.ds(pl.multiple_of((step * ROWS + row) * HEADS, 8), HEADS), :] = normed[step]
        update_ref[row] = update
        return carry

    lax.fori_loop(0, ROWS, one, 0)
    for h in range(HEADS):
        normed_ref[:, h * DV : (h + 1) * DV] = normed_all[pl.ds(h, 2 * ROWS, stride=HEADS), :].astype(bf16)


def final_kernel(slot_ref, update_ref, slots, final, slot_buf, final_buf, slot_sem, final_sem):
    def load(row):
        return pltpu.make_async_copy(
            slots.at[slot_ref[row], pl.ds(0, BODY)], slot_buf.at[row], slot_sem.at[row]
        )

    def save(row):
        return pltpu.make_async_copy(final_buf.at[row], final.at[row], final_sem.at[row])

    for row in range(ROWS):
        load(row).start()

    def one(row, carry):
        load(row).wait()

        def store(h, value):
            final_buf[row, h * DK : (h + 1) * DK, :] = value

        write_row(update_ref[row], lambda h: slot_buf[row, h * DK : (h + 1) * DK, :], store)
        save(row).start()
        return carry

    lax.fori_loop(0, ROWS, one, 0)
    for row in range(ROWS):
        save(row).wait()


VMEM = pl.BlockSpec(memory_space=pltpu.VMEM)
SMEM = pl.BlockSpec(memory_space=pltpu.SMEM)
ANY = pl.BlockSpec(memory_space=pl.ANY)
PARAMS = pltpu.CompilerParams(vmem_limit_bytes=VMEM_BYTES)


def first_half(x, tails, conv, decay_log, dt_bias, norm_gain, weights, state):
    rows, depth = x.shape
    late = rows // 2
    return pl.pallas_call(
        first_kernel,
        in_specs=[VMEM] * 6 + [ANY] * 7,
        out_specs=[VMEM] * 7,
        out_shape=(
            jax.ShapeDtypeStruct((late * WIDE, DV), f32),
            jax.ShapeDtypeStruct((late * HEADS, DV), f32),
            jax.ShapeDtypeStruct((late * HEADS, DV), f32),
            jax.ShapeDtypeStruct((late * HEADS, DV), f32),
            jax.ShapeDtypeStruct((rows, SLIM * DV), bf16),
            jax.ShapeDtypeStruct((late, HEADS * DV), bf16),
            jax.ShapeDtypeStruct((ROWS, 5 * HEADS, DV), f32),
        ),
        scratch_shapes=[
            pltpu.VMEM((depth, KEYS * DK), bf16),
            pltpu.VMEM((depth, KEYS * DK), bf16),
            pltpu.VMEM((depth, HEADS * DV), bf16),
            pltpu.VMEM((depth, HEADS * DV), bf16),
            pltpu.VMEM((depth, HEADS), bf16),
            pltpu.VMEM((depth, HEADS), bf16),
            pltpu.VMEM((ROWS, BODY, DV), bf16),
            pltpu.VMEM((rows * WIDE, DV), f32),
            pltpu.VMEM((rows * HEADS, DV), f32),
            pltpu.VMEM((rows * HEADS, DV), f32),
            pltpu.VMEM((rows * HEADS, DV), f32),
            pltpu.VMEM((late * HEADS, DV), f32),
            pltpu.SemaphoreType.DMA((4 * KEYS + 2,)),
            pltpu.SemaphoreType.DMA((ROWS,)),
        ],
        compiler_params=PARAMS,
        name="first_half",
    )(x, tails, conv, decay_log, dt_bias, norm_gain, *weights, state)


def fill_slots(wanted, update, tails, state):
    return pl.pallas_call(
        send_kernel,
        in_specs=[SMEM, VMEM, VMEM, ANY],
        out_specs=ANY,
        out_shape=jax.ShapeDtypeStruct((wanted.shape[0], SLOT, DV), bf16),
        scratch_shapes=[
            pltpu.VMEM((ROWS, BODY, DV), bf16),
            pltpu.VMEM((ROWS, BODY, DV), bf16),
            pltpu.SMEM((ROWS,), jnp.int32),
            pltpu.SemaphoreType.DMA((ROWS,)),
            pltpu.SemaphoreType.DMA((2, wanted.shape[0])),
        ],
        compiler_params=PARAMS,
        name="fill_slots",
    )(wanted, update, tails, state)


def second_half(slot_of_row, new, gates, strengths, decays, conv, slots):
    return pl.pallas_call(
        second_kernel,
        in_specs=[SMEM] + [VMEM] * 5 + [ANY],
        out_specs=[VMEM] * 3,
        out_shape=(
            jax.ShapeDtypeStruct((2 * ROWS, HEADS * DV), bf16),
            jax.ShapeDtypeStruct((ROWS, 5 * HEADS, DV), f32),
            jax.ShapeDtypeStruct((ROWS, SLIM, DV), bf16),
        ),
        scratch_shapes=[
            pltpu.VMEM((ROWS, SLOT, DV), bf16),
            pltpu.VMEM((2 * ROWS * HEADS, DV), f32),
            pltpu.SemaphoreType.DMA((ROWS,)),
        ],
        compiler_params=PARAMS,
        name="second_half",
    )(slot_of_row, new, gates, strengths, decays, conv, slots)


def last_memory(slot_of_row, update, slots):
    return pl.pallas_call(
        final_kernel,
        in_specs=[SMEM, VMEM, ANY],
        out_specs=ANY,
        out_shape=jax.ShapeDtypeStruct((ROWS, BODY, DV), bf16),
        scratch_shapes=[
            pltpu.VMEM((ROWS, BODY, DV), bf16),
            pltpu.VMEM((ROWS, BODY, DV), bf16),
            pltpu.SemaphoreType.DMA((ROWS,)),
            pltpu.SemaphoreType.DMA((ROWS,)),
        ],
        compiler_params=PARAMS,
        name="last_memory",
    )(slot_of_row, update, slots)


def sum_heads(partial):
    count, me = lax.axis_size("tensor"), lax.axis_index("tensor")
    width = partial.shape[1] // count

    def block(shift):
        return lax.dynamic_slice_in_dim(partial, (me + shift) % count * width, width, axis=1)

    total = block(0)
    for shift in range(1, count):
        pairs = [(i, (i + shift) % count) for i in range(count)]
        total = total + lax.ppermute(block(shift), "tensor", pairs)
    return total.astype(bf16)


def slim(query, key, value):
    parts = [part.reshape(part.shape[0], -1, DV) for part in (query, key, value)]
    return jnp.concatenate(parts, axis=1)


def per_device(
    inputs,
    w_query,
    w_key,
    w_value,
    w_gate_z,
    w_beta,
    w_decay,
    conv_query,
    conv_key,
    conv_value,
    decay_log,
    dt_bias,
    norm_gain,
    w_out,
    state,
    tail_query,
    tail_key,
    tail_value,
    parents,
):
    groups = lax.axis_size("branch")
    source, offset = parents // ROWS, parents % ROWS
    hits = source[:, None] == jnp.arange(groups, dtype=jnp.int32)[None, :]
    wanted = jnp.sum(jnp.where(hits, offset[:, None] + 1, 0), axis=0) - 1
    requested = lax.all_to_all(
        wanted.reshape(groups, 1), "branch", split_axis=0, concat_axis=0, tiled=True
    ).reshape(groups)

    x = inputs.reshape(-1, inputs.shape[-1])
    own_tails = jnp.concatenate(
        [slim(tail_query[:, i], tail_key[:, i], tail_value[:, i]) for i in range(TAPS - 1)], axis=1
    )
    conv = slim(conv_query, conv_key, conv_value).astype(f32)
    conv = jnp.concatenate([jnp.repeat(conv[:, : 2 * KEYS], 2, axis=1), conv[:, 2 * KEYS :]], axis=1)
    conv = conv.reshape(TAPS * WIDE, DV)
    spread = lambda value: jnp.broadcast_to(value[:, None], (HEADS, DV))
    flat_state = state.reshape(ROWS, BODY, DV)

    new, gates, strengths, decays, raw, normed, update = first_half(
        x,
        own_tails,
        conv,
        spread(decay_log),
        spread(dt_bias),
        norm_gain[None],
        (w_query, w_key, w_value, w_gate_z, w_beta, w_decay),
        flat_state,
    )
    fresh = raw.reshape(inputs.shape[0], ROWS, SLIM, DV)
    stored_tails = jnp.concatenate([own_tails[:, 2 * SLIM :], fresh[0], fresh[1]], axis=1)
    shipped = fill_slots(requested, update, stored_tails, flat_state)
    arrived = lax.all_to_all(shipped, "branch", split_axis=0, concat_axis=0, tiled=True)

    first_rows = sum_heads(dot(normed, w_out))

    normed, update, last = second_half(source, new, gates, strengths, decays, conv, arrived)
    second_rows = sum_heads(dot(normed, w_out))
    final_state = last_memory(source, update, arrived).reshape(state.shape)

    raw = raw.reshape(inputs.shape[0], ROWS, SLIM * DV)
    last = last.reshape(ROWS, SLIM * DV)
    final_tails = []
    start = 0
    for tail in (tail_query, tail_key, tail_value):
        part = slice(start, start + tail.shape[2])
        start = part.stop
        final_tails.append(jnp.stack([last[:, part], raw[2, :, part], raw[3, :, part]], axis=1))
    out_rows = jnp.concatenate([first_rows, second_rows], axis=0)
    out_rows = out_rows.reshape(inputs.shape[0], ROWS, -1)
    return (out_rows, final_state, *final_tails)


def solution(mesh):
    return jax.shard_map(
        per_device,
        mesh=mesh,
        in_specs=(
            P(None, "branch", None),
            P(None, "tensor"),
            P(None, "tensor"),
            P(None, "tensor"),
            P(None, "tensor"),
            P(None, "tensor"),
            P(None, "tensor"),
            P(None, "tensor"),
            P(None, "tensor"),
            P(None, "tensor"),
            P("tensor"),
            P("tensor"),
            P(),
            P("tensor", None),
            P("branch", "tensor", None, None),
            P("branch", None, "tensor"),
            P("branch", None, "tensor"),
            P("branch", None, "tensor"),
            P("branch"),
        ),
        out_specs=(
            P(None, "branch", "tensor"),
            P("branch", "tensor", None, None),
            P("branch", None, "tensor"),
            P("branch", None, "tensor"),
            P("branch", None, "tensor"),
        ),
        check_vma=False,
    )
```

```python
import jax
import jax.numpy as jnp
from jax import lax
from jax.experimental import pallas as pl
from jax.experimental.pallas import tpu as pltpu
from jax.sharding import PartitionSpec as P

DK = 128
DV = 128
HEADS = 8
KEYS = 4
ROWS = 16
TAPS = 4
WIDE = 3 * HEADS
SLIM = 2 * KEYS + HEADS
BODY = HEADS * DK
SLOT = BODY + (TAPS - 1) * SLIM
VMEM_BYTES = 48 * 1024 * 1024
CHUNK = 4
GROUP = 4
f32 = jnp.float32
bf16 = jnp.bfloat16


def split(value):
    high = value.astype(bf16).astype(f32)
    return high, value - high


def dot(left, right):
    return jnp.dot(left, right, preferred_element_type=f32)


def inner(left, right):
    return jnp.sum(left * right, axis=-1, keepdims=True)


def widening():
    row = lax.broadcasted_iota(jnp.int32, ((TAPS - 1) * WIDE, (TAPS - 1) * SLIM), 0)
    column = lax.broadcasted_iota(jnp.int32, ((TAPS - 1) * WIDE, (TAPS - 1) * SLIM), 1)
    tap, place = row // WIDE, row % WIDE
    origin = tap * SLIM + jnp.where(place < 2 * HEADS, place // 2, place - HEADS)
    return jnp.where(origin == column, 1.0, 0.0).astype(bf16)


def part_of(ref, index, first, count):
    return ref[pl.ds(index * ROWS * HEADS + first * HEADS, count * HEADS), :]


def find_vectors(window, conv_ref, vector_buf, value_buf):
    for first in range(0, ROWS, CHUNK):
        there = slice(first, first + CHUNK)
        for step in range(2):
            for kind in range(3):
                mixed = 0.0
                for tap in range(TAPS):
                    rows = window(kind, step + tap, first).reshape(CHUNK, HEADS, DV)
                    mixed = mixed + rows * conv_ref[kind, tap][None]
                mixed = mixed * jax.nn.sigmoid(mixed)
                if kind == 2:
                    value_buf[step, there] = mixed
                    continue
                unit = mixed * lax.rsqrt(inner(mixed, mixed) + 1e-06)
                if kind == 0:
                    unit = unit * DK ** (-0.5)
                place = 2 * step + 1 - kind
                vector_buf[there, place * HEADS : (place + 1) * HEADS, :] = unit


def recall(wait, memory, vector_buf, found_buf):
    head = lax.broadcasted_iota(jnp.int32, (HEADS, DV), 0)

    def one(row):
        high, low = split(vector_buf[row])
        left = jnp.concatenate([high, low], axis=0).astype(bf16)
        found = [jnp.zeros((HEADS, DV), f32)] * 4
        for h in range(0, HEADS, 2):
            pair = jnp.concatenate([memory(row, h), memory(row, h + 1)], axis=1)
            product = dot(left, pair)
            product = product[: 4 * HEADS] + product[4 * HEADS :]
            for i in range(4):
                block = product[i * HEADS : (i + 1) * HEADS]
                found[i] = jnp.where(head == h, block[:, :DV], found[i])
                found[i] = jnp.where(head == h + 1, block[:, DV:], found[i])
        found_buf[row] = jnp.concatenate(found, axis=0)

    def group(index, carry):
        for i in range(GROUP):
            wait(index * GROUP + i)
        for i in range(GROUP):
            one(index * GROUP + i)
        return carry

    lax.fori_loop(0, ROWS // GROUP, group, 0)


def finish(strength, decay, gate, vector_buf, value_buf, found_buf, normed_buf, update_ref):
    for first in range(0, ROWS, CHUNK):
        there = slice(first, first + CHUNK)

        def piece(ref, i):
            return ref[there, i * HEADS : (i + 1) * HEADS, :]

        def shaped(value):
            return value.reshape(CHUNK, HEADS, DV)

        key0, query0, key1, query1 = [piece(vector_buf, i) for i in range(4)]
        found0, found1, found2, found3 = [piece(found_buf, i) for i in range(4)]
        strength0, strength1 = [shaped(strength(step, first)) for step in range(2)]
        decay0, decay1 = [shaped(decay(step, first)) for step in range(2)]
        change0 = (value_buf[0, there] - decay0 * found0) * strength0
        read0 = decay0 * found1 + inner(query0, key0) * change0
        kept = decay0 * found2 + inner(key1, key0) * change0
        change1 = (value_buf[1, there] - decay1 * kept) * strength1
        kept = decay0 * found3 + inner(query1, key0) * change0
        read1 = decay1 * kept + inner(query1, key1) * change1
        for step, read in enumerate((read0, read1)):
            scale = lax.rsqrt(jnp.mean(read * read, axis=-1, keepdims=True) + 1e-06)
            normed = read * scale * shaped(gate(step, first))
            start = (step * ROWS + first) * HEADS
            normed_buf[start : start + CHUNK * HEADS, :] = normed.reshape(CHUNK * HEADS, DV)
        for i, value in enumerate((key0, key1, decay1 * change0, change1, decay0 * decay1)):
            update_ref[there, i * HEADS : (i + 1) * HEADS, :] = value


def flatten_heads(normed_buf, normed_ref):
    for h in range(HEADS):
        rows = normed_buf[pl.ds(h, 2 * ROWS, stride=HEADS), :]
        normed_ref[:, h * DV : (h + 1) * DV] = rows.astype(bf16)


def write_row(update, memory, store):
    key0, key1, change0, change1, decay = [
        update[i * HEADS : (i + 1) * HEADS] for i in range(5)
    ]
    (key0h, key0l), (key1h, key1l) = split(key0), split(key1)
    (change0h, change0l), (change1h, change1l) = split(change0), split(change1)
    left = jnp.concatenate([key0h, key0l, key0h, key1h, key1l, key1h], axis=0)
    left = left.T.astype(bf16)
    right = jnp.concatenate([change0h, change0h, change0l, change1h, change1h, change1l], axis=0)
    head = lax.broadcasted_iota(jnp.int32, right.shape, 0) % HEADS
    for h in range(0, HEADS, 2):
        pair = [jnp.where(head == h + i, right, 0.0).astype(bf16) for i in range(2)]
        added = dot(left, jnp.concatenate(pair, axis=1))
        for i in range(2):
            kept = memory(h + i).astype(f32) * decay[h + i : h + i + 1]
            store(h + i, (kept + added[:, i * DV : (i + 1) * DV]).astype(bf16))


def write_group(index, update_ref, memory_ref, target_ref):
    for i in range(GROUP):
        row = index * GROUP + i

        def store(h, value, row=row):
            target_ref[row, h * DK : (h + 1) * DK, :] = value

        write_row(
            update_ref[row], lambda h, row=row: memory_ref[row, h * DK : (h + 1) * DK, :], store
        )


def first_kernel(
    x, gain, tail_query, tail_key, tail_value, conv_query, conv_key, conv_value,
    w_query, w_key, w_value, w_gate, w_beta, w_decay, decay_log, dt_bias, state,
    late_query_ref, late_key_ref, late_value_ref, late_gate_ref, late_strength_ref, late_forget_ref,
    raw_ref, stored_ref, conv_ref, normed_ref, update_ref, state_buf,
    x_buf, gain_buf, tail_query_buf, tail_key_buf, tail_value_buf,
    conv_query_buf, conv_key_buf, conv_value_buf,
    query_buf, key_buf, value_weight_buf, gate_weight_buf, beta_buf, decay_buf, decay_ref, bias_ref,
    window_query, window_key, window_value, gate_all, strength_all, forget_all, stored_buf,
    vector_buf, value_buf, found_buf, normed_buf,
    small_sem, weight_sem, state_sem,
):
    rows = x_buf.shape[0]
    small = [
        pltpu.make_async_copy(source, target, small_sem.at[i])
        for i, (source, target) in enumerate(
            (
                (x, x_buf),
                (w_beta, beta_buf),
                (w_decay, decay_buf),
                (gain, gain_buf),
                (tail_query, tail_query_buf),
                (tail_key, tail_key_buf),
                (tail_value, tail_value_buf),
                (conv_query, conv_query_buf),
                (conv_key, conv_key_buf),
                (conv_value, conv_value_buf),
                (decay_log, decay_ref),
                (dt_bias, bias_ref),
            )
        )
    ]
    for copy in small:
        copy.start()

    def weights(j):
        pieces = (
            (w_query, query_buf, DK),
            (w_key, key_buf, DK),
            (w_value, value_weight_buf, 2 * DV),
            (w_gate, gate_weight_buf, 2 * DV),
        )
        copies = []
        for i, (hbm, buf, width) in enumerate(pieces):
            part = pl.ds(j * width, width)
            copies.append(
                pltpu.make_async_copy(hbm.at[:, part], buf.at[:, part], weight_sem.at[4 * j + i])
            )
        return copies

    def load(row):
        return pltpu.make_async_copy(state.at[row], state_buf.at[row], state_sem.at[row])

    def begin(j):
        if j < KEYS:
            for copy in weights(j):
                copy.start()
        elif j < KEYS + 2:
            for row in range((j - KEYS) * ROWS // 2, (j - KEYS + 1) * ROWS // 2):
                load(row).start()

    begin(0)
    begin(1)

    for copy in small:
        copy.wait()
    head = lax.broadcasted_iota(jnp.int32, (HEADS, DV), 0)
    rate, bias = jnp.zeros((HEADS, DV), f32), jnp.zeros((HEADS, DV), f32)
    for h in range(HEADS):
        rate = jnp.where(head == h, decay_ref[h], rate)
        bias = jnp.where(head == h, bias_ref[h], bias)
    rate = -jnp.exp(rate)
    x_all = x_buf[...]

    def spread(target, start, h, block):
        target[pl.ds(start * HEADS + h, block.shape[0], stride=HEADS), :] = block

    across = (((1,), (1,)), ((), ()))
    beta = lax.dot_general(x_all, beta_buf[...], across, preferred_element_type=f32)
    decay = lax.dot_general(x_all, decay_buf[...], across, preferred_element_type=f32)
    for h in range(HEADS):
        spread(strength_all, 0, h, jnp.broadcast_to(beta[:, h : h + 1], (rows, DV)))
        spread(forget_all, 0, h, jnp.broadcast_to(decay[:, h : h + 1], (rows, DV)))
    for first in range(0, rows, ROWS):
        there = slice(first * HEADS, (first + ROWS) * HEADS)
        strength_all[there] = jax.nn.sigmoid(strength_all[there])
        raised = forget_all[there].reshape(ROWS, HEADS, DV) + bias[None]
        forget = jnp.exp(rate[None] * jax.nn.softplus(raised))
        forget_all[there] = forget.reshape(ROWS * HEADS, DV)

    history = (TAPS - 1) * ROWS

    def place(window, h, before, fresh):
        spread(window, 0, h, before)
        spread(window, history, h, fresh)

    def keep(channel, before, fresh):
        after = jnp.concatenate([before[2 * ROWS :], fresh[: 2 * ROWS]], axis=0)
        for tap in range(TAPS - 1):
            stored_buf[pl.ds(tap * SLIM + channel, ROWS, stride=(TAPS - 1) * SLIM), :] = after[
                tap * ROWS : (tap + 1) * ROWS
            ]

    for kind, buf in enumerate((conv_query_buf, conv_key_buf, conv_value_buf)):
        wide = buf[...].astype(f32)
        for h in range(HEADS):
            channel = h if kind == 2 else h // 2
            taps = wide[:, channel * DV : (channel + 1) * DV]
            for tap in range(TAPS):
                conv_ref[kind, tap, h : h + 1, :] = taps[tap : tap + 1]

    for j in range(KEYS):
        for copy in weights(j):
            copy.wait()
        begin(j + 2)
        one, two = slice(j * DK, (j + 1) * DK), slice(2 * j * DV, 2 * (j + 1) * DV)
        query = dot(x_all, query_buf[:, one]).astype(bf16)
        key = dot(x_all, key_buf[:, one]).astype(bf16)
        value = dot(x_all, value_weight_buf[:, two]).astype(bf16)
        gate = dot(x_all, gate_weight_buf[:, two])
        raw_ref[:, j * DK : (j + 1) * DK] = query[2 * ROWS :]
        raw_ref[:, (KEYS + j) * DK : (KEYS + j + 1) * DK] = key[2 * ROWS :]
        raw_ref[:, 2 * (KEYS + j) * DK : 2 * (KEYS + j + 1) * DK] = value[2 * ROWS :]
        query, key, value = query.astype(f32), key.astype(f32), value.astype(f32)
        old_query = tail_query_buf[:, :, one].reshape(history, DK).astype(f32)
        old_key = tail_key_buf[:, :, one].reshape(history, DK).astype(f32)
        old_value = tail_value_buf[:, :, two].reshape(history, 2 * DV).astype(f32)
        gate = gate * jax.nn.sigmoid(gate)
        keep(j, old_query, query)
        keep(KEYS + j, old_key, key)
        for i in range(2):
            h, half = 2 * j + i, slice(i * DV, (i + 1) * DV)
            place(window_query, h, old_query, query)
            place(window_key, h, old_key, key)
            place(window_value, h, old_value[:, half], value[:, half])
            keep(2 * KEYS + h, old_value[:, half], value[:, half])
            spread(gate_all, 0, h, gate[:, half] * gain_buf[...])

    late = (history + 2 * ROWS) * HEADS
    late_query_ref[...] = window_query[late:, :]
    late_key_ref[...] = window_key[late:, :]
    late_value_ref[...] = window_value[late:, :]
    late_gate_ref[...] = gate_all[2 * ROWS * HEADS :, :]
    late_strength_ref[...] = strength_all[2 * ROWS * HEADS :, :]
    late_forget_ref[...] = forget_all[2 * ROWS * HEADS :, :]
    stored_ref[...] = stored_buf[...].reshape(stored_ref.shape).astype(bf16)

    windows = (window_query, window_key, window_value)
    find_vectors(
        lambda kind, tap, first: part_of(windows[kind], tap, first, CHUNK),
        conv_ref,
        vector_buf,
        value_buf,
    )
    recall(
        lambda row: load(row).wait(),
        lambda row, h: state_buf[row, h * DK : (h + 1) * DK, :],
        vector_buf,
        found_buf,
    )
    finish(
        lambda step, first: part_of(strength_all, step, first, CHUNK),
        lambda step, first: part_of(forget_all, step, first, CHUNK),
        lambda step, first: part_of(gate_all, step, first, CHUNK),
        vector_buf,
        value_buf,
        found_buf,
        normed_buf,
        update_ref,
    )
    flatten_heads(normed_buf, normed_ref)


def send_kernel(wanted_ref, update_ref, tails_ref, state_ref, slots, stored_buf, slot_sem):
    count = slots.shape[0]

    def ship(slot, row):
        return (
            pltpu.make_async_copy(
                stored_buf.at[row], slots.at[slot, pl.ds(0, BODY)], slot_sem.at[0, slot]
            ),
            pltpu.make_async_copy(
                tails_ref.at[row], slots.at[slot, pl.ds(BODY, SLOT - BODY)], slot_sem.at[1, slot]
            ),
        )

    def group(index, carry):
        write_group(index, update_ref, state_ref, stored_buf)

        def begin(slot, carry):
            row = wanted_ref[slot]

            @pl.when((row >= index * GROUP) & (row < (index + 1) * GROUP))
            def _():
                for copy in ship(slot, row):
                    copy.start()

            return carry

        return lax.fori_loop(0, count, begin, carry)

    lax.fori_loop(0, ROWS // GROUP, group, 0)

    def end(slot, carry):
        @pl.when(wanted_ref[slot] >= 0)
        def _():
            for copy in ship(slot, 0):
                copy.wait()

        return carry

    lax.fori_loop(0, count, end, 0)


def second_kernel(
    slot_ref, late_query, late_key, late_value, late_gate, late_strength, late_forget, conv_ref, slots,
    normed_ref, update_ref, last_ref, memory_buf,
    tail_buf, window_query, window_key, window_value,
    vector_buf, value_buf, found_buf, normed_buf, tail_sem, memory_sem,
):
    def load_tail(row):
        return pltpu.make_async_copy(
            slots.at[slot_ref[row], pl.ds(BODY, SLOT - BODY)], tail_buf.at[row], tail_sem.at[row]
        )

    def load(row):
        return pltpu.make_async_copy(
            slots.at[slot_ref[row], pl.ds(0, BODY)], memory_buf.at[row], memory_sem.at[row]
        )

    for row in range(ROWS):
        load_tail(row).start()
    for row in range(ROWS):
        load(row).start()
    wide = widening()
    for row in range(ROWS):
        load_tail(row).wait()
    for row in range(ROWS):
        tails = tail_buf[row]
        last_ref[row] = tails[2 * SLIM :]
        spread = dot(wide, tails)
        for tap in range(TAPS - 1):
            for kind, window in enumerate((window_query, window_key, window_value)):
                start = tap * WIDE + kind * HEADS
                window[(tap * ROWS + row) * HEADS : (tap * ROWS + row + 1) * HEADS, :] = spread[
                    start : start + HEADS
                ]
    windows = (window_query, window_key, window_value)
    fresh = (late_query, late_key, late_value)

    def window(kind, tap, first):
        if tap < TAPS - 1:
            return part_of(windows[kind], tap, first, CHUNK)
        return part_of(fresh[kind], tap - (TAPS - 1), first, CHUNK)

    find_vectors(window, conv_ref, vector_buf, value_buf)
    recall(
        lambda row: load(row).wait(),
        lambda row, h: memory_buf[row, h * DK : (h + 1) * DK, :],
        vector_buf,
        found_buf,
    )
    finish(
        lambda step, first: part_of(late_strength, step, first, CHUNK),
        lambda step, first: part_of(late_forget, step, first, CHUNK),
        lambda step, first: part_of(late_gate, step, first, CHUNK),
        vector_buf,
        value_buf,
        found_buf,
        normed_buf,
        update_ref,
    )
    flatten_heads(normed_buf, normed_ref)


def final_kernel(
    update_ref, last_ref, raw_ref, memory_ref,
    final, query_ref, key_ref, value_ref,
    final_buf, last_buf, final_sem,
):
    def save(row):
        return pltpu.make_async_copy(final_buf.at[row], final.at[row], final_sem.at[row])

    start = 0
    last_buf[...] = last_ref[...].astype(f32).reshape(ROWS * SLIM, DV)
    for ref in (query_ref, key_ref, value_ref):
        width = ref.shape[2]
        for channel in range(width // DV):
            block = last_buf[pl.ds(start // DV + channel, ROWS, stride=SLIM), :]
            ref[0, :, channel * DV : (channel + 1) * DV] = block.astype(bf16)
        for step in range(2):
            ref[1 + step] = raw_ref[step * ROWS : (step + 1) * ROWS, start : start + width]
        start += width

    def group(index, carry):
        write_group(index, update_ref, memory_ref, final_buf)
        for i in range(GROUP):
            save(index * GROUP + i).start()
        return carry

    lax.fori_loop(0, ROWS // GROUP, group, 0)
    for row in range(ROWS):
        save(row).wait()


VMEM = pl.BlockSpec(memory_space=pltpu.VMEM)
SMEM = pl.BlockSpec(memory_space=pltpu.SMEM)
HBM = pl.BlockSpec(memory_space=pltpu.HBM)
PARAMS = pltpu.CompilerParams(vmem_limit_bytes=VMEM_BYTES)


def in_hbm(array):
    return pltpu.with_memory_space_constraint(array, pltpu.HBM)


def shape(dims, kind):
    return jax.ShapeDtypeStruct(dims, kind)


def buffer(array):
    return pltpu.VMEM(array.shape, array.dtype)


def work_buffers():
    return [
        pltpu.VMEM((ROWS, 4 * HEADS, DV), f32),
        pltpu.VMEM((2, ROWS, HEADS, DV), f32),
        pltpu.VMEM((ROWS, 4 * HEADS, DV), f32),
        pltpu.VMEM((2 * ROWS * HEADS, DV), f32),
    ]


def first_half(arrays, state):
    rows = arrays[0].shape[0]
    late = rows // 2
    window = pltpu.VMEM(((TAPS - 1) * ROWS * HEADS + rows * HEADS, DV), f32)
    wide = pltpu.VMEM((rows * HEADS, DV), f32)
    return pl.pallas_call(
        first_kernel,
        in_specs=[HBM] * (len(arrays) + 1),
        out_specs=[VMEM] * 12,
        out_shape=(
            *[shape((late * HEADS, DV), f32)] * 6,
            shape((late, SLIM * DV), bf16),
            shape((ROWS, (TAPS - 1) * SLIM, DV), bf16),
            shape((3, TAPS, HEADS, DV), f32),
            shape((late, HEADS * DV), bf16),
            shape((ROWS, 5 * HEADS, DV), f32),
            shape(state.shape, bf16),
        ),
        scratch_shapes=[
            *[buffer(array) for array in arrays[:-2]],
            *[pltpu.SMEM(array.shape, f32) for array in arrays[-2:]],
            window,
            window,
            window,
            wide,
            wide,
            wide,
            pltpu.VMEM((ROWS * (TAPS - 1) * SLIM, DV), f32),
            *work_buffers(),
            pltpu.SemaphoreType.DMA((12,)),
            pltpu.SemaphoreType.DMA((4 * KEYS,)),
            pltpu.SemaphoreType.DMA((ROWS,)),
        ],
        compiler_params=PARAMS,
        name="first_half",
    )(*[in_hbm(array) for array in arrays], in_hbm(state))


def fill_slots(wanted, update, tails, state):
    return pl.pallas_call(
        send_kernel,
        in_specs=[SMEM] + [VMEM] * 3,
        out_specs=HBM,
        out_shape=shape((wanted.shape[0], SLOT, DV), bf16),
        scratch_shapes=[
            buffer(state),
            pltpu.SemaphoreType.DMA((2, wanted.shape[0])),
        ],
        compiler_params=PARAMS,
        name="fill_slots",
    )(wanted, update, tails, state)


def second_half(slot_of_row, late, conv, slots):
    window = pltpu.VMEM(((TAPS - 1) * ROWS * HEADS, DV), f32)
    return pl.pallas_call(
        second_kernel,
        in_specs=[SMEM] + [VMEM] * 7 + [HBM],
        out_specs=[VMEM] * 4,
        out_shape=(
            shape((2 * ROWS, HEADS * DV), bf16),
            shape((ROWS, 5 * HEADS, DV), f32),
            shape((ROWS, SLIM, DV), bf16),
            shape((ROWS, BODY, DV), bf16),
        ),
        scratch_shapes=[
            pltpu.VMEM((ROWS, SLOT - BODY, DV), bf16),
            window,
            window,
            window,
            *work_buffers(),
            pltpu.SemaphoreType.DMA((ROWS,)),
            pltpu.SemaphoreType.DMA((ROWS,)),
        ],
        compiler_params=PARAMS,
        name="second_half",
    )(slot_of_row, *late, conv, in_hbm(slots))


def last_memory(update, last, raw, memory):
    return pl.pallas_call(
        final_kernel,
        in_specs=[VMEM] * 4,
        out_specs=[HBM] + [VMEM] * 3,
        out_shape=(
            shape((ROWS, BODY, DV), bf16),
            shape((TAPS - 1, ROWS, KEYS * DK), bf16),
            shape((TAPS - 1, ROWS, KEYS * DK), bf16),
            shape((TAPS - 1, ROWS, HEADS * DV), bf16),
        ),
        scratch_shapes=[
            buffer(memory),
            pltpu.VMEM((ROWS * SLIM, DV), f32),
            pltpu.SemaphoreType.DMA((ROWS,)),
        ],
        compiler_params=PARAMS,
        name="last_memory",
    )(update, last, raw, memory)


def sum_heads(partial):
    count, me = lax.axis_size("tensor"), lax.axis_index("tensor")
    width = partial.shape[1] // count

    def block(shift):
        return lax.dynamic_slice_in_dim(partial, (me + shift) % count * width, width, axis=1)

    total = block(0)
    for shift in range(1, count):
        pairs = [(i, (i + shift) % count) for i in range(count)]
        total = total + lax.ppermute(block(shift), "tensor", pairs)
    return total.astype(bf16)


def per_device(
    inputs,
    w_query,
    w_key,
    w_value,
    w_gate_z,
    w_beta,
    w_decay,
    conv_query,
    conv_key,
    conv_value,
    decay_log,
    dt_bias,
    norm_gain,
    w_out,
    state,
    tail_query,
    tail_key,
    tail_value,
    parents,
):
    groups = lax.axis_size("branch")
    source, offset = parents // ROWS, parents % ROWS
    hits = source[:, None] == jnp.arange(groups, dtype=jnp.int32)[None, :]
    wanted = jnp.sum(jnp.where(hits, offset[:, None] + 1, 0), axis=0) - 1
    requested = lax.all_to_all(
        wanted.reshape(groups, 1), "branch", split_axis=0, concat_axis=0, tiled=True
    ).reshape(groups)

    flat_state = state.reshape(ROWS, BODY, DV)
    *late, raw, stored_tails, conv, normed, update, held = first_half(
        (
            inputs.reshape(-1, inputs.shape[-1]),
            norm_gain[None],
            tail_query.transpose(1, 0, 2),
            tail_key.transpose(1, 0, 2),
            tail_value.transpose(1, 0, 2),
            conv_query,
            conv_key,
            conv_value,
            w_query,
            w_key,
            w_value,
            w_gate_z,
            w_beta.T,
            w_decay.T,
            decay_log,
            dt_bias,
        ),
        flat_state,
    )
    shipped = fill_slots(requested, update, stored_tails, held)
    arrived = lax.all_to_all(shipped, "branch", split_axis=0, concat_axis=0, tiled=True)

    first_rows = sum_heads(dot(normed, w_out))

    normed, update, last, memory = second_half(source, late, conv, arrived)
    second_rows = sum_heads(dot(normed, w_out))
    final_state, *final_tails = last_memory(update, last, raw, memory)

    out_rows = jnp.concatenate([first_rows, second_rows], axis=0)
    out_rows = out_rows.reshape(inputs.shape[0], ROWS, -1)
    return (
        out_rows,
        final_state.reshape(state.shape),
        *[tail.transpose(1, 0, 2) for tail in final_tails],
    )


def solution(mesh):
    return jax.shard_map(
        per_device,
        mesh=mesh,
        in_specs=(
            P(None, "branch", None),
            P(None, "tensor"),
            P(None, "tensor"),
            P(None, "tensor"),
            P(None, "tensor"),
            P(None, "tensor"),
            P(None, "tensor"),
            P(None, "tensor"),
            P(None, "tensor"),
            P(None, "tensor"),
            P("tensor"),
            P("tensor"),
            P(),
            P("tensor", None),
            P("branch", "tensor", None, None),
            P("branch", None, "tensor"),
            P("branch", None, "tensor"),
            P("branch", None, "tensor"),
            P("branch"),
        ),
        out_specs=(
            P(None, "branch", "tensor"),
            P("branch", "tensor", None, None),
            P("branch", None, "tensor"),
            P("branch", None, "tensor"),
            P("branch", None, "tensor"),
        ),
        check_vma=False,
    )
```

```python
import jax
import jax.numpy as jnp
from jax import lax
from jax.experimental import pallas as pl
from jax.experimental.pallas import tpu as pltpu
from jax.sharding import PartitionSpec as P

DK = 128
DV = 128
HEADS = 8
KEYS = 4
ROWS = 16
TAPS = 4
WIDE = 3 * HEADS
SLIM = 2 * KEYS + HEADS
BODY = HEADS * DK
SLOT = BODY + (TAPS - 1) * SLIM
VMEM_BYTES = 48 * 1024 * 1024
CHUNK = 4
PARTS = 4
GROUP = 4
f32 = jnp.float32
bf16 = jnp.bfloat16


def split(value):
    high = value.astype(bf16).astype(f32)
    return high, value - high


def dot(left, right):
    return jnp.dot(left, right, preferred_element_type=f32)


def inner(left, right):
    return jnp.sum(left * right, axis=-1, keepdims=True)


def widening():
    row = lax.broadcasted_iota(jnp.int32, ((TAPS - 1) * WIDE, (TAPS - 1) * SLIM), 0)
    column = lax.broadcasted_iota(jnp.int32, ((TAPS - 1) * WIDE, (TAPS - 1) * SLIM), 1)
    tap, place = row // WIDE, row % WIDE
    origin = tap * SLIM + jnp.where(place < 2 * HEADS, place // 2, place - HEADS)
    return jnp.where(origin == column, 1.0, 0.0).astype(bf16)


def part_of(ref, index, first, count):
    return ref[pl.ds(index * ROWS * HEADS + first * HEADS, count * HEADS), :]


def find_vectors(window, conv_ref, vector_buf, value_buf):
    for first in range(0, ROWS, CHUNK):
        there = slice(first, first + CHUNK)
        for step in range(2):
            for kind in range(3):
                mixed = 0.0
                for tap in range(TAPS):
                    rows = window(kind, step + tap, first).reshape(CHUNK, HEADS, DV)
                    mixed = mixed + rows * conv_ref[kind, tap][None]
                mixed = mixed * jax.nn.sigmoid(mixed)
                if kind == 2:
                    value_buf[step, there] = mixed
                    continue
                unit = mixed * lax.rsqrt(inner(mixed, mixed) + 1e-06)
                if kind == 0:
                    unit = unit * DK ** (-0.5)
                place = 2 * step + 1 - kind
                vector_buf[there, place * HEADS : (place + 1) * HEADS, :] = unit


def recall(wait, memory, vector_buf, found_buf):
    head = lax.broadcasted_iota(jnp.int32, (HEADS, DV), 0)

    def one(row):
        high, low = split(vector_buf[row])
        left = jnp.concatenate([high, low], axis=0).astype(bf16)
        found = [jnp.zeros((HEADS, DV), f32)] * 4
        for h in range(0, HEADS, 2):
            pair = jnp.concatenate([memory(row, h), memory(row, h + 1)], axis=1)
            product = dot(left, pair)
            product = product[: 4 * HEADS] + product[4 * HEADS :]
            for i in range(4):
                block = product[i * HEADS : (i + 1) * HEADS]
                found[i] = jnp.where(head == h, block[:, :DV], found[i])
                found[i] = jnp.where(head == h + 1, block[:, DV:], found[i])
        found_buf[row] = jnp.concatenate(found, axis=0)

    def group(index, carry):
        for i in range(GROUP):
            wait(index * GROUP + i)
        for i in range(GROUP):
            one(index * GROUP + i)
        return carry

    lax.fori_loop(0, ROWS // GROUP, group, 0)


def finish(strength, decay, gate, vector_buf, value_buf, found_buf, normed_buf, update_ref):
    for first in range(0, ROWS, CHUNK):
        there = slice(first, first + CHUNK)

        def piece(ref, i):
            return ref[there, i * HEADS : (i + 1) * HEADS, :]

        def shaped(value):
            return value.reshape(CHUNK, HEADS, DV)

        key0, query0, key1, query1 = [piece(vector_buf, i) for i in range(4)]
        found0, found1, found2, found3 = [piece(found_buf, i) for i in range(4)]
        strength0, strength1 = [shaped(strength(step, first)) for step in range(2)]
        decay0, decay1 = [shaped(decay(step, first)) for step in range(2)]
        change0 = (value_buf[0, there] - decay0 * found0) * strength0
        read0 = decay0 * found1 + inner(query0, key0) * change0
        kept = decay0 * found2 + inner(key1, key0) * change0
        change1 = (value_buf[1, there] - decay1 * kept) * strength1
        kept = decay0 * found3 + inner(query1, key0) * change0
        read1 = decay1 * kept + inner(query1, key1) * change1
        for step, read in enumerate((read0, read1)):
            scale = lax.rsqrt(jnp.mean(read * read, axis=-1, keepdims=True) + 1e-06)
            normed = read * scale * shaped(gate(step, first))
            start = (step * ROWS + first) * HEADS
            normed_buf[start : start + CHUNK * HEADS, :] = normed.reshape(CHUNK * HEADS, DV)
        for i, value in enumerate((key0, key1, decay1 * change0, change1, decay0 * decay1)):
            update_ref[there, i * HEADS : (i + 1) * HEADS, :] = value


def flatten_heads(normed_buf, normed_ref):
    for h in range(HEADS):
        rows = normed_buf[pl.ds(h, 2 * ROWS, stride=HEADS), :]
        normed_ref[:, h * DV : (h + 1) * DV] = rows.astype(bf16)


def write_row(update, memory, store):
    key0, key1, change0, change1, decay = [
        update[i * HEADS : (i + 1) * HEADS] for i in range(5)
    ]
    (key0h, key0l), (key1h, key1l) = split(key0), split(key1)
    (change0h, change0l), (change1h, change1l) = split(change0), split(change1)
    left = jnp.concatenate([key0h, key0l, key0h, key1h, key1l, key1h], axis=0)
    left = left.T.astype(bf16)
    right = jnp.concatenate([change0h, change0h, change0l, change1h, change1h, change1l], axis=0)
    head = lax.broadcasted_iota(jnp.int32, right.shape, 0) % HEADS
    for h in range(0, HEADS, 2):
        pair = [jnp.where(head == h + i, right, 0.0).astype(bf16) for i in range(2)]
        added = dot(left, jnp.concatenate(pair, axis=1))
        for i in range(2):
            kept = memory(h + i).astype(f32) * decay[h + i : h + i + 1]
            store(h + i, (kept + added[:, i * DV : (i + 1) * DV]).astype(bf16))


def write_group(index, update_ref, memory_ref, target_ref):
    for i in range(GROUP):
        row = index * GROUP + i

        def store(h, value, row=row):
            target_ref[row, h * DK : (h + 1) * DK, :] = value

        write_row(
            update_ref[row], lambda h, row=row: memory_ref[row, h * DK : (h + 1) * DK, :], store
        )


def first_kernel(
    x, gain, tail_query, tail_key, tail_value, conv_query, conv_key, conv_value,
    w_query, w_key, w_value, w_gate, w_beta, w_decay, decay_log, dt_bias, state,
    late_query_ref, late_key_ref, late_value_ref, late_gate_ref, late_strength_ref, late_forget_ref,
    raw_ref, stored_ref, conv_ref, normed_ref, update_ref,
    x_buf, gain_buf, tail_query_buf, tail_key_buf, tail_value_buf,
    conv_query_buf, conv_key_buf, conv_value_buf,
    query_buf, key_buf, value_weight_buf, gate_weight_buf, beta_buf, decay_buf, decay_ref, bias_ref, state_buf,
    window_query, window_key, window_value, gate_all, strength_all, forget_all, stored_buf,
    vector_buf, value_buf, found_buf, normed_buf,
    small_sem, weight_sem, state_sem,
):
    rows = x_buf.shape[0]
    small = [
        pltpu.make_async_copy(source, target, small_sem.at[i])
        for i, (source, target) in enumerate(
            (
                (x, x_buf),
                (w_beta, beta_buf),
                (w_decay, decay_buf),
                (gain, gain_buf),
                (tail_query, tail_query_buf),
                (tail_key, tail_key_buf),
                (tail_value, tail_value_buf),
                (conv_query, conv_query_buf),
                (conv_key, conv_key_buf),
                (conv_value, conv_value_buf),
                (decay_log, decay_ref),
                (dt_bias, bias_ref),
            )
        )
    ]
    for copy in small:
        copy.start()

    def weights(j):
        pieces = (
            (w_query, query_buf, DK),
            (w_key, key_buf, DK),
            (w_value, value_weight_buf, 2 * DV),
            (w_gate, gate_weight_buf, 2 * DV),
        )
        copies = []
        for i, (hbm, buf, width) in enumerate(pieces):
            part = pl.ds(j * width, width)
            copies.append(
                pltpu.make_async_copy(hbm.at[:, part], buf.at[:, part], weight_sem.at[4 * j + i])
            )
        return copies

    def load(row):
        return pltpu.make_async_copy(state.at[row], state_buf.at[row], state_sem.at[row])

    def begin(j):
        if j < KEYS:
            for copy in weights(j):
                copy.start()
        elif j < KEYS + 2:
            for row in range((j - KEYS) * ROWS // 2, (j - KEYS + 1) * ROWS // 2):
                load(row).start()

    begin(0)
    begin(1)

    for copy in small:
        copy.wait()
    head = lax.broadcasted_iota(jnp.int32, (HEADS, DV), 0)
    rate, bias = jnp.zeros((HEADS, DV), f32), jnp.zeros((HEADS, DV), f32)
    for h in range(HEADS):
        rate = jnp.where(head == h, decay_ref[h], rate)
        bias = jnp.where(head == h, bias_ref[h], bias)
    rate = -jnp.exp(rate)
    x_all = x_buf[...]

    def spread(target, start, h, block):
        target[pl.ds(start * HEADS + h, block.shape[0], stride=HEADS), :] = block

    across = (((1,), (1,)), ((), ()))
    beta = lax.dot_general(x_all, beta_buf[...], across, preferred_element_type=f32)
    decay = lax.dot_general(x_all, decay_buf[...], across, preferred_element_type=f32)
    for h in range(HEADS):
        spread(strength_all, 0, h, jnp.broadcast_to(beta[:, h : h + 1], (rows, DV)))
        spread(forget_all, 0, h, jnp.broadcast_to(decay[:, h : h + 1], (rows, DV)))
    for first in range(0, rows, ROWS):
        there = slice(first * HEADS, (first + ROWS) * HEADS)
        strength_all[there] = jax.nn.sigmoid(strength_all[there])
        raised = forget_all[there].reshape(ROWS, HEADS, DV) + bias[None]
        forget = jnp.exp(rate[None] * jax.nn.softplus(raised))
        forget_all[there] = forget.reshape(ROWS * HEADS, DV)

    history = (TAPS - 1) * ROWS

    def place(window, h, before, fresh):
        spread(window, 0, h, before)
        spread(window, history, h, fresh)

    def keep(channel, before, fresh):
        after = jnp.concatenate([before[2 * ROWS :], fresh[: 2 * ROWS]], axis=0)
        for tap in range(TAPS - 1):
            stored_buf[pl.ds(tap * SLIM + channel, ROWS, stride=(TAPS - 1) * SLIM), :] = after[
                tap * ROWS : (tap + 1) * ROWS
            ]

    for kind, buf in enumerate((conv_query_buf, conv_key_buf, conv_value_buf)):
        wide = buf[...].astype(f32)
        for h in range(HEADS):
            channel = h if kind == 2 else h // 2
            taps = wide[:, channel * DV : (channel + 1) * DV]
            for tap in range(TAPS):
                conv_ref[kind, tap, h : h + 1, :] = taps[tap : tap + 1]

    for j in range(KEYS):
        for copy in weights(j):
            copy.wait()
        begin(j + 2)
        one, two = slice(j * DK, (j + 1) * DK), slice(2 * j * DV, 2 * (j + 1) * DV)
        query = dot(x_all, query_buf[:, one]).astype(bf16)
        key = dot(x_all, key_buf[:, one]).astype(bf16)
        value = dot(x_all, value_weight_buf[:, two]).astype(bf16)
        gate = dot(x_all, gate_weight_buf[:, two])
        raw_ref[:, j * DK : (j + 1) * DK] = query[2 * ROWS :]
        raw_ref[:, (KEYS + j) * DK : (KEYS + j + 1) * DK] = key[2 * ROWS :]
        raw_ref[:, 2 * (KEYS + j) * DK : 2 * (KEYS + j + 1) * DK] = value[2 * ROWS :]
        query, key, value = query.astype(f32), key.astype(f32), value.astype(f32)
        old_query = tail_query_buf[:, :, one].reshape(history, DK).astype(f32)
        old_key = tail_key_buf[:, :, one].reshape(history, DK).astype(f32)
        old_value = tail_value_buf[:, :, two].reshape(history, 2 * DV).astype(f32)
        gate = gate * jax.nn.sigmoid(gate)
        keep(j, old_query, query)
        keep(KEYS + j, old_key, key)
        for i in range(2):
            h, half = 2 * j + i, slice(i * DV, (i + 1) * DV)
            place(window_query, h, old_query, query)
            place(window_key, h, old_key, key)
            place(window_value, h, old_value[:, half], value[:, half])
            keep(2 * KEYS + h, old_value[:, half], value[:, half])
            spread(gate_all, 0, h, gate[:, half] * gain_buf[...])

    late = (history + 2 * ROWS) * HEADS
    late_query_ref[...] = window_query[late:, :]
    late_key_ref[...] = window_key[late:, :]
    late_value_ref[...] = window_value[late:, :]
    late_gate_ref[...] = gate_all[2 * ROWS * HEADS :, :]
    late_strength_ref[...] = strength_all[2 * ROWS * HEADS :, :]
    late_forget_ref[...] = forget_all[2 * ROWS * HEADS :, :]
    stored_ref[...] = stored_buf[...].reshape(stored_ref.shape).astype(bf16)

    windows = (window_query, window_key, window_value)
    find_vectors(
        lambda kind, tap, first: part_of(windows[kind], tap, first, CHUNK),
        conv_ref,
        vector_buf,
        value_buf,
    )
    recall(
        lambda row: load(row).wait(),
        lambda row, h: state_buf[row, h * DK : (h + 1) * DK, :],
        vector_buf,
        found_buf,
    )
    finish(
        lambda step, first: part_of(strength_all, step, first, CHUNK),
        lambda step, first: part_of(forget_all, step, first, CHUNK),
        lambda step, first: part_of(gate_all, step, first, CHUNK),
        vector_buf,
        value_buf,
        found_buf,
        normed_buf,
        update_ref,
    )
    flatten_heads(normed_buf, normed_ref)


def send_kernel(
    wanted_ref, update_ref, tails_ref, state, slots, state_buf, stored_buf, state_sem, slot_sem
):
    count = slots.shape[0]

    def load(row):
        return pltpu.make_async_copy(state.at[row], state_buf.at[row], state_sem.at[row])

    for row in range(ROWS):
        load(row).start()

    def ship(slot, row):
        return (
            pltpu.make_async_copy(
                stored_buf.at[row], slots.at[slot, pl.ds(0, BODY)], slot_sem.at[0, slot]
            ),
            pltpu.make_async_copy(
                tails_ref.at[row], slots.at[slot, pl.ds(BODY, SLOT - BODY)], slot_sem.at[1, slot]
            ),
        )

    def group(index, carry):
        for i in range(GROUP):
            load(index * GROUP + i).wait()
        write_group(index, update_ref, state_buf, stored_buf)

        def begin(slot, carry):
            row = wanted_ref[slot, 0, 0]

            @pl.when((row >= index * GROUP) & (row < (index + 1) * GROUP))
            def _():
                for copy in ship(slot, row):
                    copy.start()

            return carry

        return lax.fori_loop(0, count, begin, carry)

    lax.fori_loop(0, ROWS // GROUP, group, 0)

    def end(slot, carry):
        @pl.when(wanted_ref[slot, 0, 0] >= 0)
        def _():
            for copy in ship(slot, 0):
                copy.wait()

        return carry

    lax.fori_loop(0, count, end, 0)


def second_kernel(
    slot_ref, late_query, late_key, late_value, late_gate, late_strength, late_forget, conv_ref, early_ref, slots, w_out,
    *refs,
):
    sums = refs[:PARTS]
    (
        update_ref, last_ref, memory_buf,
        tail_buf, window_query, window_key, window_value,
        vector_buf, value_buf, found_buf, normed_buf, out_buf, normed_ref,
        tail_sem, memory_sem, out_sem,
    ) = refs[PARTS:]
    def load_tail(row):
        return pltpu.make_async_copy(
            slots.at[slot_ref[row], pl.ds(BODY, SLOT - BODY)], tail_buf.at[row], tail_sem.at[row]
        )

    def load(row):
        return pltpu.make_async_copy(
            slots.at[slot_ref[row], pl.ds(0, BODY)], memory_buf.at[row], memory_sem.at[row]
        )

    for row in range(ROWS):
        load_tail(row).start()
    for row in range(ROWS):
        load(row).start()
    width = out_buf.shape[2]
    place = lax.axis_index("tensor")

    def load_out(shift):
        start = pl.multiple_of((place + shift) % PARTS * width, width)
        return pltpu.make_async_copy(
            w_out.at[:, pl.ds(start, width)], out_buf.at[shift], out_sem.at[shift]
        )

    for shift in range(PARTS):
        load_out(shift).start()
    wide = widening()
    for row in range(ROWS):
        load_tail(row).wait()
    for row in range(ROWS):
        tails = tail_buf[row]
        last_ref[row] = tails[2 * SLIM :]
        spread = dot(wide, tails)
        for tap in range(TAPS - 1):
            for kind, window in enumerate((window_query, window_key, window_value)):
                start = tap * WIDE + kind * HEADS
                window[(tap * ROWS + row) * HEADS : (tap * ROWS + row + 1) * HEADS, :] = spread[
                    start : start + HEADS
                ]
    windows = (window_query, window_key, window_value)
    fresh = (late_query, late_key, late_value)

    def window(kind, tap, first):
        if tap < TAPS - 1:
            return part_of(windows[kind], tap, first, CHUNK)
        return part_of(fresh[kind], tap - (TAPS - 1), first, CHUNK)

    find_vectors(window, conv_ref, vector_buf, value_buf)
    recall(
        lambda row: load(row).wait(),
        lambda row, h: memory_buf[row, h * DK : (h + 1) * DK, :],
        vector_buf,
        found_buf,
    )
    finish(
        lambda step, first: part_of(late_strength, step, first, CHUNK),
        lambda step, first: part_of(late_forget, step, first, CHUNK),
        lambda step, first: part_of(late_gate, step, first, CHUNK),
        vector_buf,
        value_buf,
        found_buf,
        normed_buf,
        update_ref,
    )
    normed_ref[: 2 * ROWS, :] = early_ref[...]
    flatten_heads(normed_buf, normed_ref.at[2 * ROWS :])
    for shift in range(PARTS):
        load_out(shift).wait()
    normed = normed_ref[...]
    for shift in range(PARTS):
        sums[shift][...] = dot(normed, out_buf[shift])


def final_kernel(
    update_ref, last_ref, raw_ref, memory_ref,
    final, query_ref, key_ref, value_ref,
    final_buf, last_buf, final_sem,
):
    def save(row):
        return pltpu.make_async_copy(final_buf.at[row], final.at[row], final_sem.at[row])

    start = 0
    last_buf[...] = last_ref[...].astype(f32).reshape(ROWS * SLIM, DV)
    for ref in (query_ref, key_ref, value_ref):
        width = ref.shape[2]
        for channel in range(width // DV):
            block = last_buf[pl.ds(start // DV + channel, ROWS, stride=SLIM), :]
            ref[0, :, channel * DV : (channel + 1) * DV] = block.astype(bf16)
        for step in range(2):
            ref[1 + step] = raw_ref[step * ROWS : (step + 1) * ROWS, start : start + width]
        start += width

    def group(index, carry):
        write_group(index, update_ref, memory_ref, final_buf)
        for i in range(GROUP):
            save(index * GROUP + i).start()
        return carry

    lax.fori_loop(0, ROWS // GROUP, group, 0)
    for row in range(ROWS):
        save(row).wait()


VMEM = pl.BlockSpec(memory_space=pltpu.VMEM)
SMEM = pl.BlockSpec(memory_space=pltpu.SMEM)
HBM = pl.BlockSpec(memory_space=pltpu.HBM)
PARAMS = pltpu.CompilerParams(vmem_limit_bytes=VMEM_BYTES)


def in_hbm(array):
    return pltpu.with_memory_space_constraint(array, pltpu.HBM)


def shape(dims, kind):
    return jax.ShapeDtypeStruct(dims, kind)


def buffer(array):
    return pltpu.VMEM(array.shape, array.dtype)


def work_buffers():
    return [
        pltpu.VMEM((ROWS, 4 * HEADS, DV), f32),
        pltpu.VMEM((2, ROWS, HEADS, DV), f32),
        pltpu.VMEM((ROWS, 4 * HEADS, DV), f32),
        pltpu.VMEM((2 * ROWS * HEADS, DV), f32),
    ]


def first_half(arrays, state):
    rows = arrays[0].shape[0]
    late = rows // 2
    window = pltpu.VMEM(((TAPS - 1) * ROWS * HEADS + rows * HEADS, DV), f32)
    wide = pltpu.VMEM((rows * HEADS, DV), f32)
    return pl.pallas_call(
        first_kernel,
        in_specs=[HBM] * (len(arrays) + 1),
        out_specs=[VMEM] * 11,
        out_shape=(
            *[shape((late * HEADS, DV), f32)] * 6,
            shape((late, SLIM * DV), bf16),
            shape((ROWS, (TAPS - 1) * SLIM, DV), bf16),
            shape((3, TAPS, HEADS, DV), f32),
            shape((late, HEADS * DV), bf16),
            shape((ROWS, 5 * HEADS, DV), f32),
        ),
        scratch_shapes=[
            *[buffer(array) for array in arrays[:-2]],
            *[pltpu.SMEM(array.shape, f32) for array in arrays[-2:]],
            buffer(state),
            window,
            window,
            window,
            wide,
            wide,
            wide,
            pltpu.VMEM((ROWS * (TAPS - 1) * SLIM, DV), f32),
            *work_buffers(),
            pltpu.SemaphoreType.DMA((12,)),
            pltpu.SemaphoreType.DMA((4 * KEYS,)),
            pltpu.SemaphoreType.DMA((ROWS,)),
        ],
        compiler_params=PARAMS,
        name="first_half",
    )(*[in_hbm(array) for array in arrays], in_hbm(state))


def fill_slots(wanted, update, tails, state):
    return pl.pallas_call(
        send_kernel,
        in_specs=[SMEM, VMEM, VMEM, HBM],
        out_specs=HBM,
        out_shape=shape((wanted.shape[0], SLOT, DV), bf16),
        scratch_shapes=[
            buffer(state),
            buffer(state),
            pltpu.SemaphoreType.DMA((ROWS,)),
            pltpu.SemaphoreType.DMA((2, wanted.shape[0])),
        ],
        compiler_params=PARAMS,
        name="fill_slots",
    )(wanted, update, tails, in_hbm(state))


def second_half(slot_of_row, late, conv, normed, slots, w_out):
    window = pltpu.VMEM(((TAPS - 1) * ROWS * HEADS, DV), f32)
    rows, width = 2 * normed.shape[0], w_out.shape[1] // PARTS
    *sums, update, last, memory = pl.pallas_call(
        second_kernel,
        in_specs=[SMEM] + [VMEM] * 8 + [HBM] * 2,
        out_specs=[VMEM] * (PARTS + 3),
        out_shape=(
            *[shape((rows, width), f32)] * PARTS,
            shape((ROWS, 5 * HEADS, DV), f32),
            shape((ROWS, SLIM, DV), bf16),
            shape((ROWS, BODY, DV), bf16),
        ),
        scratch_shapes=[
            pltpu.VMEM((ROWS, SLOT - BODY, DV), bf16),
            window,
            window,
            window,
            *work_buffers(),
            pltpu.VMEM((PARTS, w_out.shape[0], width), bf16),
            pltpu.VMEM((rows, normed.shape[1]), bf16),
            pltpu.SemaphoreType.DMA((ROWS,)),
            pltpu.SemaphoreType.DMA((ROWS,)),
            pltpu.SemaphoreType.DMA((PARTS,)),
        ],
        compiler_params=PARAMS,
        name="second_half",
    )(slot_of_row, *late, conv, normed, in_hbm(slots), in_hbm(w_out))
    return sums, update, last, memory


def last_memory(update, last, raw, memory):
    return pl.pallas_call(
        final_kernel,
        in_specs=[VMEM] * 4,
        out_specs=[HBM] + [VMEM] * 3,
        out_shape=(
            shape((ROWS, BODY, DV), bf16),
            shape((TAPS - 1, ROWS, KEYS * DK), bf16),
            shape((TAPS - 1, ROWS, KEYS * DK), bf16),
            shape((TAPS - 1, ROWS, HEADS * DV), bf16),
        ),
        scratch_shapes=[
            buffer(memory),
            pltpu.VMEM((ROWS * SLIM, DV), f32),
            pltpu.SemaphoreType.DMA((ROWS,)),
        ],
        compiler_params=PARAMS,
        name="last_memory",
    )(update, last, raw, memory)


def sum_heads(blocks):
    total = blocks[0]
    for shift in range(1, PARTS):
        pairs = [(i, (i + shift) % PARTS) for i in range(PARTS)]
        total = total + lax.ppermute(blocks[shift], "tensor", pairs)
    return total.astype(bf16)


def per_device(
    inputs,
    w_query,
    w_key,
    w_value,
    w_gate_z,
    w_beta,
    w_decay,
    conv_query,
    conv_key,
    conv_value,
    decay_log,
    dt_bias,
    norm_gain,
    w_out,
    state,
    tail_query,
    tail_key,
    tail_value,
    parents,
):
    groups = lax.axis_size("branch")
    source, offset = parents // ROWS, parents % ROWS
    hits = source[:, None] == jnp.arange(groups, dtype=jnp.int32)[None, :]
    wanted = jnp.sum(jnp.where(hits, offset[:, None] + 1, 0), axis=0) - 1
    requested = lax.all_to_all(
        wanted.reshape(groups, 1, 1), "branch", split_axis=0, concat_axis=0, tiled=True
    )

    flat_state = state.reshape(ROWS, BODY, DV)
    *late, raw, stored_tails, conv, normed, update = first_half(
        (
            inputs.reshape(-1, inputs.shape[-1]),
            norm_gain[None],
            tail_query.transpose(1, 0, 2),
            tail_key.transpose(1, 0, 2),
            tail_value.transpose(1, 0, 2),
            conv_query,
            conv_key,
            conv_value,
            w_query,
            w_key,
            w_value,
            w_gate_z,
            w_beta.T,
            w_decay.T,
            decay_log,
            dt_bias,
        ),
        flat_state,
    )
    shipped = fill_slots(requested, update, stored_tails, flat_state)
    arrived = lax.all_to_all(shipped, "branch", split_axis=0, concat_axis=0, tiled=True)

    sums, update, last, memory = second_half(source, late, conv, normed, arrived, w_out)
    out_rows = sum_heads(sums).reshape(inputs.shape[0], ROWS, -1)
    final_state, *final_tails = last_memory(update, last, raw, memory)
    return (
        out_rows,
        final_state.reshape(state.shape),
        *[tail.transpose(1, 0, 2) for tail in final_tails],
    )


def solution(mesh):
    return jax.shard_map(
        per_device,
        mesh=mesh,
        in_specs=(
            P(None, "branch", None),
            P(None, "tensor"),
            P(None, "tensor"),
            P(None, "tensor"),
            P(None, "tensor"),
            P(None, "tensor"),
            P(None, "tensor"),
            P(None, "tensor"),
            P(None, "tensor"),
            P(None, "tensor"),
            P("tensor"),
            P("tensor"),
            P(),
            P("tensor", None),
            P("branch", "tensor", None, None),
            P("branch", None, "tensor"),
            P("branch", None, "tensor"),
            P("branch", None, "tensor"),
            P("branch"),
        ),
        out_specs=(
            P(None, "branch", "tensor"),
            P("branch", "tensor", None, None),
            P("branch", None, "tensor"),
            P("branch", None, "tensor"),
            P("branch", None, "tensor"),
        ),
        check_vma=False,
    )
```

```python
import jax
import jax.numpy as jnp
from jax import lax
from jax.experimental import pallas as pl
from jax.experimental.pallas import tpu as pltpu
from jax.sharding import PartitionSpec as P

DK = 128
DV = 128
HEADS = 8
KEYS = 4
ROWS = 16
TAPS = 4
WIDE = 3 * HEADS
SLIM = 2 * KEYS + HEADS
BODY = HEADS * DK
SLOT = BODY + (TAPS - 1) * SLIM
VMEM_BYTES = 48 * 1024 * 1024
CHUNK = 4
PARTS = 4
GROUP = 8
f32 = jnp.float32
bf16 = jnp.bfloat16


def split(value):
    high = value.astype(bf16).astype(f32)
    return high, value - high


def dot(left, right):
    return jnp.dot(left, right, preferred_element_type=f32)


def inner(left, right):
    return jnp.sum(left * right, axis=-1, keepdims=True)


def widening():
    row = lax.broadcasted_iota(jnp.int32, ((TAPS - 1) * WIDE, (TAPS - 1) * SLIM), 0)
    column = lax.broadcasted_iota(jnp.int32, ((TAPS - 1) * WIDE, (TAPS - 1) * SLIM), 1)
    tap, place = row // WIDE, row % WIDE
    origin = tap * SLIM + jnp.where(place < 2 * HEADS, place // 2, place - HEADS)
    return jnp.where(origin == column, 1.0, 0.0).astype(bf16)


def spread(target, start, h, block):
    target[pl.ds(start * HEADS + h, block.shape[0], stride=HEADS), :] = block


def part_of(ref, index, first, count):
    return ref[pl.ds(index * ROWS * HEADS + first * HEADS, count * HEADS), :]


def find_vectors(window, conv_ref, vector_buf, value_buf):
    for first in range(0, ROWS, CHUNK):
        there = slice(first, first + CHUNK)
        for step in range(2):
            for kind in range(3):
                mixed = 0.0
                for tap in range(TAPS):
                    rows = window(kind, step + tap, first).reshape(CHUNK, HEADS, DV)
                    mixed = mixed + rows * conv_ref[kind, tap][None]
                mixed = mixed * jax.nn.sigmoid(mixed)
                if kind == 2:
                    value_buf[step, there] = mixed
                    continue
                unit = mixed * lax.rsqrt(inner(mixed, mixed) + 1e-06)
                if kind == 0:
                    unit = unit * DK ** (-0.5)
                place = 2 * step + 1 - kind
                vector_buf[there, place * HEADS : (place + 1) * HEADS, :] = unit


def recall(wait, memory, vector_buf, found_buf):
    head = lax.broadcasted_iota(jnp.int32, (HEADS, DV), 0)

    def one(row):
        high, low = split(vector_buf[row])
        left = jnp.concatenate([high, low], axis=0).astype(bf16)
        found = [jnp.zeros((HEADS, DV), f32)] * 4
        for h in range(0, HEADS, 2):
            pair = jnp.concatenate([memory(row, h), memory(row, h + 1)], axis=1)
            product = dot(left, pair)
            product = product[: 4 * HEADS] + product[4 * HEADS :]
            for i in range(4):
                block = product[i * HEADS : (i + 1) * HEADS]
                found[i] = jnp.where(head == h, block[:, :DV], found[i])
                found[i] = jnp.where(head == h + 1, block[:, DV:], found[i])
        found_buf[row] = jnp.concatenate(found, axis=0)

    def group(index, carry):
        for i in range(GROUP):
            wait(index * GROUP + i)
        for i in range(GROUP):
            one(index * GROUP + i)
        return carry

    lax.fori_loop(0, ROWS // GROUP, group, 0)


def finish(strength, decay, gate, vector_buf, value_buf, found_buf, normed_buf, update_ref):
    for first in range(0, ROWS, CHUNK):
        there = slice(first, first + CHUNK)

        def piece(ref, i):
            return ref[there, i * HEADS : (i + 1) * HEADS, :]

        def shaped(value):
            return value.reshape(CHUNK, HEADS, DV)

        key0, query0, key1, query1 = [piece(vector_buf, i) for i in range(4)]
        found0, found1, found2, found3 = [piece(found_buf, i) for i in range(4)]
        strength0, strength1 = [shaped(strength(step, first)) for step in range(2)]
        decay0, decay1 = [shaped(decay(step, first)) for step in range(2)]
        change0 = (value_buf[0, there] - decay0 * found0) * strength0
        read0 = decay0 * found1 + inner(query0, key0) * change0
        kept = decay0 * found2 + inner(key1, key0) * change0
        change1 = (value_buf[1, there] - decay1 * kept) * strength1
        kept = decay0 * found3 + inner(query1, key0) * change0
        read1 = decay1 * kept + inner(query1, key1) * change1
        for step, read in enumerate((read0, read1)):
            scale = lax.rsqrt(jnp.mean(read * read, axis=-1, keepdims=True) + 1e-06)
            normed = read * scale
            if gate is not None:
                normed = normed * shaped(gate(step, first))
            start = (step * ROWS + first) * HEADS
            normed_buf[start : start + CHUNK * HEADS, :] = normed.reshape(CHUNK * HEADS, DV)
        for i, value in enumerate((key0, key1, decay1 * change0, change1, decay0 * decay1)):
            update_ref[there, i * HEADS : (i + 1) * HEADS, :] = value


def flatten_heads(normed_buf, normed_ref):
    for h in range(HEADS):
        rows = normed_buf[pl.ds(h, 2 * ROWS, stride=HEADS), :]
        normed_ref[:, h * DV : (h + 1) * DV] = rows.astype(bf16)


def write_row(update, memory, store):
    key0, key1, change0, change1, decay = [
        update[i * HEADS : (i + 1) * HEADS] for i in range(5)
    ]
    (key0h, key0l), (key1h, key1l) = split(key0), split(key1)
    (change0h, change0l), (change1h, change1l) = split(change0), split(change1)
    left = jnp.concatenate([key0h, key0l, key0h, key1h, key1l, key1h], axis=0)
    left = left.T.astype(bf16)
    right = jnp.concatenate([change0h, change0h, change0l, change1h, change1h, change1l], axis=0)
    head = lax.broadcasted_iota(jnp.int32, right.shape, 0) % HEADS
    for h in range(0, HEADS, 2):
        pair = [jnp.where(head == h + i, right, 0.0).astype(bf16) for i in range(2)]
        added = dot(left, jnp.concatenate(pair, axis=1))
        for i in range(2):
            kept = memory(h + i).astype(f32) * decay[h + i : h + i + 1]
            store(h + i, (kept + added[:, i * DV : (i + 1) * DV]).astype(bf16))


def write_group(index, update_ref, memory_ref, target_ref):
    for i in range(GROUP):
        row = index * GROUP + i

        def store(h, value, row=row):
            target_ref[row, h * DK : (h + 1) * DK, :] = value

        write_row(
            update_ref[row], lambda h, row=row: memory_ref[row, h * DK : (h + 1) * DK, :], store
        )


def first_kernel(
    x, tail_query, tail_key, tail_value, conv_query, conv_key, conv_value,
    w_query, w_key, w_value, w_beta, w_decay, decay_log, dt_bias, state,
    late_query_ref, late_key_ref, late_value_ref, late_strength_ref, late_forget_ref,
    raw_ref, stored_ref, conv_ref, normed_buf, update_ref,
    x_buf, tail_query_buf, tail_key_buf, tail_value_buf,
    conv_query_buf, conv_key_buf, conv_value_buf,
    query_buf, key_buf, value_weight_buf, beta_buf, decay_buf, decay_ref, bias_ref, state_buf,
    window_query, window_key, window_value, strength_all, forget_all, stored_buf,
    vector_buf, value_buf, found_buf,
    small_sem, weight_sem, state_sem,
):
    rows = x_buf.shape[0]
    small = [
        pltpu.make_async_copy(source, target, small_sem.at[i])
        for i, (source, target) in enumerate(
            (
                (x, x_buf),
                (w_beta, beta_buf),
                (w_decay, decay_buf),
                (tail_query, tail_query_buf),
                (tail_key, tail_key_buf),
                (tail_value, tail_value_buf),
                (conv_query, conv_query_buf),
                (conv_key, conv_key_buf),
                (conv_value, conv_value_buf),
                (decay_log, decay_ref),
                (dt_bias, bias_ref),
            )
        )
    ]
    for copy in small:
        copy.start()

    def weights(j):
        pieces = (
            (w_query, query_buf, DK),
            (w_key, key_buf, DK),
            (w_value, value_weight_buf, 2 * DV),
        )
        copies = []
        for i, (hbm, buf, width) in enumerate(pieces):
            part = pl.ds(j * width, width)
            copies.append(
                pltpu.make_async_copy(hbm.at[:, part], buf.at[:, part], weight_sem.at[3 * j + i])
            )
        return copies

    def load(row):
        return pltpu.make_async_copy(state.at[row], state_buf.at[row], state_sem.at[row])

    def begin(j):
        if j < KEYS:
            for copy in weights(j):
                copy.start()
        elif j < KEYS + 2:
            for row in range((j - KEYS) * ROWS // 2, (j - KEYS + 1) * ROWS // 2):
                load(row).start()

    begin(0)
    begin(1)

    for copy in small:
        copy.wait()
    head = lax.broadcasted_iota(jnp.int32, (HEADS, DV), 0)
    rate, bias = jnp.zeros((HEADS, DV), f32), jnp.zeros((HEADS, DV), f32)
    for h in range(HEADS):
        rate = jnp.where(head == h, decay_ref[h], rate)
        bias = jnp.where(head == h, bias_ref[h], bias)
    rate = -jnp.exp(rate)
    x_all = x_buf[...]

    across = (((1,), (1,)), ((), ()))
    beta = lax.dot_general(x_all, beta_buf[...], across, preferred_element_type=f32)
    decay = lax.dot_general(x_all, decay_buf[...], across, preferred_element_type=f32)
    for h in range(HEADS):
        spread(strength_all, 0, h, jnp.broadcast_to(beta[:, h : h + 1], (rows, DV)))
        spread(forget_all, 0, h, jnp.broadcast_to(decay[:, h : h + 1], (rows, DV)))
    for first in range(0, rows, ROWS):
        there = slice(first * HEADS, (first + ROWS) * HEADS)
        strength_all[there] = jax.nn.sigmoid(strength_all[there])
        raised = forget_all[there].reshape(ROWS, HEADS, DV) + bias[None]
        forget = jnp.exp(rate[None] * jax.nn.softplus(raised))
        forget_all[there] = forget.reshape(ROWS * HEADS, DV)

    history = (TAPS - 1) * ROWS

    def place(window, h, before, fresh):
        spread(window, 0, h, before)
        spread(window, history, h, fresh)

    def keep(channel, before, fresh):
        after = jnp.concatenate([before[2 * ROWS :], fresh[: 2 * ROWS]], axis=0)
        for tap in range(TAPS - 1):
            stored_buf[pl.ds(tap * SLIM + channel, ROWS, stride=(TAPS - 1) * SLIM), :] = after[
                tap * ROWS : (tap + 1) * ROWS
            ]

    for kind, buf in enumerate((conv_query_buf, conv_key_buf, conv_value_buf)):
        wide = buf[...].astype(f32)
        for h in range(HEADS):
            channel = h if kind == 2 else h // 2
            taps = wide[:, channel * DV : (channel + 1) * DV]
            for tap in range(TAPS):
                conv_ref[kind, tap, h : h + 1, :] = taps[tap : tap + 1]

    for j in range(KEYS):
        for copy in weights(j):
            copy.wait()
        begin(j + 2)
        one, two = slice(j * DK, (j + 1) * DK), slice(2 * j * DV, 2 * (j + 1) * DV)
        query = dot(x_all, query_buf[:, one]).astype(bf16)
        key = dot(x_all, key_buf[:, one]).astype(bf16)
        value = dot(x_all, value_weight_buf[:, two]).astype(bf16)
        raw_ref[:, j * DK : (j + 1) * DK] = query[2 * ROWS :]
        raw_ref[:, (KEYS + j) * DK : (KEYS + j + 1) * DK] = key[2 * ROWS :]
        raw_ref[:, 2 * (KEYS + j) * DK : 2 * (KEYS + j + 1) * DK] = value[2 * ROWS :]
        query, key, value = query.astype(f32), key.astype(f32), value.astype(f32)
        old_query = tail_query_buf[:, :, one].reshape(history, DK).astype(f32)
        old_key = tail_key_buf[:, :, one].reshape(history, DK).astype(f32)
        old_value = tail_value_buf[:, :, two].reshape(history, 2 * DV).astype(f32)
        keep(j, old_query, query)
        keep(KEYS + j, old_key, key)
        for i in range(2):
            h, half = 2 * j + i, slice(i * DV, (i + 1) * DV)
            place(window_query, h, old_query, query)
            place(window_key, h, old_key, key)
            place(window_value, h, old_value[:, half], value[:, half])
            keep(2 * KEYS + h, old_value[:, half], value[:, half])

    late = (history + 2 * ROWS) * HEADS
    late_query_ref[...] = window_query[late:, :]
    late_key_ref[...] = window_key[late:, :]
    late_value_ref[...] = window_value[late:, :]
    late_strength_ref[...] = strength_all[2 * ROWS * HEADS :, :]
    late_forget_ref[...] = forget_all[2 * ROWS * HEADS :, :]
    stored_ref[...] = stored_buf[...].reshape(stored_ref.shape).astype(bf16)

    windows = (window_query, window_key, window_value)
    find_vectors(
        lambda kind, tap, first: part_of(windows[kind], tap, first, CHUNK),
        conv_ref,
        vector_buf,
        value_buf,
    )
    recall(
        lambda row: load(row).wait(),
        lambda row, h: state_buf[row, h * DK : (h + 1) * DK, :],
        vector_buf,
        found_buf,
    )
    finish(
        lambda step, first: part_of(strength_all, step, first, CHUNK),
        lambda step, first: part_of(forget_all, step, first, CHUNK),
        None,
        vector_buf,
        value_buf,
        found_buf,
        normed_buf,
        update_ref,
    )


def gate_kernel(
    x, gain, w_gate, read_ref, late_ref, normed_ref, x_buf, gain_buf, weight_buf, gate_all, small_sem, weight_sem
):
    small = [
        pltpu.make_async_copy(x, x_buf, small_sem.at[0]),
        pltpu.make_async_copy(gain, gain_buf, small_sem.at[1]),
    ]
    for copy in small:
        copy.start()
    copies = []
    for j in range(KEYS):
        part = pl.ds(2 * j * DV, 2 * DV)
        copies.append(
            pltpu.make_async_copy(w_gate.at[:, part], weight_buf.at[:, part], weight_sem.at[j])
        )
        copies[j].start()
    for copy in small:
        copy.wait()
    for j in range(KEYS):
        copies[j].wait()
        gate = dot(x_buf[...], weight_buf[:, 2 * j * DV : 2 * (j + 1) * DV])
        gate = gate * jax.nn.sigmoid(gate)
        for i in range(2):
            spread(gate_all, 0, 2 * j + i, gate[:, i * DV : (i + 1) * DV] * gain_buf[...])
    half = 2 * ROWS * HEADS
    late_ref[...] = gate_all[half:, :]
    gate_all[:half, :] = gate_all[:half, :] * read_ref[...]
    flatten_heads(gate_all, normed_ref)


def ask_kernel(parent_ref, wanted_ref):
    slot = lax.broadcasted_iota(jnp.int32, wanted_ref.shape, 0)
    wanted = jnp.full(wanted_ref.shape, -1, jnp.int32)
    for row in range(ROWS):
        parent = parent_ref[row]
        wanted = jnp.where(slot == parent // ROWS, parent % ROWS, wanted)
    wanted_ref[...] = wanted


def send_kernel(
    wanted_ref, update_ref, tails_ref, state, slots, state_buf, stored_buf, state_sem, slot_sem
):
    count = slots.shape[0]

    def load(row):
        return pltpu.make_async_copy(state.at[row], state_buf.at[row], state_sem.at[row])

    for row in range(ROWS):
        load(row).start()

    def ship(slot, row):
        return (
            pltpu.make_async_copy(
                stored_buf.at[row], slots.at[slot, pl.ds(0, BODY)], slot_sem.at[0, slot]
            ),
            pltpu.make_async_copy(
                tails_ref.at[row], slots.at[slot, pl.ds(BODY, SLOT - BODY)], slot_sem.at[1, slot]
            ),
        )

    def group(index, carry):
        for i in range(GROUP):
            load(index * GROUP + i).wait()
        write_group(index, update_ref, state_buf, stored_buf)

        def begin(slot, carry):
            row = wanted_ref[slot, 0, 0]

            @pl.when((row >= index * GROUP) & (row < (index + 1) * GROUP))
            def _():
                for copy in ship(slot, row):
                    copy.start()

            return carry

        return lax.fori_loop(0, count, begin, carry)

    lax.fori_loop(0, ROWS // GROUP, group, 0)

    def end(slot, carry):
        @pl.when(wanted_ref[slot, 0, 0] >= 0)
        def _():
            for copy in ship(slot, 0):
                copy.wait()

        return carry

    lax.fori_loop(0, count, end, 0)


def second_kernel(
    parent_ref, late_query, late_key, late_value, late_strength, late_forget, late_gate, conv_ref, early_ref, slots, w_out,
    *refs,
):
    sums = refs[:PARTS]
    (
        update_ref, last_ref, memory_buf,
        tail_buf, window_query, window_key, window_value,
        vector_buf, value_buf, found_buf, normed_buf, out_buf, normed_ref,
        tail_sem, memory_sem, out_sem,
    ) = refs[PARTS:]
    def load_tail(row):
        return pltpu.make_async_copy(
            slots.at[parent_ref[row] // ROWS, pl.ds(BODY, SLOT - BODY)], tail_buf.at[row], tail_sem.at[row]
        )

    def load(row):
        return pltpu.make_async_copy(
            slots.at[parent_ref[row] // ROWS, pl.ds(0, BODY)], memory_buf.at[row], memory_sem.at[row]
        )

    for row in range(ROWS):
        load_tail(row).start()
    for row in range(ROWS):
        load(row).start()
    width = out_buf.shape[2]
    place = lax.axis_index("tensor")

    def load_out(shift):
        start = pl.multiple_of((place + shift) % PARTS * width, width)
        return pltpu.make_async_copy(
            w_out.at[:, pl.ds(start, width)], out_buf.at[shift], out_sem.at[shift]
        )

    for shift in range(PARTS):
        load_out(shift).start()
    wide = widening()
    for row in range(ROWS):
        load_tail(row).wait()
    for row in range(ROWS):
        tails = tail_buf[row]
        last_ref[row] = tails[2 * SLIM :]
        spaced = dot(wide, tails)
        for tap in range(TAPS - 1):
            for kind, window in enumerate((window_query, window_key, window_value)):
                start = tap * WIDE + kind * HEADS
                window[(tap * ROWS + row) * HEADS : (tap * ROWS + row + 1) * HEADS, :] = spaced[
                    start : start + HEADS
                ]
    windows = (window_query, window_key, window_value)
    fresh = (late_query, late_key, late_value)

    def window(kind, tap, first):
        if tap < TAPS - 1:
            return part_of(windows[kind], tap, first, CHUNK)
        return part_of(fresh[kind], tap - (TAPS - 1), first, CHUNK)

    find_vectors(window, conv_ref, vector_buf, value_buf)
    recall(
        lambda row: load(row).wait(),
        lambda row, h: memory_buf[row, h * DK : (h + 1) * DK, :],
        vector_buf,
        found_buf,
    )
    finish(
        lambda step, first: part_of(late_strength, step, first, CHUNK),
        lambda step, first: part_of(late_forget, step, first, CHUNK),
        lambda step, first: part_of(late_gate, step, first, CHUNK),
        vector_buf,
        value_buf,
        found_buf,
        normed_buf,
        update_ref,
    )
    normed_ref[: 2 * ROWS, :] = early_ref[...]
    flatten_heads(normed_buf, normed_ref.at[2 * ROWS :])
    for shift in range(PARTS):
        load_out(shift).wait()
    normed = normed_ref[...]
    for shift in range(PARTS):
        sums[shift][...] = dot(normed, out_buf[shift]).astype(sums[shift].dtype)


def final_kernel(
    update_ref, last_ref, raw_ref, memory_ref,
    final, query_ref, key_ref, value_ref,
    final_buf, last_buf, final_sem,
):
    def save(row):
        return pltpu.make_async_copy(final_buf.at[row], final.at[row], final_sem.at[row])

    start = 0
    last_buf[...] = last_ref[...].astype(f32).reshape(ROWS * SLIM, DV)
    for ref in (query_ref, key_ref, value_ref):
        width = ref.shape[2]
        for channel in range(width // DV):
            block = last_buf[pl.ds(start // DV + channel, ROWS, stride=SLIM), :]
            ref[0, :, channel * DV : (channel + 1) * DV] = block.astype(bf16)
        for step in range(2):
            ref[1 + step] = raw_ref[step * ROWS : (step + 1) * ROWS, start : start + width]
        start += width

    def group(index, carry):
        write_group(index, update_ref, memory_ref, final_buf)
        for i in range(GROUP):
            save(index * GROUP + i).start()
        return carry

    lax.fori_loop(0, ROWS // GROUP, group, 0)
    for row in range(ROWS):
        save(row).wait()


VMEM = pl.BlockSpec(memory_space=pltpu.VMEM)
SMEM = pl.BlockSpec(memory_space=pltpu.SMEM)
HBM = pl.BlockSpec(memory_space=pltpu.HBM)
PARAMS = pltpu.CompilerParams(vmem_limit_bytes=VMEM_BYTES)


def in_hbm(array):
    return pltpu.with_memory_space_constraint(array, pltpu.HBM)


def shape(dims, kind):
    return jax.ShapeDtypeStruct(dims, kind)


def buffer(array):
    return pltpu.VMEM(array.shape, array.dtype)


def work_buffers():
    return [
        pltpu.VMEM((ROWS, 4 * HEADS, DV), f32),
        pltpu.VMEM((2, ROWS, HEADS, DV), f32),
        pltpu.VMEM((ROWS, 4 * HEADS, DV), f32),
        pltpu.VMEM((2 * ROWS * HEADS, DV), f32),
    ]


def ask(parents, groups):
    return pl.pallas_call(
        ask_kernel,
        in_specs=[SMEM],
        out_specs=VMEM,
        out_shape=shape((groups, 1, DV), jnp.int32),
        name="ask",
    )(parents)


def first_half(arrays, state):
    rows = arrays[0].shape[0]
    late = rows // 2
    window = pltpu.VMEM(((TAPS - 1) * ROWS * HEADS + rows * HEADS, DV), f32)
    wide = pltpu.VMEM((rows * HEADS, DV), f32)
    vectors, values, found, _ = work_buffers()
    return pl.pallas_call(
        first_kernel,
        in_specs=[HBM] * (len(arrays) + 1),
        out_specs=[VMEM] * 10,
        out_shape=(
            *[shape((late * HEADS, DV), f32)] * 5,
            shape((late, SLIM * DV), bf16),
            shape((ROWS, (TAPS - 1) * SLIM, DV), bf16),
            shape((3, TAPS, HEADS, DV), f32),
            shape((late * HEADS, DV), f32),
            shape((ROWS, 5 * HEADS, DV), f32),
        ),
        scratch_shapes=[
            *[buffer(array) for array in arrays[:-2]],
            *[pltpu.SMEM(array.shape, f32) for array in arrays[-2:]],
            buffer(state),
            window,
            window,
            window,
            wide,
            wide,
            pltpu.VMEM((ROWS * (TAPS - 1) * SLIM, DV), f32),
            vectors,
            values,
            found,
            pltpu.SemaphoreType.DMA((len(arrays) - 3,)),
            pltpu.SemaphoreType.DMA((3 * KEYS,)),
            pltpu.SemaphoreType.DMA((ROWS,)),
        ],
        compiler_params=PARAMS,
        name="first_half",
    )(*[in_hbm(array) for array in arrays], in_hbm(state))


def apply_gates(x, norm_gain, w_gate, read):
    rows = x.shape[0]
    return pl.pallas_call(
        gate_kernel,
        in_specs=[HBM] * 3 + [VMEM],
        out_specs=[VMEM] * 2,
        out_shape=(
            shape((rows * HEADS // 2, DV), f32),
            shape((rows // 2, HEADS * DV), bf16),
        ),
        scratch_shapes=[
            buffer(x),
            buffer(norm_gain),
            buffer(w_gate),
            pltpu.VMEM((rows * HEADS, DV), f32),
            pltpu.SemaphoreType.DMA((2,)),
            pltpu.SemaphoreType.DMA((KEYS,)),
        ],
        compiler_params=PARAMS,
        name="apply_gates",
    )(in_hbm(x), in_hbm(norm_gain), in_hbm(w_gate), read)


def fill_slots(wanted, update, tails, state):
    return pl.pallas_call(
        send_kernel,
        in_specs=[SMEM, VMEM, VMEM, HBM],
        out_specs=HBM,
        out_shape=shape((wanted.shape[0], SLOT, DV), bf16),
        scratch_shapes=[
            buffer(state),
            buffer(state),
            pltpu.SemaphoreType.DMA((ROWS,)),
            pltpu.SemaphoreType.DMA((2, wanted.shape[0])),
        ],
        compiler_params=PARAMS,
        name="fill_slots",
    )(wanted, update, tails, in_hbm(state))


def second_half(parents, late, conv, normed, slots, w_out):
    window = pltpu.VMEM(((TAPS - 1) * ROWS * HEADS, DV), f32)
    rows, width = 2 * normed.shape[0], w_out.shape[1] // PARTS
    *sums, update, last, memory = pl.pallas_call(
        second_kernel,
        in_specs=[SMEM] + [VMEM] * 8 + [HBM] * 2,
        out_specs=[VMEM] * (PARTS + 3),
        out_shape=(
            shape((rows, width), f32),
            *[shape((rows, width), bf16)] * (PARTS - 1),
            shape((ROWS, 5 * HEADS, DV), f32),
            shape((ROWS, SLIM, DV), bf16),
            shape((ROWS, BODY, DV), bf16),
        ),
        scratch_shapes=[
            pltpu.VMEM((ROWS, SLOT - BODY, DV), bf16),
            window,
            window,
            window,
            *work_buffers(),
            pltpu.VMEM((PARTS, w_out.shape[0], width), bf16),
            pltpu.VMEM((rows, normed.shape[1]), bf16),
            pltpu.SemaphoreType.DMA((ROWS,)),
            pltpu.SemaphoreType.DMA((ROWS,)),
            pltpu.SemaphoreType.DMA((PARTS,)),
        ],
        compiler_params=PARAMS,
        name="second_half",
    )(parents, *late, conv, normed, in_hbm(slots), in_hbm(w_out))
    return sums, update, last, memory


def last_memory(update, last, raw, memory):
    return pl.pallas_call(
        final_kernel,
        in_specs=[VMEM] * 4,
        out_specs=[HBM] + [VMEM] * 3,
        out_shape=(
            shape((ROWS, BODY, DV), bf16),
            shape((TAPS - 1, ROWS, KEYS * DK), bf16),
            shape((TAPS - 1, ROWS, KEYS * DK), bf16),
            shape((TAPS - 1, ROWS, HEADS * DV), bf16),
        ),
        scratch_shapes=[
            buffer(memory),
            pltpu.VMEM((ROWS * SLIM, DV), f32),
            pltpu.SemaphoreType.DMA((ROWS,)),
        ],
        compiler_params=PARAMS,
        name="last_memory",
    )(update, last, raw, memory)


def sum_heads(blocks):
    total = blocks[0]
    for shift in range(1, PARTS):
        pairs = [(i, (i + shift) % PARTS) for i in range(PARTS)]
        total = total + lax.ppermute(blocks[shift], "tensor", pairs).astype(f32)
    return total.astype(bf16)


def per_device(
    inputs,
    w_query,
    w_key,
    w_value,
    w_gate_z,
    w_beta,
    w_decay,
    conv_query,
    conv_key,
    conv_value,
    decay_log,
    dt_bias,
    norm_gain,
    w_out,
    state,
    tail_query,
    tail_key,
    tail_value,
    parents,
):
    wanted = ask(parents, lax.axis_size("branch"))
    requested = lax.all_to_all(wanted, "branch", split_axis=0, concat_axis=0, tiled=True)

    x = inputs.reshape(-1, inputs.shape[-1])
    flat_state = state.reshape(ROWS, BODY, DV)
    *late, raw, stored_tails, conv, read, update = first_half(
        (
            x,
            tail_query.transpose(1, 0, 2),
            tail_key.transpose(1, 0, 2),
            tail_value.transpose(1, 0, 2),
            conv_query,
            conv_key,
            conv_value,
            w_query,
            w_key,
            w_value,
            w_beta.T,
            w_decay.T,
            decay_log,
            dt_bias,
        ),
        flat_state,
    )
    shipped = fill_slots(requested, update, stored_tails, flat_state)
    arrived = lax.all_to_all(shipped, "branch", split_axis=0, concat_axis=0, tiled=True)
    late_gate, normed = apply_gates(x, norm_gain[None], w_gate_z, read)
    sums, update, last, memory = second_half(
        parents, (*late, late_gate), conv, normed, arrived, w_out
    )
    out_rows = sum_heads(sums).reshape(inputs.shape[0], ROWS, -1)
    final_state, *final_tails = last_memory(update, last, raw, memory)
    return (
        out_rows,
        final_state.reshape(state.shape),
        *[tail.transpose(1, 0, 2) for tail in final_tails],
    )


def solution(mesh):
    return jax.shard_map(
        per_device,
        mesh=mesh,
        in_specs=(
            P(None, "branch", None),
            P(None, "tensor"),
            P(None, "tensor"),
            P(None, "tensor"),
            P(None, "tensor"),
            P(None, "tensor"),
            P(None, "tensor"),
            P(None, "tensor"),
            P(None, "tensor"),
            P(None, "tensor"),
            P("tensor"),
            P("tensor"),
            P(),
            P("tensor", None),
            P("branch", "tensor", None, None),
            P("branch", None, "tensor"),
            P("branch", None, "tensor"),
            P("branch", None, "tensor"),
            P("branch"),
        ),
        out_specs=(
            P(None, "branch", "tensor"),
            P("branch", "tensor", None, None),
            P("branch", None, "tensor"),
            P("branch", None, "tensor"),
            P("branch", None, "tensor"),
        ),
        check_vma=False,
    )
```

```python
import jax
import jax.numpy as jnp
from jax import lax
from jax.experimental import pallas as pl
from jax.experimental.pallas import tpu as pltpu
from jax.sharding import PartitionSpec as P

DK = 128
DV = 128
HEADS = 8
KEYS = 4
ROWS = 16
TAPS = 4
WIDE = 3 * HEADS
SLIM = 2 * KEYS + HEADS
BODY = HEADS * DK
SLOT = BODY + (TAPS - 1) * SLIM
VMEM_BYTES = 48 * 1024 * 1024
CHUNK = 4
PARTS = 4
GROUP = 8
AHEAD = 2
SHIP = 8
f32 = jnp.float32
bf16 = jnp.bfloat16


def split(value):
    high = value.astype(bf16).astype(f32)
    return high, value - high


def dot(left, right):
    return jnp.dot(left, right, preferred_element_type=f32)


def inner(left, right):
    return jnp.sum(left * right, axis=-1, keepdims=True)


def widening():
    row = lax.broadcasted_iota(jnp.int32, ((TAPS - 1) * WIDE, (TAPS - 1) * SLIM), 0)
    column = lax.broadcasted_iota(jnp.int32, ((TAPS - 1) * WIDE, (TAPS - 1) * SLIM), 1)
    tap, place = row // WIDE, row % WIDE
    origin = tap * SLIM + jnp.where(place < 2 * HEADS, place // 2, place - HEADS)
    return jnp.where(origin == column, 1.0, 0.0).astype(bf16)


def spread(target, start, h, block):
    target[pl.ds(start * HEADS + h, block.shape[0], stride=HEADS), :] = block


def part_of(ref, index, first, count):
    return ref[pl.ds(index * ROWS * HEADS + first * HEADS, count * HEADS), :]


def find_vectors(window, conv_ref, vector_buf, value_buf):
    for first in range(0, ROWS, CHUNK):
        there = slice(first, first + CHUNK)
        for step in range(2):
            for kind in range(3):
                mixed = 0.0
                for tap in range(TAPS):
                    rows = window(kind, step + tap, first).reshape(CHUNK, HEADS, DV)
                    mixed = mixed + rows * conv_ref[kind, tap][None]
                mixed = mixed * jax.nn.sigmoid(mixed)
                if kind == 2:
                    value_buf[step, there] = mixed
                    continue
                unit = mixed * lax.rsqrt(inner(mixed, mixed) + 1e-06)
                if kind == 0:
                    unit = unit * DK ** (-0.5)
                place = 2 * step + 1 - kind
                vector_buf[there, place * HEADS : (place + 1) * HEADS, :] = unit


def recall(rows, memory, vector_buf, found_buf):
    head = lax.broadcasted_iota(jnp.int32, (HEADS, DV), 0)
    for row in rows:
        high, low = split(vector_buf[row])
        left = jnp.concatenate([high, low], axis=0).astype(bf16)
        found = [jnp.zeros((HEADS, DV), f32)] * 4
        for h in range(0, HEADS, 2):
            pair = jnp.concatenate([memory(row, h), memory(row, h + 1)], axis=1)
            product = dot(left, pair)
            product = product[: 4 * HEADS] + product[4 * HEADS :]
            for i in range(4):
                block = product[i * HEADS : (i + 1) * HEADS]
                found[i] = jnp.where(head == h, block[:, :DV], found[i])
                found[i] = jnp.where(head == h + 1, block[:, DV:], found[i])
        found_buf[row] = jnp.concatenate(found, axis=0)


def finish(first, strengths, decays, gates, vector_buf, value_buf, found_buf, normed_buf, update_buf):
    there = slice(first, first + CHUNK)

    def piece(ref, i):
        return ref[there, i * HEADS : (i + 1) * HEADS, :]

    def steps(ref):
        return [part_of(ref, step, first, CHUNK).reshape(CHUNK, HEADS, DV) for step in range(2)]

    key0, query0, key1, query1 = [piece(vector_buf, i) for i in range(4)]
    found0, found1, found2, found3 = [piece(found_buf, i) for i in range(4)]
    strength0, strength1 = steps(strengths)
    decay0, decay1 = steps(decays)
    change0 = (value_buf[0, there] - decay0 * found0) * strength0
    read0 = decay0 * found1 + inner(query0, key0) * change0
    kept = decay0 * found2 + inner(key1, key0) * change0
    change1 = (value_buf[1, there] - decay1 * kept) * strength1
    kept = decay0 * found3 + inner(query1, key0) * change0
    read1 = decay1 * kept + inner(query1, key1) * change1
    for step, (read, gate) in enumerate(zip((read0, read1), steps(gates))):
        scale = lax.rsqrt(jnp.mean(read * read, axis=-1, keepdims=True) + 1e-06)
        start = (step * ROWS + first) * HEADS
        normed_buf[start : start + CHUNK * HEADS, :] = (read * scale * gate).reshape(
            CHUNK * HEADS, DV
        )
    for i, value in enumerate((key0, key1, decay1 * change0, change1, decay0 * decay1)):
        update_buf[there, i * HEADS : (i + 1) * HEADS, :] = value


def flatten_heads(normed_buf, normed_ref):
    for h in range(HEADS):
        rows = normed_buf[pl.ds(h, 2 * ROWS, stride=HEADS), :]
        normed_ref[:, h * DV : (h + 1) * DV] = rows.astype(bf16)


def write_row(update, memory, store):
    key0, key1, change0, change1, decay = [
        update[i * HEADS : (i + 1) * HEADS] for i in range(5)
    ]
    (key0h, key0l), (key1h, key1l) = split(key0), split(key1)
    (change0h, change0l), (change1h, change1l) = split(change0), split(change1)
    left = jnp.concatenate([key0h, key0l, key0h, key1h, key1l, key1h], axis=0)
    left = left.T.astype(bf16)
    right = jnp.concatenate([change0h, change0h, change0l, change1h, change1h, change1l], axis=0)
    head = lax.broadcasted_iota(jnp.int32, right.shape, 0) % HEADS
    for h in range(0, HEADS, 2):
        pair = [jnp.where(head == h + i, right, 0.0).astype(bf16) for i in range(2)]
        added = dot(left, jnp.concatenate(pair, axis=1))
        for i in range(2):
            kept = memory(h + i).astype(f32) * decay[h + i : h + i + 1]
            store(h + i, (kept + added[:, i * DV : (i + 1) * DV]).astype(bf16))


def write_rows(rows, update_buf, memory, target_ref):
    for row in rows:

        def store(h, value, row=row):
            target_ref[row, h * DK : (h + 1) * DK, :] = value

        write_row(update_buf[row], lambda h, row=row: memory(row, h), store)


def first_kernel(
    x, gain, tail_query, tail_key, tail_value, conv_query, conv_key, conv_value,
    w_query, w_key, w_value, w_gate, w_beta, w_decay, decay_log, dt_bias,
    late_query_ref, late_key_ref, late_value_ref,
    early_strength_ref, early_forget_ref, early_gate_ref,
    late_strength_ref, late_forget_ref, late_gate_ref,
    raw_ref, stored_ref, conv_ref, vector_ref, value_ref,
    x_buf, gain_buf, tail_query_buf, tail_key_buf, tail_value_buf,
    conv_query_buf, conv_key_buf, conv_value_buf,
    query_buf, key_buf, value_buf, gate_buf, beta_buf, decay_buf, decay_ref, bias_ref,
    window_query, window_key, window_value, strength_all, forget_all, stored_buf,
    small_sem, weight_sem,
):
    rows = x_buf.shape[0]
    small = [
        pltpu.make_async_copy(source, target, small_sem.at[i])
        for i, (source, target) in enumerate(
            (
                (x, x_buf),
                (w_beta, beta_buf),
                (w_decay, decay_buf),
                (gain, gain_buf),
                (tail_query, tail_query_buf),
                (tail_key, tail_key_buf),
                (tail_value, tail_value_buf),
                (conv_query, conv_query_buf),
                (conv_key, conv_key_buf),
                (conv_value, conv_value_buf),
                (decay_log, decay_ref),
                (dt_bias, bias_ref),
            )
        )
    ]
    for copy in small:
        copy.start()

    def weights(j):
        pieces = (
            (w_query, query_buf, DK),
            (w_key, key_buf, DK),
            (w_value, value_buf, 2 * DV),
            (w_gate, gate_buf, 2 * DV),
        )
        copies = []
        for i, (hbm, buf, width) in enumerate(pieces):
            part = pl.ds(j * width, width)
            copies.append(
                pltpu.make_async_copy(hbm.at[:, part], buf.at[:, part], weight_sem.at[4 * j + i])
            )
        return copies

    def begin(j):
        for copy in weights(j):
            copy.start()

    for j in range(AHEAD):
        begin(j)

    for copy in small:
        copy.wait()
    head = lax.broadcasted_iota(jnp.int32, (HEADS, DV), 0)
    rate, bias = jnp.zeros((HEADS, DV), f32), jnp.zeros((HEADS, DV), f32)
    for h in range(HEADS):
        rate = jnp.where(head == h, decay_ref[h], rate)
        bias = jnp.where(head == h, bias_ref[h], bias)
    rate = -jnp.exp(rate)
    x_all = x_buf[...]

    across = (((1,), (1,)), ((), ()))
    beta = lax.dot_general(x_all, beta_buf[...], across, preferred_element_type=f32)
    decay = lax.dot_general(x_all, decay_buf[...], across, preferred_element_type=f32)
    for h in range(HEADS):
        spread(strength_all, 0, h, jnp.broadcast_to(beta[:, h : h + 1], (rows, DV)))
        spread(forget_all, 0, h, jnp.broadcast_to(decay[:, h : h + 1], (rows, DV)))
    for first in range(0, rows, ROWS):
        there = slice(first * HEADS, (first + ROWS) * HEADS)
        strength_all[there] = jax.nn.sigmoid(strength_all[there])
        raised = forget_all[there].reshape(ROWS, HEADS, DV) + bias[None]
        forget = jnp.exp(rate[None] * jax.nn.softplus(raised))
        forget_all[there] = forget.reshape(ROWS * HEADS, DV)

    history = (TAPS - 1) * ROWS

    def place(window, h, before, fresh):
        spread(window, 0, h, before)
        spread(window, history, h, fresh)

    def keep(channel, before, fresh):
        after = jnp.concatenate([before[2 * ROWS :], fresh[: 2 * ROWS]], axis=0)
        for tap in range(TAPS - 1):
            stored_buf[pl.ds(tap * SLIM + channel, ROWS, stride=(TAPS - 1) * SLIM), :] = after[
                tap * ROWS : (tap + 1) * ROWS
            ]

    for kind, buf in enumerate((conv_query_buf, conv_key_buf, conv_value_buf)):
        wide = buf[...].astype(f32)
        for h in range(HEADS):
            channel = h if kind == 2 else h // 2
            taps = wide[:, channel * DV : (channel + 1) * DV]
            for tap in range(TAPS):
                conv_ref[kind, tap, h : h + 1, :] = taps[tap : tap + 1]

    for j in range(KEYS):
        for copy in weights(j):
            copy.wait()
        if j + AHEAD < KEYS:
            begin(j + AHEAD)
        one, two = slice(j * DK, (j + 1) * DK), slice(2 * j * DV, 2 * (j + 1) * DV)
        query = dot(x_all, query_buf[:, one]).astype(bf16)
        key = dot(x_all, key_buf[:, one]).astype(bf16)
        value = dot(x_all, value_buf[:, two]).astype(bf16)
        gate = dot(x_all, gate_buf[:, two])
        gate = gate * jax.nn.sigmoid(gate)
        raw_ref[:, j * DK : (j + 1) * DK] = query[2 * ROWS :]
        raw_ref[:, (KEYS + j) * DK : (KEYS + j + 1) * DK] = key[2 * ROWS :]
        raw_ref[:, 2 * (KEYS + j) * DK : 2 * (KEYS + j + 1) * DK] = value[2 * ROWS :]
        query, key, value = query.astype(f32), key.astype(f32), value.astype(f32)
        old_query = tail_query_buf[:, :, one].reshape(history, DK).astype(f32)
        old_key = tail_key_buf[:, :, one].reshape(history, DK).astype(f32)
        old_value = tail_value_buf[:, :, two].reshape(history, 2 * DV).astype(f32)
        keep(j, old_query, query)
        keep(KEYS + j, old_key, key)
        for i in range(2):
            h, half = 2 * j + i, slice(i * DV, (i + 1) * DV)
            place(window_query, h, old_query, query)
            place(window_key, h, old_key, key)
            place(window_value, h, old_value[:, half], value[:, half])
            keep(2 * KEYS + h, old_value[:, half], value[:, half])
            scaled = gate[:, half] * gain_buf[...]
            spread(early_gate_ref, 0, h, scaled[: 2 * ROWS])
            spread(late_gate_ref, 0, h, scaled[2 * ROWS :])

    late = (history + 2 * ROWS) * HEADS
    late_query_ref[...] = window_query[late:, :].astype(bf16)
    late_key_ref[...] = window_key[late:, :].astype(bf16)
    late_value_ref[...] = window_value[late:, :].astype(bf16)
    half = 2 * ROWS * HEADS
    for value, early_ref, late_ref in (
        (strength_all, early_strength_ref, late_strength_ref),
        (forget_all, early_forget_ref, late_forget_ref),
    ):
        early_ref[...] = value[:half, :]
        late_ref[...] = value[half:, :]
    stored_ref[...] = stored_buf[...].reshape(stored_ref.shape).astype(bf16)
    windows = (window_query, window_key, window_value)
    find_vectors(
        lambda kind, tap, first: part_of(windows[kind], tap, first, CHUNK),
        conv_ref,
        vector_ref,
        value_ref,
    )


def send_kernel(
    parent_ref, vector_ref, value_ref, strength_ref, forget_ref, gate_ref, tails_ref, state,
    slots, normed_ref,
    state_buf, stored_buf, found_buf, normed_buf, update_buf, wanted_buf, wanted_ref,
    look_sem, state_sem, slot_sem,
):
    count = slots.shape[0]

    def load(row):
        return pltpu.make_async_copy(state.at[row], state_buf.at[row], state_sem.at[row])

    for row in range(ROWS):
        load(row).start()
    parent = parent_ref[...]
    mine = parent // ROWS == lax.axis_index("branch")
    wanted = jnp.max(jnp.where(mine, parent % ROWS, -1).astype(f32), axis=-1, keepdims=True)
    wanted_buf[...] = jnp.broadcast_to(wanted.astype(jnp.int32), wanted_buf.shape)
    look = pltpu.make_async_copy(wanted_buf, wanted_ref, look_sem.at[0])
    look.start()
    for row in range(ROWS):
        stored_buf[row, BODY:, :] = tails_ref[row]

    def ship(slot, row):
        return pltpu.make_async_copy(stored_buf.at[row], slots.at[slot], slot_sem.at[slot])

    def memory(row, h):
        return state_buf[row, h * DK : (h + 1) * DK, :]

    for start in range(0, ROWS, SHIP):
        rows = range(start, start + SHIP)
        for row in rows:
            load(row).wait()
        recall(rows, memory, vector_ref, found_buf)
        for first in range(start, start + SHIP, CHUNK):
            finish(
                first, strength_ref, forget_ref, gate_ref,
                vector_ref, value_ref, found_buf, normed_buf, update_buf,
            )
        write_rows(rows, update_buf, memory, stored_buf)

        if start == 0:
            look.wait()

        def begin(slot, carry, start=start):
            row = wanted_ref[slot, 0, 0]

            @pl.when((row >= start) & (row < start + SHIP))
            def _():
                ship(slot, row).start()

            return carry

        lax.fori_loop(0, count, begin, 0, unroll=4)
    flatten_heads(normed_buf, normed_ref)

    def end(slot, carry):
        @pl.when(wanted_ref[slot, 0, 0] >= 0)
        def _():
            ship(slot, 0).wait()

        return carry

    lax.fori_loop(0, count, end, 0, unroll=4)


def second_kernel(
    parent_ref, late_query, late_key, late_value, late_strength, late_forget, late_gate, conv_ref, early_ref, slots, w_out,
    *refs,
):
    sums = refs[:PARTS]
    (
        update_ref, last_ref, memory_buf,
        tail_buf, window_query, window_key, window_value,
        vector_buf, value_buf, found_buf, normed_buf, out_buf, normed_ref,
        tail_sem, memory_sem, out_sem,
    ) = refs[PARTS:]
    def load_tail(row):
        return pltpu.make_async_copy(
            slots.at[parent_ref[row] // ROWS, pl.ds(BODY, SLOT - BODY)], tail_buf.at[row], tail_sem.at[row]
        )

    def load(row):
        return pltpu.make_async_copy(
            slots.at[parent_ref[row] // ROWS, pl.ds(0, BODY)], memory_buf.at[row], memory_sem.at[row]
        )

    for row in range(ROWS):
        load_tail(row).start()
    for row in range(ROWS):
        load(row).start()
    width = out_buf.shape[2]
    place = lax.axis_index("tensor")

    def load_out(shift):
        start = pl.multiple_of((place + shift) % PARTS * width, width)
        return pltpu.make_async_copy(
            w_out.at[:, pl.ds(start, width)], out_buf.at[shift], out_sem.at[shift]
        )

    for shift in range(PARTS):
        load_out(shift).start()
    wide = widening()
    for row in range(ROWS):
        load_tail(row).wait()
    for row in range(ROWS):
        tails = tail_buf[row]
        last_ref[row] = tails[2 * SLIM :]
        spaced = dot(wide, tails)
        for tap in range(TAPS - 1):
            for kind, window in enumerate((window_query, window_key, window_value)):
                start = tap * WIDE + kind * HEADS
                window[(tap * ROWS + row) * HEADS : (tap * ROWS + row + 1) * HEADS, :] = spaced[
                    start : start + HEADS
                ]
    windows = (window_query, window_key, window_value)
    fresh = (late_query, late_key, late_value)

    def window(kind, tap, first):
        if tap < TAPS - 1:
            return part_of(windows[kind], tap, first, CHUNK)
        return part_of(fresh[kind], tap - (TAPS - 1), first, CHUNK).astype(f32)

    find_vectors(window, conv_ref, vector_buf, value_buf)

    def group(index, carry):
        rows = [index * GROUP + i for i in range(GROUP)]
        for row in rows:
            load(row).wait()
        recall(rows, lambda row, h: memory_buf[row, h * DK : (h + 1) * DK, :], vector_buf, found_buf)
        return carry

    lax.fori_loop(0, ROWS // GROUP, group, 0)
    for first in range(0, ROWS, CHUNK):
        finish(
            first, late_strength, late_forget, late_gate,
            vector_buf, value_buf, found_buf, normed_buf, update_ref,
        )
    normed_ref[: 2 * ROWS, :] = early_ref[...]
    flatten_heads(normed_buf, normed_ref.at[2 * ROWS :])
    for shift in range(PARTS):
        load_out(shift).wait()
    normed = normed_ref[...]
    for shift in range(PARTS):
        sums[shift][...] = dot(normed, out_buf[shift]).astype(sums[shift].dtype)


def final_kernel(
    update_ref, last_ref, raw_ref, memory_ref,
    final, query_ref, key_ref, value_ref,
    final_buf, last_buf, final_sem,
):
    def save(row):
        return pltpu.make_async_copy(final_buf.at[row], final.at[row], final_sem.at[row])

    start = 0
    last_buf[...] = last_ref[...].astype(f32).reshape(ROWS * SLIM, DV)
    for ref in (query_ref, key_ref, value_ref):
        width = ref.shape[2]
        for channel in range(width // DV):
            block = last_buf[pl.ds(start // DV + channel, ROWS, stride=SLIM), :]
            ref[0, :, channel * DV : (channel + 1) * DV] = block.astype(bf16)
        for step in range(2):
            ref[1 + step] = raw_ref[step * ROWS : (step + 1) * ROWS, start : start + width]
        start += width

    def group(index, carry):
        rows = [index * GROUP + i for i in range(GROUP)]
        write_rows(
            rows, update_ref, lambda row, h: memory_ref[row, h * DK : (h + 1) * DK, :], final_buf
        )
        for row in rows:
            save(row).start()
        return carry

    lax.fori_loop(0, ROWS // GROUP, group, 0)
    for row in range(ROWS):
        save(row).wait()


VMEM = pl.BlockSpec(memory_space=pltpu.VMEM)
SMEM = pl.BlockSpec(memory_space=pltpu.SMEM)
HBM = pl.BlockSpec(memory_space=pltpu.HBM)
PARAMS = pltpu.CompilerParams(vmem_limit_bytes=VMEM_BYTES)


def in_hbm(array):
    return pltpu.with_memory_space_constraint(array, pltpu.HBM)


def shape(dims, kind):
    return jax.ShapeDtypeStruct(dims, kind)


def buffer(array):
    return pltpu.VMEM(array.shape, array.dtype)


def work_buffers():
    return [
        pltpu.VMEM((ROWS, 4 * HEADS, DV), f32),
        pltpu.VMEM((2, ROWS, HEADS, DV), f32),
        pltpu.VMEM((ROWS, 4 * HEADS, DV), f32),
        pltpu.VMEM((2 * ROWS * HEADS, DV), f32),
    ]


def first_half(arrays):
    rows = arrays[0].shape[0]
    half = rows // 2
    window = pltpu.VMEM(((TAPS - 1) * ROWS * HEADS + rows * HEADS, DV), f32)
    wide = pltpu.VMEM((rows * HEADS, DV), f32)
    return pl.pallas_call(
        first_kernel,
        in_specs=[HBM] * len(arrays),
        out_specs=[VMEM] * 14,
        out_shape=(
            *[shape((half * HEADS, DV), bf16)] * 3,
            *[shape((half * HEADS, DV), f32)] * 6,
            shape((half, SLIM * DV), bf16),
            shape((ROWS, (TAPS - 1) * SLIM, DV), bf16),
            shape((3, TAPS, HEADS, DV), f32),
            shape((ROWS, 4 * HEADS, DV), f32),
            shape((2, ROWS, HEADS, DV), f32),
        ),
        scratch_shapes=[
            *[buffer(array) for array in arrays[:-2]],
            *[pltpu.SMEM(array.shape, f32) for array in arrays[-2:]],
            window,
            window,
            window,
            wide,
            wide,
            pltpu.VMEM((ROWS * (TAPS - 1) * SLIM, DV), f32),
            pltpu.SemaphoreType.DMA((len(arrays) - 4,)),
            pltpu.SemaphoreType.DMA((4 * KEYS,)),
        ],
        compiler_params=PARAMS,
        name="first_half",
    )(*[in_hbm(array) for array in arrays])


def fill_slots(parents, early, tails, state):
    count = parents.shape[0]
    _, _, found, normed = work_buffers()
    return pl.pallas_call(
        send_kernel,
        in_specs=[VMEM] * 7 + [HBM],
        out_specs=[HBM, VMEM],
        out_shape=(
            shape((count, SLOT, DV), bf16),
            shape((2 * ROWS, HEADS * DV), bf16),
        ),
        scratch_shapes=[
            buffer(state),
            pltpu.VMEM((ROWS, SLOT, DV), bf16),
            found,
            normed,
            pltpu.VMEM((ROWS, 5 * HEADS, DV), f32),
            pltpu.VMEM((count, 1, DV), jnp.int32),
            pltpu.SMEM((count, 1, DV), jnp.int32),
            pltpu.SemaphoreType.DMA((1,)),
            pltpu.SemaphoreType.DMA((ROWS,)),
            pltpu.SemaphoreType.DMA((count,)),
        ],
        compiler_params=PARAMS,
        name="fill_slots",
    )(parents, *early, tails, in_hbm(state))


def second_half(parents, late, conv, normed, slots, w_out):
    window = pltpu.VMEM(((TAPS - 1) * ROWS * HEADS, DV), f32)
    rows, width = 2 * normed.shape[0], w_out.shape[1] // PARTS
    *sums, update, last, memory = pl.pallas_call(
        second_kernel,
        in_specs=[SMEM] + [VMEM] * 8 + [HBM] * 2,
        out_specs=[VMEM] * (PARTS + 3),
        out_shape=(
            shape((rows, width), f32),
            *[shape((rows, width), bf16)] * (PARTS - 1),
            shape((ROWS, 5 * HEADS, DV), f32),
            shape((ROWS, SLIM, DV), bf16),
            shape((ROWS, BODY, DV), bf16),
        ),
        scratch_shapes=[
            pltpu.VMEM((ROWS, SLOT - BODY, DV), bf16),
            window,
            window,
            window,
            *work_buffers(),
            pltpu.VMEM((PARTS, w_out.shape[0], width), bf16),
            pltpu.VMEM((rows, normed.shape[1]), bf16),
            pltpu.SemaphoreType.DMA((ROWS,)),
            pltpu.SemaphoreType.DMA((ROWS,)),
            pltpu.SemaphoreType.DMA((PARTS,)),
        ],
        compiler_params=PARAMS,
        name="second_half",
    )(parents, *late, conv, normed, in_hbm(slots), in_hbm(w_out))
    return sums, update, last, memory


def last_memory(update, last, raw, memory):
    return pl.pallas_call(
        final_kernel,
        in_specs=[VMEM] * 4,
        out_specs=[HBM] + [VMEM] * 3,
        out_shape=(
            shape((ROWS, BODY, DV), bf16),
            shape((TAPS - 1, ROWS, KEYS * DK), bf16),
            shape((TAPS - 1, ROWS, KEYS * DK), bf16),
            shape((TAPS - 1, ROWS, HEADS * DV), bf16),
        ),
        scratch_shapes=[
            buffer(memory),
            pltpu.VMEM((ROWS * SLIM, DV), f32),
            pltpu.SemaphoreType.DMA((ROWS,)),
        ],
        compiler_params=PARAMS,
        name="last_memory",
    )(update, last, raw, memory)


def sum_heads(blocks):
    total = blocks[0]
    for shift in (1, 3, 2):
        pairs = [(i, (i + shift) % PARTS) for i in range(PARTS)]
        total = total + lax.ppermute(blocks[shift], "tensor", pairs).astype(f32)
    return total.astype(bf16)


def per_device(
    inputs,
    w_query,
    w_key,
    w_value,
    w_gate_z,
    w_beta,
    w_decay,
    conv_query,
    conv_key,
    conv_value,
    decay_log,
    dt_bias,
    norm_gain,
    w_out,
    state,
    tail_query,
    tail_key,
    tail_value,
    parents,
):
    groups = lax.axis_size("branch")
    asked = jnp.broadcast_to(parents[None, None, :], (groups, 1, ROWS))
    asked = lax.all_to_all(asked, "branch", split_axis=0, concat_axis=0, tiled=True)

    flat_state = state.reshape(ROWS, BODY, DV)
    (
        late_query, late_key, late_value, *scales, raw, stored_tails, conv, vectors, values
    ) = first_half(
        (
            inputs.reshape(-1, inputs.shape[-1]),
            norm_gain[None],
            tail_query.transpose(1, 0, 2),
            tail_key.transpose(1, 0, 2),
            tail_value.transpose(1, 0, 2),
            conv_query,
            conv_key,
            conv_value,
            w_query,
            w_key,
            w_value,
            w_gate_z,
            w_beta.T,
            w_decay.T,
            decay_log,
            dt_bias,
        )
    )
    shipped, normed = fill_slots(asked, (vectors, values, *scales[:3]), stored_tails, flat_state)
    arrived = lax.all_to_all(shipped, "branch", split_axis=0, concat_axis=0, tiled=True)
    late = (late_query, late_key, late_value, *scales[3:])
    sums, update, last, memory = second_half(
        parents, late, conv, normed, arrived, w_out
    )
    out_rows = sum_heads(sums).reshape(inputs.shape[0], ROWS, -1)
    final_state, *final_tails = last_memory(update, last, raw, memory)
    return (
        out_rows,
        final_state.reshape(state.shape),
        *[tail.transpose(1, 0, 2) for tail in final_tails],
    )


def solution(mesh):
    return jax.shard_map(
        per_device,
        mesh=mesh,
        in_specs=(
            P(None, "branch", None),
            P(None, "tensor"),
            P(None, "tensor"),
            P(None, "tensor"),
            P(None, "tensor"),
            P(None, "tensor"),
            P(None, "tensor"),
            P(None, "tensor"),
            P(None, "tensor"),
            P(None, "tensor"),
            P("tensor"),
            P("tensor"),
            P(),
            P("tensor", None),
            P("branch", "tensor", None, None),
            P("branch", None, "tensor"),
            P("branch", None, "tensor"),
            P("branch", None, "tensor"),
            P("branch"),
        ),
        out_specs=(
            P(None, "branch", "tensor"),
            P("branch", "tensor", None, None),
            P("branch", None, "tensor"),
            P("branch", None, "tensor"),
            P("branch", None, "tensor"),
        ),
        check_vma=False,
    )
```

```python
import jax
import jax.numpy as jnp
from jax import lax
from jax.experimental import pallas as pl
from jax.experimental.pallas import tpu as pltpu
from jax.sharding import PartitionSpec as P

DK = 128
DV = 128
HEADS = 8
KEYS = 4
ROWS = 16
TAPS = 4
WIDE = 3 * HEADS
SLIM = 2 * KEYS + HEADS
BODY = HEADS * DK
SLOT = BODY + (TAPS - 1) * SLIM
VMEM_BYTES = 48 * 1024 * 1024
CHUNK = 4
PARTS = 4
GROUP = 8
LATE = 16
AHEAD = 2
SHIP = 8
f32 = jnp.float32
bf16 = jnp.bfloat16


def split(value):
    high = value.astype(bf16).astype(f32)
    return high, value - high


def dot(left, right):
    return jnp.dot(left, right, preferred_element_type=f32)


def inner(left, right):
    return jnp.sum(left * right, axis=-1, keepdims=True)


def widening():
    row = lax.broadcasted_iota(jnp.int32, ((TAPS - 1) * WIDE, (TAPS - 1) * SLIM), 0)
    column = lax.broadcasted_iota(jnp.int32, ((TAPS - 1) * WIDE, (TAPS - 1) * SLIM), 1)
    tap, place = row // WIDE, row % WIDE
    origin = tap * SLIM + jnp.where(place < 2 * HEADS, place // 2, place - HEADS)
    return jnp.where(origin == column, 1.0, 0.0).astype(bf16)


def spread(target, start, h, block):
    target[pl.ds(start * HEADS + h, block.shape[0], stride=HEADS), :] = block


def part_of(ref, index, first, count):
    return ref[pl.ds(index * ROWS * HEADS + first * HEADS, count * HEADS), :]


def find_vectors(window, conv_ref, vector_buf, value_buf):
    for first in range(0, ROWS, CHUNK):
        there = slice(first, first + CHUNK)
        for step in range(2):
            for kind in range(3):
                mixed = 0.0
                for tap in range(TAPS):
                    rows = window(kind, step + tap, first).reshape(CHUNK, HEADS, DV)
                    mixed = mixed + rows * conv_ref[kind, tap][None]
                mixed = mixed * jax.nn.sigmoid(mixed)
                if kind == 2:
                    value_buf[step, there] = mixed
                    continue
                unit = mixed * lax.rsqrt(inner(mixed, mixed) + 1e-06)
                if kind == 0:
                    unit = unit * DK ** (-0.5)
                place = 2 * step + 1 - kind
                vector_buf[there, place * HEADS : (place + 1) * HEADS, :] = unit


def recall(rows, memory, vector_buf, found_buf):
    head = lax.broadcasted_iota(jnp.int32, (HEADS, DV), 0)
    for row in rows:
        high, low = split(vector_buf[row])
        left = jnp.concatenate([high, low], axis=0).astype(bf16)
        found = [jnp.zeros((HEADS, DV), f32)] * 4
        for h in range(0, HEADS, 2):
            pair = jnp.concatenate([memory(row, h), memory(row, h + 1)], axis=1)
            product = dot(left, pair)
            product = product[: 4 * HEADS] + product[4 * HEADS :]
            for i in range(4):
                block = product[i * HEADS : (i + 1) * HEADS]
                found[i] = jnp.where(head == h, block[:, :DV], found[i])
                found[i] = jnp.where(head == h + 1, block[:, DV:], found[i])
        found_buf[row] = jnp.concatenate(found, axis=0)


def finish(first, strengths, decays, gates, vector_buf, value_buf, found_buf, normed_buf, update_buf):
    there = slice(first, first + CHUNK)

    def piece(ref, i):
        return ref[there, i * HEADS : (i + 1) * HEADS, :]

    def steps(ref):
        return [part_of(ref, step, first, CHUNK).reshape(CHUNK, HEADS, DV) for step in range(2)]

    key0, query0, key1, query1 = [piece(vector_buf, i) for i in range(4)]
    found0, found1, found2, found3 = [piece(found_buf, i) for i in range(4)]
    strength0, strength1 = steps(strengths)
    decay0, decay1 = steps(decays)
    change0 = (value_buf[0, there] - decay0 * found0) * strength0
    read0 = decay0 * found1 + inner(query0, key0) * change0
    kept = decay0 * found2 + inner(key1, key0) * change0
    change1 = (value_buf[1, there] - decay1 * kept) * strength1
    kept = decay0 * found3 + inner(query1, key0) * change0
    read1 = decay1 * kept + inner(query1, key1) * change1
    for step, (read, gate) in enumerate(zip((read0, read1), steps(gates))):
        scale = lax.rsqrt(jnp.mean(read * read, axis=-1, keepdims=True) + 1e-06)
        start = (step * ROWS + first) * HEADS
        normed_buf[start : start + CHUNK * HEADS, :] = (read * scale * gate).reshape(
            CHUNK * HEADS, DV
        )
    for i, value in enumerate((key0, key1, decay1 * change0, change1, decay0 * decay1)):
        update_buf[there, i * HEADS : (i + 1) * HEADS, :] = value


def flatten_heads(normed_buf, normed_ref):
    for h in range(HEADS):
        rows = normed_buf[pl.ds(h, 2 * ROWS, stride=HEADS), :]
        normed_ref[:, h * DV : (h + 1) * DV] = rows.astype(bf16)


def write_row(update, memory, store):
    key0, key1, change0, change1, decay = [
        update[i * HEADS : (i + 1) * HEADS] for i in range(5)
    ]
    (key0h, key0l), (key1h, key1l) = split(key0), split(key1)
    (change0h, change0l), (change1h, change1l) = split(change0), split(change1)
    left = jnp.concatenate([key0h, key0l, key0h, key1h, key1l, key1h], axis=0)
    left = left.T.astype(bf16)
    right = jnp.concatenate([change0h, change0h, change0l, change1h, change1h, change1l], axis=0)
    head = lax.broadcasted_iota(jnp.int32, right.shape, 0) % HEADS
    for h in range(0, HEADS, 2):
        pair = [jnp.where(head == h + i, right, 0.0).astype(bf16) for i in range(2)]
        added = dot(left, jnp.concatenate(pair, axis=1))
        for i in range(2):
            kept = memory(h + i).astype(f32) * decay[h + i : h + i + 1]
            store(h + i, (kept + added[:, i * DV : (i + 1) * DV]).astype(bf16))


def write_rows(rows, update_buf, memory, target_ref):
    for row in rows:

        def store(h, value, row=row):
            target_ref[row, h * DK : (h + 1) * DK, :] = value

        write_row(update_buf[row], lambda h, row=row: memory(row, h), store)


def first_kernel(
    x, gain, tail_query, tail_key, tail_value, conv_query, conv_key, conv_value,
    w_query, w_key, w_value, w_gate, w_beta, w_decay, decay_log, dt_bias,
    late_query_ref, late_key_ref, late_value_ref,
    early_strength_ref, early_forget_ref, early_gate_ref,
    late_strength_ref, late_forget_ref, late_gate_ref,
    raw_ref, stored_ref, conv_ref, vector_ref, value_ref,
    x_buf, gain_buf, tail_query_buf, tail_key_buf, tail_value_buf,
    conv_query_buf, conv_key_buf, conv_value_buf,
    query_buf, key_buf, value_buf, gate_buf, beta_buf, decay_buf, decay_ref, bias_ref,
    window_query, window_key, window_value, strength_all, forget_all, stored_buf,
    small_sem, weight_sem,
):
    rows = x_buf.shape[0]
    small = [
        pltpu.make_async_copy(source, target, small_sem.at[i])
        for i, (source, target) in enumerate(
            (
                (x, x_buf),
                (w_beta, beta_buf),
                (w_decay, decay_buf),
                (gain, gain_buf),
                (tail_query, tail_query_buf),
                (tail_key, tail_key_buf),
                (tail_value, tail_value_buf),
                (conv_query, conv_query_buf),
                (conv_key, conv_key_buf),
                (conv_value, conv_value_buf),
                (decay_log, decay_ref),
                (dt_bias, bias_ref),
            )
        )
    ]
    for copy in small:
        copy.start()

    def weights(j):
        pieces = (
            (w_query, query_buf, DK),
            (w_key, key_buf, DK),
            (w_value, value_buf, 2 * DV),
            (w_gate, gate_buf, 2 * DV),
        )
        copies = []
        for i, (hbm, buf, width) in enumerate(pieces):
            part = pl.ds(j * width, width)
            copies.append(
                pltpu.make_async_copy(hbm.at[:, part], buf.at[:, part], weight_sem.at[4 * j + i])
            )
        return copies

    def begin(j):
        for copy in weights(j):
            copy.start()

    for j in range(AHEAD):
        begin(j)

    for copy in small:
        copy.wait()
    head = lax.broadcasted_iota(jnp.int32, (HEADS, DV), 0)
    rate, bias = jnp.zeros((HEADS, DV), f32), jnp.zeros((HEADS, DV), f32)
    for h in range(HEADS):
        rate = jnp.where(head == h, decay_ref[h], rate)
        bias = jnp.where(head == h, bias_ref[h], bias)
    rate = -jnp.exp(rate)
    x_all = x_buf[...]

    across = (((1,), (1,)), ((), ()))
    beta = lax.dot_general(x_all, beta_buf[...], across, preferred_element_type=f32)
    decay = lax.dot_general(x_all, decay_buf[...], across, preferred_element_type=f32)
    for h in range(HEADS):
        spread(strength_all, 0, h, jnp.broadcast_to(beta[:, h : h + 1], (rows, DV)))
        spread(forget_all, 0, h, jnp.broadcast_to(decay[:, h : h + 1], (rows, DV)))
    for first in range(0, rows, ROWS):
        there = slice(first * HEADS, (first + ROWS) * HEADS)
        strength_all[there] = jax.nn.sigmoid(strength_all[there])
        raised = forget_all[there].reshape(ROWS, HEADS, DV) + bias[None]
        forget = jnp.exp(rate[None] * jax.nn.softplus(raised))
        forget_all[there] = forget.reshape(ROWS * HEADS, DV)

    history = (TAPS - 1) * ROWS

    def place(window, h, before, fresh):
        spread(window, 0, h, before)
        spread(window, history, h, fresh)

    def keep(channel, before, fresh):
        after = jnp.concatenate([before[2 * ROWS :], fresh[: 2 * ROWS]], axis=0)
        for tap in range(TAPS - 1):
            stored_buf[pl.ds(tap * SLIM + channel, ROWS, stride=(TAPS - 1) * SLIM), :] = after[
                tap * ROWS : (tap + 1) * ROWS
            ]

    for kind, buf in enumerate((conv_query_buf, conv_key_buf, conv_value_buf)):
        wide = buf[...].astype(f32)
        for h in range(HEADS):
            channel = h if kind == 2 else h // 2
            taps = wide[:, channel * DV : (channel + 1) * DV]
            for tap in range(TAPS):
                conv_ref[kind, tap, h : h + 1, :] = taps[tap : tap + 1]

    for j in range(KEYS):
        for copy in weights(j):
            copy.wait()
        if j + AHEAD < KEYS:
            begin(j + AHEAD)
        one, two = slice(j * DK, (j + 1) * DK), slice(2 * j * DV, 2 * (j + 1) * DV)
        query = dot(x_all, query_buf[:, one]).astype(bf16)
        key = dot(x_all, key_buf[:, one]).astype(bf16)
        value = dot(x_all, value_buf[:, two]).astype(bf16)
        gate = dot(x_all, gate_buf[:, two])
        gate = gate * jax.nn.sigmoid(gate)
        raw_ref[:, j * DK : (j + 1) * DK] = query[2 * ROWS :]
        raw_ref[:, (KEYS + j) * DK : (KEYS + j + 1) * DK] = key[2 * ROWS :]
        raw_ref[:, 2 * (KEYS + j) * DK : 2 * (KEYS + j + 1) * DK] = value[2 * ROWS :]
        query, key, value = query.astype(f32), key.astype(f32), value.astype(f32)
        old_query = tail_query_buf[:, :, one].reshape(history, DK).astype(f32)
        old_key = tail_key_buf[:, :, one].reshape(history, DK).astype(f32)
        old_value = tail_value_buf[:, :, two].reshape(history, 2 * DV).astype(f32)
        keep(j, old_query, query)
        keep(KEYS + j, old_key, key)
        for i in range(2):
            h, half = 2 * j + i, slice(i * DV, (i + 1) * DV)
            place(window_query, h, old_query, query)
            place(window_key, h, old_key, key)
            place(window_value, h, old_value[:, half], value[:, half])
            keep(2 * KEYS + h, old_value[:, half], value[:, half])
            scaled = gate[:, half] * gain_buf[...]
            spread(early_gate_ref, 0, h, scaled[: 2 * ROWS])
            spread(late_gate_ref, 0, h, scaled[2 * ROWS :])

    late = (history + 2 * ROWS) * HEADS
    late_query_ref[...] = window_query[late:, :].astype(bf16)
    late_key_ref[...] = window_key[late:, :].astype(bf16)
    late_value_ref[...] = window_value[late:, :].astype(bf16)
    half = 2 * ROWS * HEADS
    for value, early_ref, late_ref in (
        (strength_all, early_strength_ref, late_strength_ref),
        (forget_all, early_forget_ref, late_forget_ref),
    ):
        early_ref[...] = value[:half, :]
        late_ref[...] = value[half:, :]
    stored_ref[...] = stored_buf[...].reshape(stored_ref.shape).astype(bf16)
    windows = (window_query, window_key, window_value)
    find_vectors(
        lambda kind, tap, first: part_of(windows[kind], tap, first, CHUNK),
        conv_ref,
        vector_ref,
        value_ref,
    )


def send_kernel(
    parent_ref, vector_ref, value_ref, strength_ref, forget_ref, gate_ref, tails_ref, state,
    slots, normed_ref,
    state_buf, stored_buf, found_buf, normed_buf, update_buf, wanted_buf, wanted_ref,
    look_sem, state_sem, slot_sem,
):
    count = slots.shape[0]

    def load(row):
        return pltpu.make_async_copy(state.at[row], state_buf.at[row], state_sem.at[row])

    for row in range(ROWS):
        load(row).start()
    parent = parent_ref[...]
    mine = parent // ROWS == lax.axis_index("branch")
    wanted = jnp.max(jnp.where(mine, parent % ROWS, -1).astype(f32), axis=-1, keepdims=True)
    wanted_buf[...] = jnp.broadcast_to(wanted.astype(jnp.int32), wanted_buf.shape)
    look = pltpu.make_async_copy(wanted_buf, wanted_ref, look_sem.at[0])
    look.start()
    for row in range(ROWS):
        stored_buf[row, BODY:, :] = tails_ref[row]

    def ship(slot, row):
        return pltpu.make_async_copy(stored_buf.at[row], slots.at[slot], slot_sem.at[slot])

    def memory(row, h):
        return state_buf[row, h * DK : (h + 1) * DK, :]

    for start in range(0, ROWS, SHIP):
        rows = range(start, start + SHIP)
        for row in rows:
            load(row).wait()
        recall(rows, memory, vector_ref, found_buf)
        for first in range(start, start + SHIP, CHUNK):
            finish(
                first, strength_ref, forget_ref, gate_ref,
                vector_ref, value_ref, found_buf, normed_buf, update_buf,
            )
        write_rows(rows, update_buf, memory, stored_buf)

        if start == 0:
            look.wait()

        def begin(slot, carry, start=start):
            row = wanted_ref[slot, 0, 0]

            @pl.when((row >= start) & (row < start + SHIP))
            def _():
                ship(slot, row).start()

            return carry

        lax.fori_loop(0, count, begin, 0, unroll=4)
    flatten_heads(normed_buf, normed_ref)

    def end(slot, carry):
        @pl.when(wanted_ref[slot, 0, 0] >= 0)
        def _():
            ship(slot, 0).wait()

        return carry

    lax.fori_loop(0, count, end, 0, unroll=4)


def second_kernel(
    parent_ref, late_query, late_key, late_value, late_strength, late_forget, late_gate, conv_ref, early_ref, slots, w_out,
    *refs,
):
    sums = refs[:PARTS]
    (
        update_ref, last_ref, memory_buf,
        tail_buf, window_query, window_key, window_value,
        vector_buf, value_buf, found_buf, normed_buf, out_buf, normed_ref,
        tail_sem, memory_sem, out_sem,
    ) = refs[PARTS:]
    def load_tail(row):
        return pltpu.make_async_copy(
            slots.at[parent_ref[row] // ROWS, pl.ds(BODY, SLOT - BODY)], tail_buf.at[row], tail_sem.at[row]
        )

    def load(row):
        return pltpu.make_async_copy(
            slots.at[parent_ref[row] // ROWS, pl.ds(0, BODY)], memory_buf.at[row], memory_sem.at[row]
        )

    for row in range(ROWS):
        load_tail(row).start()
    for row in range(ROWS):
        load(row).start()
    width = out_buf.shape[2]
    place = lax.axis_index("tensor")

    def load_out(shift):
        start = pl.multiple_of((place + shift) % PARTS * width, width)
        return pltpu.make_async_copy(
            w_out.at[:, pl.ds(start, width)], out_buf.at[shift], out_sem.at[shift]
        )

    for shift in range(PARTS):
        load_out(shift).start()
    wide = widening()
    for row in range(ROWS):
        load_tail(row).wait()
    for row in range(ROWS):
        tails = tail_buf[row]
        last_ref[row] = tails[2 * SLIM :]
        spaced = dot(wide, tails)
        for tap in range(TAPS - 1):
            for kind, window in enumerate((window_query, window_key, window_value)):
                start = tap * WIDE + kind * HEADS
                window[(tap * ROWS + row) * HEADS : (tap * ROWS + row + 1) * HEADS, :] = spaced[
                    start : start + HEADS
                ]
    windows = (window_query, window_key, window_value)
    fresh = (late_query, late_key, late_value)

    def window(kind, tap, first):
        if tap < TAPS - 1:
            return part_of(windows[kind], tap, first, CHUNK)
        return part_of(fresh[kind], tap - (TAPS - 1), first, CHUNK).astype(f32)

    find_vectors(window, conv_ref, vector_buf, value_buf)

    def group(index, carry):
        rows = [index * LATE + i for i in range(LATE)]
        for row in rows:
            load(row).wait()
        recall(rows, lambda row, h: memory_buf[row, h * DK : (h + 1) * DK, :], vector_buf, found_buf)
        return carry

    lax.fori_loop(0, ROWS // LATE, group, 0)
    for first in range(0, ROWS, CHUNK):
        finish(
            first, late_strength, late_forget, late_gate,
            vector_buf, value_buf, found_buf, normed_buf, update_ref,
        )
    normed_ref[: 2 * ROWS, :] = early_ref[...]
    flatten_heads(normed_buf, normed_ref.at[2 * ROWS :])
    for shift in range(PARTS):
        load_out(shift).wait()
    normed = normed_ref[...]
    for shift in range(PARTS):
        sums[shift][...] = dot(normed, out_buf[shift]).astype(sums[shift].dtype)


def final_kernel(
    update_ref, last_ref, raw_ref, memory_ref,
    final, query, key, value,
    final_buf, last_buf, query_buf, key_buf, value_buf, final_sem, tail_sem,
):
    def save(row):
        return pltpu.make_async_copy(final_buf.at[row], final.at[row], final_sem.at[row])

    start = 0
    last_buf[...] = last_ref[...].astype(f32).reshape(ROWS * SLIM, DV)
    tails = []
    for i, (ref, target) in enumerate(((query_buf, query), (key_buf, key), (value_buf, value))):
        width = ref.shape[2]
        for channel in range(width // DV):
            block = last_buf[pl.ds(start // DV + channel, ROWS, stride=SLIM), :]
            ref[0, :, channel * DV : (channel + 1) * DV] = block.astype(bf16)
        for step in range(2):
            ref[1 + step] = raw_ref[step * ROWS : (step + 1) * ROWS, start : start + width]
        start += width
        tails.append(pltpu.make_async_copy(ref, target, tail_sem.at[i]))
        tails[i].start()

    def group(index, carry):
        rows = [index * GROUP + i for i in range(GROUP)]
        write_rows(
            rows, update_ref, lambda row, h: memory_ref[row, h * DK : (h + 1) * DK, :], final_buf
        )
        for row in rows:
            save(row).start()
        return carry

    lax.fori_loop(0, ROWS // GROUP, group, 0)
    for copy in tails:
        copy.wait()
    for row in range(ROWS):
        save(row).wait()


VMEM = pl.BlockSpec(memory_space=pltpu.VMEM)
SMEM = pl.BlockSpec(memory_space=pltpu.SMEM)
HBM = pl.BlockSpec(memory_space=pltpu.HBM)
PARAMS = pltpu.CompilerParams(vmem_limit_bytes=VMEM_BYTES)


def in_hbm(array):
    return pltpu.with_memory_space_constraint(array, pltpu.HBM)


def shape(dims, kind):
    return jax.ShapeDtypeStruct(dims, kind)


def buffer(array):
    return pltpu.VMEM(array.shape, array.dtype)


def work_buffers():
    return [
        pltpu.VMEM((ROWS, 4 * HEADS, DV), f32),
        pltpu.VMEM((2, ROWS, HEADS, DV), f32),
        pltpu.VMEM((ROWS, 4 * HEADS, DV), f32),
        pltpu.VMEM((2 * ROWS * HEADS, DV), f32),
    ]


def first_half(arrays):
    rows = arrays[0].shape[0]
    half = rows // 2
    window = pltpu.VMEM(((TAPS - 1) * ROWS * HEADS + rows * HEADS, DV), f32)
    wide = pltpu.VMEM((rows * HEADS, DV), f32)
    return pl.pallas_call(
        first_kernel,
        in_specs=[HBM] * len(arrays),
        out_specs=[VMEM] * 14,
        out_shape=(
            *[shape((half * HEADS, DV), bf16)] * 3,
            *[shape((half * HEADS, DV), f32)] * 6,
            shape((half, SLIM * DV), bf16),
            shape((ROWS, (TAPS - 1) * SLIM, DV), bf16),
            shape((3, TAPS, HEADS, DV), f32),
            shape((ROWS, 4 * HEADS, DV), f32),
            shape((2, ROWS, HEADS, DV), f32),
        ),
        scratch_shapes=[
            *[buffer(array) for array in arrays[:-2]],
            *[pltpu.SMEM(array.shape, f32) for array in arrays[-2:]],
            window,
            window,
            window,
            wide,
            wide,
            pltpu.VMEM((ROWS * (TAPS - 1) * SLIM, DV), f32),
            pltpu.SemaphoreType.DMA((len(arrays) - 4,)),
            pltpu.SemaphoreType.DMA((4 * KEYS,)),
        ],
        compiler_params=PARAMS,
        name="first_half",
    )(*[in_hbm(array) for array in arrays])


def fill_slots(parents, early, tails, state):
    count = parents.shape[0]
    _, _, found, normed = work_buffers()
    return pl.pallas_call(
        send_kernel,
        in_specs=[VMEM] * 7 + [HBM],
        out_specs=[HBM, VMEM],
        out_shape=(
            shape((count, SLOT, DV), bf16),
            shape((2 * ROWS, HEADS * DV), bf16),
        ),
        scratch_shapes=[
            buffer(state),
            pltpu.VMEM((ROWS, SLOT, DV), bf16),
            found,
            normed,
            pltpu.VMEM((ROWS, 5 * HEADS, DV), f32),
            pltpu.VMEM((count, 1, DV), jnp.int32),
            pltpu.SMEM((count, 1, DV), jnp.int32),
            pltpu.SemaphoreType.DMA((1,)),
            pltpu.SemaphoreType.DMA((ROWS,)),
            pltpu.SemaphoreType.DMA((count,)),
        ],
        compiler_params=PARAMS,
        name="fill_slots",
    )(parents, *early, tails, in_hbm(state))


def second_half(parents, late, conv, normed, slots, w_out):
    window = pltpu.VMEM(((TAPS - 1) * ROWS * HEADS, DV), f32)
    rows, width = 2 * normed.shape[0], w_out.shape[1] // PARTS
    *sums, update, last, memory = pl.pallas_call(
        second_kernel,
        in_specs=[SMEM] + [VMEM] * 8 + [HBM] * 2,
        out_specs=[VMEM] * (PARTS + 3),
        out_shape=(
            shape((rows, width), f32),
            *[shape((rows, width), bf16)] * (PARTS - 1),
            shape((ROWS, 5 * HEADS, DV), f32),
            shape((ROWS, SLIM, DV), bf16),
            shape((ROWS, BODY, DV), bf16),
        ),
        scratch_shapes=[
            pltpu.VMEM((ROWS, SLOT - BODY, DV), bf16),
            window,
            window,
            window,
            *work_buffers(),
            pltpu.VMEM((PARTS, w_out.shape[0], width), bf16),
            pltpu.VMEM((rows, normed.shape[1]), bf16),
            pltpu.SemaphoreType.DMA((ROWS,)),
            pltpu.SemaphoreType.DMA((ROWS,)),
            pltpu.SemaphoreType.DMA((PARTS,)),
        ],
        compiler_params=PARAMS,
        name="second_half",
    )(parents, *late, conv, normed, in_hbm(slots), in_hbm(w_out))
    return sums, update, last, memory


def last_memory(update, last, raw, memory):
    tails = [shape((TAPS - 1, ROWS, width), bf16) for width in (KEYS * DK, KEYS * DK, HEADS * DV)]
    return pl.pallas_call(
        final_kernel,
        in_specs=[VMEM] * 4,
        out_specs=[HBM] * 4,
        out_shape=(shape((ROWS, BODY, DV), bf16), *tails),
        scratch_shapes=[
            buffer(memory),
            pltpu.VMEM((ROWS * SLIM, DV), f32),
            *[buffer(tail) for tail in tails],
            pltpu.SemaphoreType.DMA((ROWS,)),
            pltpu.SemaphoreType.DMA((3,)),
        ],
        compiler_params=PARAMS,
        name="last_memory",
    )(update, last, raw, memory)


def sum_heads(blocks):
    total = blocks[0]
    for shift in (1, 3, 2):
        pairs = [(i, (i + shift) % PARTS) for i in range(PARTS)]
        total = total + lax.ppermute(blocks[shift], "tensor", pairs).astype(f32)
    return total.astype(bf16)


def per_device(
    inputs,
    w_query,
    w_key,
    w_value,
    w_gate_z,
    w_beta,
    w_decay,
    conv_query,
    conv_key,
    conv_value,
    decay_log,
    dt_bias,
    norm_gain,
    w_out,
    state,
    tail_query,
    tail_key,
    tail_value,
    parents,
):
    groups = lax.axis_size("branch")
    asked = jnp.broadcast_to(parents[None, None, :], (groups, 1, ROWS))
    asked = lax.all_to_all(asked, "branch", split_axis=0, concat_axis=0, tiled=True)

    flat_state = state.reshape(ROWS, BODY, DV)
    (
        late_query, late_key, late_value, *scales, raw, stored_tails, conv, vectors, values
    ) = first_half(
        (
            inputs.reshape(-1, inputs.shape[-1]),
            norm_gain[None],
            tail_query.transpose(1, 0, 2),
            tail_key.transpose(1, 0, 2),
            tail_value.transpose(1, 0, 2),
            conv_query,
            conv_key,
            conv_value,
            w_query,
            w_key,
            w_value,
            w_gate_z,
            w_beta.T,
            w_decay.T,
            decay_log,
            dt_bias,
        )
    )
    shipped, normed = fill_slots(asked, (vectors, values, *scales[:3]), stored_tails, flat_state)
    arrived = lax.all_to_all(shipped, "branch", split_axis=0, concat_axis=0, tiled=True)
    late = (late_query, late_key, late_value, *scales[3:])
    sums, update, last, memory = second_half(
        parents, late, conv, normed, arrived, w_out
    )
    out_rows = sum_heads(sums).reshape(inputs.shape[0], ROWS, -1)
    final_state, *final_tails = last_memory(update, last, raw, memory)
    return (
        out_rows,
        final_state.reshape(state.shape),
        *[tail.transpose(1, 0, 2) for tail in final_tails],
    )


def solution(mesh):
    return jax.shard_map(
        per_device,
        mesh=mesh,
        in_specs=(
            P(None, "branch", None),
            P(None, "tensor"),
            P(None, "tensor"),
            P(None, "tensor"),
            P(None, "tensor"),
            P(None, "tensor"),
            P(None, "tensor"),
            P(None, "tensor"),
            P(None, "tensor"),
            P(None, "tensor"),
            P("tensor"),
            P("tensor"),
            P(),
            P("tensor", None),
            P("branch", "tensor", None, None),
            P("branch", None, "tensor"),
            P("branch", None, "tensor"),
            P("branch", None, "tensor"),
            P("branch"),
        ),
        out_specs=(
            P(None, "branch", "tensor"),
            P("branch", "tensor", None, None),
            P("branch", None, "tensor"),
            P("branch", None, "tensor"),
            P("branch", None, "tensor"),
        ),
        check_vma=False,
    )
```

```python
import jax
import jax.numpy as jnp
from jax import lax
from jax.experimental import pallas as pl
from jax.experimental.pallas import tpu as pltpu
from jax.sharding import PartitionSpec as P

DK = 128
DV = 128
HEADS = 8
KEYS = 4
ROWS = 16
TAPS = 4
WIDE = 3 * HEADS
SLIM = 2 * KEYS + HEADS
BODY = HEADS * DK
SLOT = BODY + (TAPS - 1) * SLIM
VMEM_BYTES = 48 * 1024 * 1024
CHUNK = 4
PARTS = 4
GROUP = 8
LATE = 16
AHEAD = 2
SHIP = 8
f32 = jnp.float32
bf16 = jnp.bfloat16


def split(value):
    high = value.astype(bf16).astype(f32)
    return high, value - high


def dot(left, right):
    return jnp.dot(left, right, preferred_element_type=f32)


def inner(left, right):
    return jnp.sum(left * right, axis=-1, keepdims=True)


def widening():
    row = lax.broadcasted_iota(jnp.int32, ((TAPS - 1) * WIDE, (TAPS - 1) * SLIM), 0)
    column = lax.broadcasted_iota(jnp.int32, ((TAPS - 1) * WIDE, (TAPS - 1) * SLIM), 1)
    tap, place = row // WIDE, row % WIDE
    origin = tap * SLIM + jnp.where(place < 2 * HEADS, place // 2, place - HEADS)
    return jnp.where(origin == column, 1.0, 0.0).astype(bf16)


def spread(target, start, h, block):
    target[pl.ds(start * HEADS + h, block.shape[0], stride=HEADS), :] = block


def part_of(ref, index, first, count):
    return ref[pl.ds(index * ROWS * HEADS + first * HEADS, count * HEADS), :]


def find_vectors(window, conv_ref, vector_buf, value_buf):
    for first in range(0, ROWS, CHUNK):
        there = slice(first, first + CHUNK)
        for step in range(2):
            for kind in range(3):
                mixed = 0.0
                for tap in range(TAPS):
                    rows = window(kind, step + tap, first).reshape(CHUNK, HEADS, DV)
                    mixed = mixed + rows * conv_ref[kind, tap][None]
                mixed = mixed * jax.nn.sigmoid(mixed)
                if kind == 2:
                    value_buf[step, there] = mixed
                    continue
                unit = mixed * lax.rsqrt(inner(mixed, mixed) + 1e-06)
                if kind == 0:
                    unit = unit * DK ** (-0.5)
                place = 2 * step + 1 - kind
                vector_buf[there, place * HEADS : (place + 1) * HEADS, :] = unit


def recall(rows, memory, vector_buf, found_buf):
    head = lax.broadcasted_iota(jnp.int32, (HEADS, DV), 0)
    for row in rows:
        high, low = split(vector_buf[row])
        left = jnp.concatenate([high, low], axis=0).astype(bf16)
        found = [jnp.zeros((HEADS, DV), f32)] * 4
        for h in range(0, HEADS, 2):
            pair = jnp.concatenate([memory(row, h), memory(row, h + 1)], axis=1)
            product = dot(left, pair)
            product = product[: 4 * HEADS] + product[4 * HEADS :]
            for i in range(4):
                block = product[i * HEADS : (i + 1) * HEADS]
                found[i] = jnp.where(head == h, block[:, :DV], found[i])
                found[i] = jnp.where(head == h + 1, block[:, DV:], found[i])
        found_buf[row] = jnp.concatenate(found, axis=0)


def finish(first, strengths, decays, vector_buf, value_buf, found_buf, normed_buf, update_buf):
    there = slice(first, first + CHUNK)

    def piece(ref, i):
        return ref[there, i * HEADS : (i + 1) * HEADS, :]

    def steps(ref):
        return [part_of(ref, step, first, CHUNK).reshape(CHUNK, HEADS, DV) for step in range(2)]

    key0, query0, key1, query1 = [piece(vector_buf, i) for i in range(4)]
    found0, found1, found2, found3 = [piece(found_buf, i) for i in range(4)]
    strength0, strength1 = steps(strengths)
    decay0, decay1 = steps(decays)
    change0 = (value_buf[0, there] - decay0 * found0) * strength0
    read0 = decay0 * found1 + inner(query0, key0) * change0
    kept = decay0 * found2 + inner(key1, key0) * change0
    change1 = (value_buf[1, there] - decay1 * kept) * strength1
    kept = decay0 * found3 + inner(query1, key0) * change0
    read1 = decay1 * kept + inner(query1, key1) * change1
    for step, read in enumerate((read0, read1)):
        scale = lax.rsqrt(jnp.mean(read * read, axis=-1, keepdims=True) + 1e-06)
        start = (step * ROWS + first) * HEADS
        normed_buf[start : start + CHUNK * HEADS, :] = (read * scale).reshape(CHUNK * HEADS, DV)
    for i, value in enumerate((key0, key1, decay1 * change0, change1, decay0 * decay1)):
        update_buf[there, i * HEADS : (i + 1) * HEADS, :] = value


def flatten_heads(normed_buf, gate_buf, first, normed_ref):
    for h in range(HEADS):
        normed = normed_buf[pl.ds(h, 2 * ROWS, stride=HEADS), :]
        gate = gate_buf[pl.ds(first * HEADS + h, 2 * ROWS, stride=HEADS), :]
        normed_ref[first : first + 2 * ROWS, h * DV : (h + 1) * DV] = (normed * gate).astype(bf16)


def write_row(update, memory, store):
    key0, key1, change0, change1, decay = [
        update[i * HEADS : (i + 1) * HEADS] for i in range(5)
    ]
    (key0h, key0l), (key1h, key1l) = split(key0), split(key1)
    (change0h, change0l), (change1h, change1l) = split(change0), split(change1)
    left = jnp.concatenate([key0h, key0l, key0h, key1h, key1l, key1h], axis=0)
    left = left.T.astype(bf16)
    right = jnp.concatenate([change0h, change0h, change0l, change1h, change1h, change1l], axis=0)
    head = lax.broadcasted_iota(jnp.int32, right.shape, 0) % HEADS
    for h in range(0, HEADS, 2):
        pair = [jnp.where(head == h + i, right, 0.0).astype(bf16) for i in range(2)]
        added = dot(left, jnp.concatenate(pair, axis=1))
        for i in range(2):
            kept = memory(h + i).astype(f32) * decay[h + i : h + i + 1]
            store(h + i, (kept + added[:, i * DV : (i + 1) * DV]).astype(bf16))


def write_rows(rows, update_buf, memory, target_ref):
    for row in rows:

        def store(h, value, row=row):
            target_ref[row, h * DK : (h + 1) * DK, :] = value

        write_row(update_buf[row], lambda h, row=row: memory(row, h), store)


def first_kernel(
    x, gain, tail_query, tail_key, tail_value, conv_query, conv_key, conv_value,
    w_query, w_key, w_value, w_gate, w_beta, w_decay, decay_log, dt_bias,
    late_query_ref, late_key_ref, late_value_ref,
    early_strength_ref, early_forget_ref, late_strength_ref, late_forget_ref,
    gate_ref, raw_ref, stored_ref, conv_ref, vector_ref, value_ref,
    x_buf, gain_buf, tail_query_buf, tail_key_buf, tail_value_buf,
    conv_query_buf, conv_key_buf, conv_value_buf,
    query_buf, key_buf, value_buf, gate_buf, beta_buf, decay_buf, decay_ref, bias_ref,
    window_query, window_key, window_value, strength_all, forget_all, stored_buf,
    small_sem, weight_sem,
):
    rows = x_buf.shape[0]
    small = [
        pltpu.make_async_copy(source, target, small_sem.at[i])
        for i, (source, target) in enumerate(
            (
                (x, x_buf),
                (w_beta, beta_buf),
                (w_decay, decay_buf),
                (gain, gain_buf),
                (tail_query, tail_query_buf),
                (tail_key, tail_key_buf),
                (tail_value, tail_value_buf),
                (conv_query, conv_query_buf),
                (conv_key, conv_key_buf),
                (conv_value, conv_value_buf),
                (decay_log, decay_ref),
                (dt_bias, bias_ref),
            )
        )
    ]
    for copy in small:
        copy.start()

    def weights(j):
        pieces = (
            (w_query, query_buf, DK),
            (w_key, key_buf, DK),
            (w_value, value_buf, 2 * DV),
            (w_gate, gate_buf, 2 * DV),
        )
        copies = []
        for i, (hbm, buf, width) in enumerate(pieces):
            part = pl.ds(j * width, width)
            copies.append(
                pltpu.make_async_copy(hbm.at[:, part], buf.at[:, part], weight_sem.at[4 * j + i])
            )
        return copies

    def begin(j):
        for copy in weights(j):
            copy.start()

    for j in range(AHEAD):
        begin(j)

    for copy in small:
        copy.wait()
    head = lax.broadcasted_iota(jnp.int32, (HEADS, DV), 0)
    rate, bias = jnp.zeros((HEADS, DV), f32), jnp.zeros((HEADS, DV), f32)
    for h in range(HEADS):
        rate = jnp.where(head == h, decay_ref[h], rate)
        bias = jnp.where(head == h, bias_ref[h], bias)
    rate = -jnp.exp(rate)
    x_all = x_buf[...]

    across = (((1,), (1,)), ((), ()))
    beta = lax.dot_general(x_all, beta_buf[...], across, preferred_element_type=f32)
    decay = lax.dot_general(x_all, decay_buf[...], across, preferred_element_type=f32)
    for h in range(HEADS):
        spread(strength_all, 0, h, jnp.broadcast_to(beta[:, h : h + 1], (rows, DV)))
        spread(forget_all, 0, h, jnp.broadcast_to(decay[:, h : h + 1], (rows, DV)))
    for first in range(0, rows, ROWS):
        there = slice(first * HEADS, (first + ROWS) * HEADS)
        strength_all[there] = jax.nn.sigmoid(strength_all[there])
        raised = forget_all[there].reshape(ROWS, HEADS, DV) + bias[None]
        forget = jnp.exp(rate[None] * jax.nn.softplus(raised))
        forget_all[there] = forget.reshape(ROWS * HEADS, DV)

    history = (TAPS - 1) * ROWS

    def place(window, h, before, fresh):
        spread(window, 0, h, before)
        spread(window, history, h, fresh)

    def keep(channel, before, fresh):
        after = jnp.concatenate([before[2 * ROWS :], fresh[: 2 * ROWS]], axis=0)
        for tap in range(TAPS - 1):
            stored_buf[pl.ds(tap * SLIM + channel, ROWS, stride=(TAPS - 1) * SLIM), :] = after[
                tap * ROWS : (tap + 1) * ROWS
            ]

    for kind, buf in enumerate((conv_query_buf, conv_key_buf, conv_value_buf)):
        wide = buf[...].astype(f32)
        for h in range(HEADS):
            channel = h if kind == 2 else h // 2
            taps = wide[:, channel * DV : (channel + 1) * DV]
            for tap in range(TAPS):
                conv_ref[kind, tap, h : h + 1, :] = taps[tap : tap + 1]

    for j in range(KEYS):
        for copy in weights(j):
            copy.wait()
        if j + AHEAD < KEYS:
            begin(j + AHEAD)
        one, two = slice(j * DK, (j + 1) * DK), slice(2 * j * DV, 2 * (j + 1) * DV)
        query = dot(x_all, query_buf[:, one]).astype(bf16)
        key = dot(x_all, key_buf[:, one]).astype(bf16)
        value = dot(x_all, value_buf[:, two]).astype(bf16)
        gate = dot(x_all, gate_buf[:, two])
        gate = gate * jax.nn.sigmoid(gate)
        raw_ref[:, j * DK : (j + 1) * DK] = query[2 * ROWS :]
        raw_ref[:, (KEYS + j) * DK : (KEYS + j + 1) * DK] = key[2 * ROWS :]
        raw_ref[:, 2 * (KEYS + j) * DK : 2 * (KEYS + j + 1) * DK] = value[2 * ROWS :]
        query, key, value = query.astype(f32), key.astype(f32), value.astype(f32)
        old_query = tail_query_buf[:, :, one].reshape(history, DK).astype(f32)
        old_key = tail_key_buf[:, :, one].reshape(history, DK).astype(f32)
        old_value = tail_value_buf[:, :, two].reshape(history, 2 * DV).astype(f32)
        keep(j, old_query, query)
        keep(KEYS + j, old_key, key)
        for i in range(2):
            h, half = 2 * j + i, slice(i * DV, (i + 1) * DV)
            place(window_query, h, old_query, query)
            place(window_key, h, old_key, key)
            place(window_value, h, old_value[:, half], value[:, half])
            keep(2 * KEYS + h, old_value[:, half], value[:, half])
            spread(gate_ref, 0, h, gate[:, half] * gain_buf[...])

    late = (history + 2 * ROWS) * HEADS
    late_query_ref[...] = window_query[late:, :].astype(bf16)
    late_key_ref[...] = window_key[late:, :].astype(bf16)
    late_value_ref[...] = window_value[late:, :].astype(bf16)
    half = 2 * ROWS * HEADS
    for value, early_ref, late_ref in (
        (strength_all, early_strength_ref, late_strength_ref),
        (forget_all, early_forget_ref, late_forget_ref),
    ):
        early_ref[...] = value[:half, :]
        late_ref[...] = value[half:, :]
    stored_ref[...] = stored_buf[...].reshape(stored_ref.shape).astype(bf16)
    windows = (window_query, window_key, window_value)
    find_vectors(
        lambda kind, tap, first: part_of(windows[kind], tap, first, CHUNK),
        conv_ref,
        vector_ref,
        value_ref,
    )


def send_kernel(
    parent_ref, vector_ref, value_ref, strength_ref, forget_ref, tails_ref, state,
    slots, normed_buf,
    state_buf, stored_buf, found_buf, update_buf, wanted_buf, wanted_ref,
    look_sem, state_sem, slot_sem,
):
    count = slots.shape[0]

    def load(row):
        return pltpu.make_async_copy(state.at[row], state_buf.at[row], state_sem.at[row])

    for row in range(ROWS):
        load(row).start()
    parent = parent_ref[...]
    mine = parent // ROWS == lax.axis_index("branch")
    wanted = jnp.max(jnp.where(mine, parent % ROWS, -1).astype(f32), axis=-1, keepdims=True)
    wanted_buf[...] = jnp.broadcast_to(wanted.astype(jnp.int32), wanted_buf.shape)
    look = pltpu.make_async_copy(wanted_buf, wanted_ref, look_sem.at[0])
    look.start()
    for row in range(ROWS):
        stored_buf[row, BODY:, :] = tails_ref[row]

    def ship(slot, row):
        return pltpu.make_async_copy(stored_buf.at[row], slots.at[slot], slot_sem.at[slot])

    def memory(row, h):
        return state_buf[row, h * DK : (h + 1) * DK, :]

    for start in range(0, ROWS, SHIP):
        rows = range(start, start + SHIP)
        for row in rows:
            load(row).wait()
        recall(rows, memory, vector_ref, found_buf)
        for first in range(start, start + SHIP, CHUNK):
            finish(
                first, strength_ref, forget_ref,
                vector_ref, value_ref, found_buf, normed_buf, update_buf,
            )
        write_rows(rows, update_buf, memory, stored_buf)

        if start == 0:
            look.wait()

        def begin(slot, carry, start=start):
            row = wanted_ref[slot, 0, 0]

            @pl.when((row >= start) & (row < start + SHIP))
            def _():
                ship(slot, row).start()

            return carry

        lax.fori_loop(0, count, begin, 0, unroll=4)
    def end(slot, carry):
        @pl.when(wanted_ref[slot, 0, 0] >= 0)
        def _():
            ship(slot, 0).wait()

        return carry

    lax.fori_loop(0, count, end, 0, unroll=4)


def second_kernel(
    parent_ref, late_query, late_key, late_value, late_strength, late_forget, gate_ref, conv_ref,
    early_ref, slots, w_out,
    *refs,
):
    sums = refs[:PARTS]
    (
        update_ref, last_ref, memory_buf,
        tail_buf, window_query, window_key, window_value,
        vector_buf, value_buf, found_buf, normed_buf, out_buf, normed_ref,
        tail_sem, memory_sem, out_sem,
    ) = refs[PARTS:]
    def load_tail(row):
        return pltpu.make_async_copy(
            slots.at[parent_ref[row] // ROWS, pl.ds(BODY, SLOT - BODY)], tail_buf.at[row], tail_sem.at[row]
        )

    def load(row):
        return pltpu.make_async_copy(
            slots.at[parent_ref[row] // ROWS, pl.ds(0, BODY)], memory_buf.at[row], memory_sem.at[row]
        )

    for row in range(ROWS):
        load_tail(row).start()
    for row in range(ROWS):
        load(row).start()
    width = out_buf.shape[2]
    place = lax.axis_index("tensor")

    def load_out(shift):
        start = pl.multiple_of((place + shift) % PARTS * width, width)
        return pltpu.make_async_copy(
            w_out.at[:, pl.ds(start, width)], out_buf.at[shift], out_sem.at[shift]
        )

    for shift in range(PARTS):
        load_out(shift).start()
    wide = widening()
    flatten_heads(early_ref, gate_ref, 0, normed_ref)
    for row in range(ROWS):
        load_tail(row).wait()
    for row in range(ROWS):
        tails = tail_buf[row]
        last_ref[row] = tails[2 * SLIM :]
        spaced = dot(wide, tails)
        for tap in range(TAPS - 1):
            for kind, window in enumerate((window_query, window_key, window_value)):
                start = tap * WIDE + kind * HEADS
                window[(tap * ROWS + row) * HEADS : (tap * ROWS + row + 1) * HEADS, :] = spaced[
                    start : start + HEADS
                ]
    windows = (window_query, window_key, window_value)
    fresh = (late_query, late_key, late_value)

    def window(kind, tap, first):
        if tap < TAPS - 1:
            return part_of(windows[kind], tap, first, CHUNK)
        return part_of(fresh[kind], tap - (TAPS - 1), first, CHUNK).astype(f32)

    find_vectors(window, conv_ref, vector_buf, value_buf)

    def group(index, carry):
        rows = [index * LATE + i for i in range(LATE)]
        for row in rows:
            load(row).wait()
        recall(rows, lambda row, h: memory_buf[row, h * DK : (h + 1) * DK, :], vector_buf, found_buf)
        return carry

    lax.fori_loop(0, ROWS // LATE, group, 0)
    for first in range(0, ROWS, CHUNK):
        finish(
            first, late_strength, late_forget,
            vector_buf, value_buf, found_buf, normed_buf, update_ref,
        )
    flatten_heads(normed_buf, gate_ref, 2 * ROWS, normed_ref)
    for shift in range(PARTS):
        load_out(shift).wait()
    normed = normed_ref[...]
    for shift in range(PARTS):
        sums[shift][...] = dot(normed, out_buf[shift]).astype(sums[shift].dtype)


def final_kernel(
    update_ref, last_ref, raw_ref, memory_ref,
    final, query, key, value,
    final_buf, last_buf, query_buf, key_buf, value_buf, final_sem, tail_sem,
):
    def save(row):
        return pltpu.make_async_copy(final_buf.at[row], final.at[row], final_sem.at[row])

    start = 0
    last_buf[...] = last_ref[...].astype(f32).reshape(ROWS * SLIM, DV)
    tails = []
    for i, (ref, target) in enumerate(((query_buf, query), (key_buf, key), (value_buf, value))):
        width = ref.shape[2]
        for channel in range(width // DV):
            block = last_buf[pl.ds(start // DV + channel, ROWS, stride=SLIM), :]
            ref[0, :, channel * DV : (channel + 1) * DV] = block.astype(bf16)
        for step in range(2):
            ref[1 + step] = raw_ref[step * ROWS : (step + 1) * ROWS, start : start + width]
        start += width
        tails.append(pltpu.make_async_copy(ref, target, tail_sem.at[i]))
        tails[i].start()

    def group(index, carry):
        rows = [index * GROUP + i for i in range(GROUP)]
        write_rows(
            rows, update_ref, lambda row, h: memory_ref[row, h * DK : (h + 1) * DK, :], final_buf
        )
        for row in rows:
            save(row).start()
        return carry

    lax.fori_loop(0, ROWS // GROUP, group, 0)
    for copy in tails:
        copy.wait()
    for row in range(ROWS):
        save(row).wait()


VMEM = pl.BlockSpec(memory_space=pltpu.VMEM)
SMEM = pl.BlockSpec(memory_space=pltpu.SMEM)
HBM = pl.BlockSpec(memory_space=pltpu.HBM)
PARAMS = pltpu.CompilerParams(vmem_limit_bytes=VMEM_BYTES)


def in_hbm(array):
    return pltpu.with_memory_space_constraint(array, pltpu.HBM)


def shape(dims, kind):
    return jax.ShapeDtypeStruct(dims, kind)


def buffer(array):
    return pltpu.VMEM(array.shape, array.dtype)


def work_buffers():
    return [
        pltpu.VMEM((ROWS, 4 * HEADS, DV), f32),
        pltpu.VMEM((2, ROWS, HEADS, DV), f32),
        pltpu.VMEM((ROWS, 4 * HEADS, DV), f32),
        pltpu.VMEM((2 * ROWS * HEADS, DV), f32),
    ]


def first_half(arrays):
    rows = arrays[0].shape[0]
    half = rows // 2
    window = pltpu.VMEM(((TAPS - 1) * ROWS * HEADS + rows * HEADS, DV), f32)
    wide = pltpu.VMEM((rows * HEADS, DV), f32)
    return pl.pallas_call(
        first_kernel,
        in_specs=[HBM] * len(arrays),
        out_specs=[VMEM] * 13,
        out_shape=(
            *[shape((half * HEADS, DV), bf16)] * 3,
            *[shape((half * HEADS, DV), f32)] * 4,
            shape((rows * HEADS, DV), f32),
            shape((half, SLIM * DV), bf16),
            shape((ROWS, (TAPS - 1) * SLIM, DV), bf16),
            shape((3, TAPS, HEADS, DV), f32),
            shape((ROWS, 4 * HEADS, DV), f32),
            shape((2, ROWS, HEADS, DV), f32),
        ),
        scratch_shapes=[
            *[buffer(array) for array in arrays[:-2]],
            *[pltpu.SMEM(array.shape, f32) for array in arrays[-2:]],
            window,
            window,
            window,
            wide,
            wide,
            pltpu.VMEM((ROWS * (TAPS - 1) * SLIM, DV), f32),
            pltpu.SemaphoreType.DMA((len(arrays) - 4,)),
            pltpu.SemaphoreType.DMA((4 * KEYS,)),
        ],
        compiler_params=PARAMS,
        name="first_half",
    )(*[in_hbm(array) for array in arrays])


def fill_slots(parents, early, tails, state):
    count = parents.shape[0]
    _, _, found, _ = work_buffers()
    return pl.pallas_call(
        send_kernel,
        in_specs=[VMEM] * 6 + [HBM],
        out_specs=[HBM, VMEM],
        out_shape=(
            shape((count, SLOT, DV), bf16),
            shape((2 * ROWS * HEADS, DV), f32),
        ),
        scratch_shapes=[
            buffer(state),
            pltpu.VMEM((ROWS, SLOT, DV), bf16),
            found,
            pltpu.VMEM((ROWS, 5 * HEADS, DV), f32),
            pltpu.VMEM((count, 1, DV), jnp.int32),
            pltpu.SMEM((count, 1, DV), jnp.int32),
            pltpu.SemaphoreType.DMA((1,)),
            pltpu.SemaphoreType.DMA((ROWS,)),
            pltpu.SemaphoreType.DMA((count,)),
        ],
        compiler_params=PARAMS,
        name="fill_slots",
    )(parents, *early, tails, in_hbm(state))


def second_half(parents, late, conv, early, slots, w_out):
    window = pltpu.VMEM(((TAPS - 1) * ROWS * HEADS, DV), f32)
    rows, width = 4 * ROWS, w_out.shape[1] // PARTS
    *sums, update, last, memory = pl.pallas_call(
        second_kernel,
        in_specs=[SMEM] + [VMEM] * 8 + [HBM] * 2,
        out_specs=[VMEM] * (PARTS + 3),
        out_shape=(
            shape((rows, width), f32),
            *[shape((rows, width), bf16)] * (PARTS - 1),
            shape((ROWS, 5 * HEADS, DV), f32),
            shape((ROWS, SLIM, DV), bf16),
            shape((ROWS, BODY, DV), bf16),
        ),
        scratch_shapes=[
            pltpu.VMEM((ROWS, SLOT - BODY, DV), bf16),
            window,
            window,
            window,
            *work_buffers(),
            pltpu.VMEM((PARTS, w_out.shape[0], width), bf16),
            pltpu.VMEM((rows, HEADS * DV), bf16),
            pltpu.SemaphoreType.DMA((ROWS,)),
            pltpu.SemaphoreType.DMA((ROWS,)),
            pltpu.SemaphoreType.DMA((PARTS,)),
        ],
        compiler_params=PARAMS,
        name="second_half",
    )(parents, *late, conv, early, in_hbm(slots), in_hbm(w_out))
    return sums, update, last, memory


def last_memory(update, last, raw, memory):
    tails = [shape((TAPS - 1, ROWS, width), bf16) for width in (KEYS * DK, KEYS * DK, HEADS * DV)]
    return pl.pallas_call(
        final_kernel,
        in_specs=[VMEM] * 4,
        out_specs=[HBM] * 4,
        out_shape=(shape((ROWS, BODY, DV), bf16), *tails),
        scratch_shapes=[
            buffer(memory),
            pltpu.VMEM((ROWS * SLIM, DV), f32),
            *[buffer(tail) for tail in tails],
            pltpu.SemaphoreType.DMA((ROWS,)),
            pltpu.SemaphoreType.DMA((3,)),
        ],
        compiler_params=PARAMS,
        name="last_memory",
    )(update, last, raw, memory)


def sum_heads(blocks):
    total = blocks[0]
    for shift in (2, 1, 3):
        pairs = [(i, (i + shift) % PARTS) for i in range(PARTS)]
        total = total + lax.ppermute(blocks[shift], "tensor", pairs).astype(f32)
    return total.astype(bf16)


def per_device(
    inputs,
    w_query,
    w_key,
    w_value,
    w_gate_z,
    w_beta,
    w_decay,
    conv_query,
    conv_key,
    conv_value,
    decay_log,
    dt_bias,
    norm_gain,
    w_out,
    state,
    tail_query,
    tail_key,
    tail_value,
    parents,
):
    groups = lax.axis_size("branch")
    asked = jnp.broadcast_to(parents[None, None, :], (groups, 1, ROWS))
    asked = lax.all_to_all(asked, "branch", split_axis=0, concat_axis=0, tiled=True)

    flat_state = state.reshape(ROWS, BODY, DV)
    (
        late_query, late_key, late_value, *scales, raw, stored_tails, conv, vectors, values
    ) = first_half(
        (
            inputs.reshape(-1, inputs.shape[-1]),
            norm_gain[None],
            tail_query.transpose(1, 0, 2),
            tail_key.transpose(1, 0, 2),
            tail_value.transpose(1, 0, 2),
            conv_query,
            conv_key,
            conv_value,
            w_query,
            w_key,
            w_value,
            w_gate_z,
            w_beta.T,
            w_decay.T,
            decay_log,
            dt_bias,
        )
    )
    shipped, early = fill_slots(asked, (vectors, values, *scales[:2]), stored_tails, flat_state)
    arrived = lax.all_to_all(shipped, "branch", split_axis=0, concat_axis=0, tiled=True)
    late = (late_query, late_key, late_value, *scales[2:])
    sums, update, last, memory = second_half(
        parents, late, conv, early, arrived, w_out
    )
    out_rows = sum_heads(sums).reshape(inputs.shape[0], ROWS, -1)
    final_state, *final_tails = last_memory(update, last, raw, memory)
    return (
        out_rows,
        final_state.reshape(state.shape),
        *[tail.transpose(1, 0, 2) for tail in final_tails],
    )


def solution(mesh):
    return jax.shard_map(
        per_device,
        mesh=mesh,
        in_specs=(
            P(None, "branch", None),
            P(None, "tensor"),
            P(None, "tensor"),
            P(None, "tensor"),
            P(None, "tensor"),
            P(None, "tensor"),
            P(None, "tensor"),
            P(None, "tensor"),
            P(None, "tensor"),
            P(None, "tensor"),
            P("tensor"),
            P("tensor"),
            P(),
            P("tensor", None),
            P("branch", "tensor", None, None),
            P("branch", None, "tensor"),
            P("branch", None, "tensor"),
            P("branch", None, "tensor"),
            P("branch"),
        ),
        out_specs=(
            P(None, "branch", "tensor"),
            P("branch", "tensor", None, None),
            P("branch", None, "tensor"),
            P("branch", None, "tensor"),
            P("branch", None, "tensor"),
        ),
        check_vma=False,
    )
```

```python
import jax
import jax.numpy as jnp
from jax import lax
from jax.experimental import pallas as pl
from jax.experimental.pallas import tpu as pltpu
from jax.sharding import PartitionSpec as P

DK = 128
DV = 128
HEADS = 8
KEYS = 4
ROWS = 16
TAPS = 4
WIDE = 3 * HEADS
SLIM = 2 * KEYS + HEADS
BODY = HEADS * DK
SLOT = BODY + (TAPS - 1) * SLIM
VMEM_BYTES = 48 * 1024 * 1024
CHUNK = 4
PARTS = 4
GROUP = 8
LATE = 16
AHEAD = 2
SHIP = 4
f32 = jnp.float32
bf16 = jnp.bfloat16


def split(value):
    high = value.astype(bf16).astype(f32)
    return high, value - high


def dot(left, right):
    return jnp.dot(left, right, preferred_element_type=f32)


def inner(left, right):
    return jnp.sum(left * right, axis=-1, keepdims=True)


def widening():
    row = lax.broadcasted_iota(jnp.int32, ((TAPS - 1) * WIDE, (TAPS - 1) * SLIM), 0)
    column = lax.broadcasted_iota(jnp.int32, ((TAPS - 1) * WIDE, (TAPS - 1) * SLIM), 1)
    tap, place = row // WIDE, row % WIDE
    origin = tap * SLIM + jnp.where(place < 2 * HEADS, place // 2, place - HEADS)
    return jnp.where(origin == column, 1.0, 0.0).astype(bf16)


def spread(target, start, h, block):
    target[pl.ds(start * HEADS + h, block.shape[0], stride=HEADS), :] = block


def part_of(ref, index, first, count):
    return ref[pl.ds(index * ROWS * HEADS + first * HEADS, count * HEADS), :]


def find_vectors(window, conv_ref, vector_buf, value_buf):
    for first in range(0, ROWS, CHUNK):
        there = slice(first, first + CHUNK)
        for step in range(2):
            for kind in range(3):
                mixed = 0.0
                for tap in range(TAPS):
                    rows = window(kind, step + tap, first).reshape(CHUNK, HEADS, DV)
                    mixed = mixed + rows * conv_ref[kind, tap][None]
                mixed = mixed * jax.nn.sigmoid(mixed)
                if kind == 2:
                    value_buf[step, there] = mixed
                    continue
                unit = mixed * lax.rsqrt(inner(mixed, mixed) + 1e-06)
                if kind == 0:
                    unit = unit * DK ** (-0.5)
                place = 2 * step + 1 - kind
                vector_buf[there, place * HEADS : (place + 1) * HEADS, :] = unit


def recall(rows, memory, vector_buf, found_buf):
    head = lax.broadcasted_iota(jnp.int32, (HEADS, DV), 0)
    for row in rows:
        high, low = split(vector_buf[row])
        left = jnp.concatenate([high, low], axis=0).astype(bf16)
        found = [jnp.zeros((HEADS, DV), f32)] * 4
        for h in range(0, HEADS, 2):
            pair = jnp.concatenate([memory(row, h), memory(row, h + 1)], axis=1)
            product = dot(left, pair)
            product = product[: 4 * HEADS] + product[4 * HEADS :]
            for i in range(4):
                block = product[i * HEADS : (i + 1) * HEADS]
                found[i] = jnp.where(head == h, block[:, :DV], found[i])
                found[i] = jnp.where(head == h + 1, block[:, DV:], found[i])
        found_buf[row] = jnp.concatenate(found, axis=0)


def finish(first, strengths, decays, vector_buf, value_buf, found_buf, normed_buf, update_buf):
    there = slice(first, first + CHUNK)

    def piece(ref, i):
        return ref[there, i * HEADS : (i + 1) * HEADS, :]

    def steps(ref):
        return [part_of(ref, step, first, CHUNK).reshape(CHUNK, HEADS, DV) for step in range(2)]

    key0, query0, key1, query1 = [piece(vector_buf, i) for i in range(4)]
    found0, found1, found2, found3 = [piece(found_buf, i) for i in range(4)]
    strength0, strength1 = steps(strengths)
    decay0, decay1 = steps(decays)
    change0 = (value_buf[0, there] - decay0 * found0) * strength0
    read0 = decay0 * found1 + inner(query0, key0) * change0
    kept = decay0 * found2 + inner(key1, key0) * change0
    change1 = (value_buf[1, there] - decay1 * kept) * strength1
    kept = decay0 * found3 + inner(query1, key0) * change0
    read1 = decay1 * kept + inner(query1, key1) * change1
    for step, read in enumerate((read0, read1)):
        scale = lax.rsqrt(jnp.mean(read * read, axis=-1, keepdims=True) + 1e-06)
        start = (step * ROWS + first) * HEADS
        normed_buf[start : start + CHUNK * HEADS, :] = (read * scale).reshape(CHUNK * HEADS, DV)
    for i, value in enumerate((key0, key1, decay1 * change0, change1, decay0 * decay1)):
        update_buf[there, i * HEADS : (i + 1) * HEADS, :] = value


def flatten_heads(normed_buf, gate_buf, first, normed_ref):
    for h in range(HEADS):
        normed = normed_buf[pl.ds(h, 2 * ROWS, stride=HEADS), :]
        gate = gate_buf[pl.ds(first * HEADS + h, 2 * ROWS, stride=HEADS), :]
        normed_ref[first : first + 2 * ROWS, h * DV : (h + 1) * DV] = (normed * gate).astype(bf16)


def write_row(update, memory, store):
    key0, key1, change0, change1, decay = [
        update[i * HEADS : (i + 1) * HEADS] for i in range(5)
    ]
    (key0h, key0l), (key1h, key1l) = split(key0), split(key1)
    (change0h, change0l), (change1h, change1l) = split(change0), split(change1)
    left = jnp.concatenate([key0h, key0l, key0h, key1h, key1l, key1h], axis=0)
    left = left.T.astype(bf16)
    right = jnp.concatenate([change0h, change0h, change0l, change1h, change1h, change1l], axis=0)
    head = lax.broadcasted_iota(jnp.int32, right.shape, 0) % HEADS
    for h in range(0, HEADS, 2):
        pair = [jnp.where(head == h + i, right, 0.0).astype(bf16) for i in range(2)]
        added = dot(left, jnp.concatenate(pair, axis=1))
        for i in range(2):
            kept = memory(h + i).astype(f32) * decay[h + i : h + i + 1]
            store(h + i, (kept + added[:, i * DV : (i + 1) * DV]).astype(bf16))


def write_rows(rows, update_buf, memory, target_ref):
    for row in rows:

        def store(h, value, row=row):
            target_ref[row, h * DK : (h + 1) * DK, :] = value

        write_row(update_buf[row], lambda h, row=row: memory(row, h), store)


def first_kernel(
    x, gain, tail_query, tail_key, tail_value, conv_query, conv_key, conv_value,
    w_query, w_key, w_value, w_gate, w_beta, w_decay, decay_log, dt_bias,
    late_query_ref, late_key_ref, late_value_ref,
    early_strength_ref, early_forget_ref, late_strength_ref, late_forget_ref,
    gate_ref, raw_ref, stored_ref, conv_ref, vector_ref, value_ref,
    x_buf, gain_buf, tail_query_buf, tail_key_buf, tail_value_buf,
    conv_query_buf, conv_key_buf, conv_value_buf,
    query_buf, key_buf, value_buf, gate_buf, beta_buf, decay_buf, decay_ref, bias_ref,
    window_query, window_key, window_value, strength_all, forget_all, stored_buf,
    small_sem, weight_sem,
):
    rows = x_buf.shape[0]
    small = [
        pltpu.make_async_copy(source, target, small_sem.at[i])
        for i, (source, target) in enumerate(
            (
                (x, x_buf),
                (w_beta, beta_buf),
                (w_decay, decay_buf),
                (gain, gain_buf),
                (tail_query, tail_query_buf),
                (tail_key, tail_key_buf),
                (tail_value, tail_value_buf),
                (conv_query, conv_query_buf),
                (conv_key, conv_key_buf),
                (conv_value, conv_value_buf),
                (decay_log, decay_ref),
                (dt_bias, bias_ref),
            )
        )
    ]
    for copy in small:
        copy.start()

    def weights(j):
        pieces = (
            (w_query, query_buf, DK),
            (w_key, key_buf, DK),
            (w_value, value_buf, 2 * DV),
            (w_gate, gate_buf, 2 * DV),
        )
        copies = []
        for i, (hbm, buf, width) in enumerate(pieces):
            part = pl.ds(j * width, width)
            copies.append(
                pltpu.make_async_copy(hbm.at[:, part], buf.at[:, part], weight_sem.at[4 * j + i])
            )
        return copies

    def begin(j):
        for copy in weights(j):
            copy.start()

    for j in range(AHEAD):
        begin(j)

    for copy in small:
        copy.wait()
    head = lax.broadcasted_iota(jnp.int32, (HEADS, DV), 0)
    rate, bias = jnp.zeros((HEADS, DV), f32), jnp.zeros((HEADS, DV), f32)
    for h in range(HEADS):
        rate = jnp.where(head == h, decay_ref[h], rate)
        bias = jnp.where(head == h, bias_ref[h], bias)
    rate = -jnp.exp(rate)
    x_all = x_buf[...]

    across = (((1,), (1,)), ((), ()))
    beta = lax.dot_general(x_all, beta_buf[...], across, preferred_element_type=f32)
    decay = lax.dot_general(x_all, decay_buf[...], across, preferred_element_type=f32)
    for h in range(HEADS):
        spread(strength_all, 0, h, jnp.broadcast_to(beta[:, h : h + 1], (rows, DV)))
        spread(forget_all, 0, h, jnp.broadcast_to(decay[:, h : h + 1], (rows, DV)))
    for first in range(0, rows, ROWS):
        there = slice(first * HEADS, (first + ROWS) * HEADS)
        strength_all[there] = jax.nn.sigmoid(strength_all[there])
        raised = forget_all[there].reshape(ROWS, HEADS, DV) + bias[None]
        forget = jnp.exp(rate[None] * jax.nn.softplus(raised))
        forget_all[there] = forget.reshape(ROWS * HEADS, DV)

    history = (TAPS - 1) * ROWS

    def place(window, h, before, fresh):
        spread(window, 0, h, before)
        spread(window, history, h, fresh)

    def keep(channel, before, fresh):
        after = jnp.concatenate([before[2 * ROWS :], fresh[: 2 * ROWS]], axis=0)
        for tap in range(TAPS - 1):
            stored_buf[pl.ds(tap * SLIM + channel, ROWS, stride=(TAPS - 1) * SLIM), :] = after[
                tap * ROWS : (tap + 1) * ROWS
            ]

    for kind, buf in enumerate((conv_query_buf, conv_key_buf, conv_value_buf)):
        wide = buf[...].astype(f32)
        for h in range(HEADS):
            channel = h if kind == 2 else h // 2
            taps = wide[:, channel * DV : (channel + 1) * DV]
            for tap in range(TAPS):
                conv_ref[kind, tap, h : h + 1, :] = taps[tap : tap + 1]

    for j in range(KEYS):
        for copy in weights(j):
            copy.wait()
        if j + AHEAD < KEYS:
            begin(j + AHEAD)
        one, two = slice(j * DK, (j + 1) * DK), slice(2 * j * DV, 2 * (j + 1) * DV)
        query = dot(x_all, query_buf[:, one]).astype(bf16)
        key = dot(x_all, key_buf[:, one]).astype(bf16)
        value = dot(x_all, value_buf[:, two]).astype(bf16)
        gate = dot(x_all, gate_buf[:, two])
        gate = gate * jax.nn.sigmoid(gate)
        raw_ref[:, j * DK : (j + 1) * DK] = query[2 * ROWS :]
        raw_ref[:, (KEYS + j) * DK : (KEYS + j + 1) * DK] = key[2 * ROWS :]
        raw_ref[:, 2 * (KEYS + j) * DK : 2 * (KEYS + j + 1) * DK] = value[2 * ROWS :]
        query, key, value = query.astype(f32), key.astype(f32), value.astype(f32)
        old_query = tail_query_buf[:, :, one].reshape(history, DK).astype(f32)
        old_key = tail_key_buf[:, :, one].reshape(history, DK).astype(f32)
        old_value = tail_value_buf[:, :, two].reshape(history, 2 * DV).astype(f32)
        keep(j, old_query, query)
        keep(KEYS + j, old_key, key)
        for i in range(2):
            h, half = 2 * j + i, slice(i * DV, (i + 1) * DV)
            place(window_query, h, old_query, query)
            place(window_key, h, old_key, key)
            place(window_value, h, old_value[:, half], value[:, half])
            keep(2 * KEYS + h, old_value[:, half], value[:, half])
            spread(gate_ref, 0, h, gate[:, half] * gain_buf[...])

    late = (history + 2 * ROWS) * HEADS
    late_query_ref[...] = window_query[late:, :].astype(bf16)
    late_key_ref[...] = window_key[late:, :].astype(bf16)
    late_value_ref[...] = window_value[late:, :].astype(bf16)
    half = 2 * ROWS * HEADS
    for value, early_ref, late_ref in (
        (strength_all, early_strength_ref, late_strength_ref),
        (forget_all, early_forget_ref, late_forget_ref),
    ):
        early_ref[...] = value[:half, :]
        late_ref[...] = value[half:, :]
    stored_ref[...] = stored_buf[...].reshape(stored_ref.shape).astype(bf16)
    windows = (window_query, window_key, window_value)
    find_vectors(
        lambda kind, tap, first: part_of(windows[kind], tap, first, CHUNK),
        conv_ref,
        vector_ref,
        value_ref,
    )


def send_kernel(
    parent_ref, vector_ref, value_ref, strength_ref, forget_ref, tails_ref, state,
    slots, normed_buf,
    state_buf, stored_buf, found_buf, update_buf, wanted_buf, wanted_ref,
    look_sem, state_sem, slot_sem,
):
    count = slots.shape[0]

    def load(row):
        return pltpu.make_async_copy(state.at[row], state_buf.at[row], state_sem.at[row])

    for row in range(ROWS):
        load(row).start()
    parent = parent_ref[...]
    mine = parent // ROWS == lax.axis_index("branch")
    wanted = jnp.max(jnp.where(mine, parent % ROWS, -1).astype(f32), axis=-1, keepdims=True)
    wanted_buf[...] = jnp.broadcast_to(wanted.astype(jnp.int32), wanted_buf.shape)
    look = pltpu.make_async_copy(wanted_buf, wanted_ref, look_sem.at[0])
    look.start()
    for row in range(ROWS):
        stored_buf[row, BODY:, :] = tails_ref[row]

    def ship(slot, row):
        return pltpu.make_async_copy(stored_buf.at[row], slots.at[slot], slot_sem.at[slot])

    def memory(row, h):
        return state_buf[row, h * DK : (h + 1) * DK, :]

    for start in range(0, ROWS, SHIP):
        rows = range(start, start + SHIP)
        for row in rows:
            load(row).wait()
        recall(rows, memory, vector_ref, found_buf)
        for first in range(start, start + SHIP, CHUNK):
            finish(
                first, strength_ref, forget_ref,
                vector_ref, value_ref, found_buf, normed_buf, update_buf,
            )
        write_rows(rows, update_buf, memory, stored_buf)

        if start == 0:
            look.wait()

        def begin(slot, carry, start=start):
            row = wanted_ref[slot, 0, 0]

            @pl.when((row >= start) & (row < start + SHIP))
            def _():
                ship(slot, row).start()

            return carry

        lax.fori_loop(0, count, begin, 0, unroll=count)
    def end(slot, carry):
        @pl.when(wanted_ref[slot, 0, 0] >= 0)
        def _():
            ship(slot, 0).wait()

        return carry

    lax.fori_loop(0, count, end, 0, unroll=count)


def second_kernel(
    parent_ref, late_query, late_key, late_value, late_strength, late_forget, gate_ref, conv_ref,
    early_ref, slots, w_out,
    *refs,
):
    sums = refs[:PARTS]
    (
        update_ref, last_ref, memory_buf,
        tail_buf, window_query, window_key, window_value,
        vector_buf, value_buf, found_buf, normed_buf, out_buf, normed_ref,
        tail_sem, memory_sem, out_sem,
    ) = refs[PARTS:]
    def load_tail(row):
        return pltpu.make_async_copy(
            slots.at[parent_ref[row] // ROWS, pl.ds(BODY, SLOT - BODY)], tail_buf.at[row], tail_sem.at[row]
        )

    def load(row):
        return pltpu.make_async_copy(
            slots.at[parent_ref[row] // ROWS, pl.ds(0, BODY)], memory_buf.at[row], memory_sem.at[row]
        )

    for row in range(ROWS):
        load_tail(row).start()
    for row in range(ROWS):
        load(row).start()
    width = out_buf.shape[2]
    place = lax.axis_index("tensor")

    def load_out(shift):
        start = pl.multiple_of((place + shift) % PARTS * width, width)
        return pltpu.make_async_copy(
            w_out.at[:, pl.ds(start, width)], out_buf.at[shift], out_sem.at[shift]
        )

    for shift in range(PARTS):
        load_out(shift).start()
    wide = widening()
    flatten_heads(early_ref, gate_ref, 0, normed_ref)
    for row in range(ROWS):
        load_tail(row).wait()
    for row in range(ROWS):
        tails = tail_buf[row]
        last_ref[row] = tails[2 * SLIM :]
        spaced = dot(wide, tails)
        for tap in range(TAPS - 1):
            for kind, window in enumerate((window_query, window_key, window_value)):
                start = tap * WIDE + kind * HEADS
                window[(tap * ROWS + row) * HEADS : (tap * ROWS + row + 1) * HEADS, :] = spaced[
                    start : start + HEADS
                ]
    windows = (window_query, window_key, window_value)
    fresh = (late_query, late_key, late_value)

    def window(kind, tap, first):
        if tap < TAPS - 1:
            return part_of(windows[kind], tap, first, CHUNK)
        return part_of(fresh[kind], tap - (TAPS - 1), first, CHUNK).astype(f32)

    find_vectors(window, conv_ref, vector_buf, value_buf)

    def group(index, carry):
        rows = [index * LATE + i for i in range(LATE)]
        for row in rows:
            load(row).wait()
        recall(rows, lambda row, h: memory_buf[row, h * DK : (h + 1) * DK, :], vector_buf, found_buf)
        return carry

    lax.fori_loop(0, ROWS // LATE, group, 0)
    for first in range(0, ROWS, CHUNK):
        finish(
            first, late_strength, late_forget,
            vector_buf, value_buf, found_buf, normed_buf, update_ref,
        )
    flatten_heads(normed_buf, gate_ref, 2 * ROWS, normed_ref)
    for shift in range(PARTS):
        load_out(shift).wait()
    normed = normed_ref[...]
    for shift in range(PARTS):
        sums[shift][...] = dot(normed, out_buf[shift]).astype(sums[shift].dtype)


def final_kernel(
    update_ref, last_ref, raw_ref, memory_ref,
    final, query, key, value,
    final_buf, last_buf, query_buf, key_buf, value_buf, final_sem, tail_sem,
):
    def save(row):
        return pltpu.make_async_copy(final_buf.at[row], final.at[row], final_sem.at[row])

    start = 0
    last_buf[...] = last_ref[...].astype(f32).reshape(ROWS * SLIM, DV)
    tails = []
    for i, (ref, target) in enumerate(((query_buf, query), (key_buf, key), (value_buf, value))):
        width = ref.shape[2]
        for channel in range(width // DV):
            block = last_buf[pl.ds(start // DV + channel, ROWS, stride=SLIM), :]
            ref[0, :, channel * DV : (channel + 1) * DV] = block.astype(bf16)
        for step in range(2):
            ref[1 + step] = raw_ref[step * ROWS : (step + 1) * ROWS, start : start + width]
        start += width
        tails.append(pltpu.make_async_copy(ref, target, tail_sem.at[i]))
        tails[i].start()

    def group(index, carry):
        rows = [index * GROUP + i for i in range(GROUP)]
        write_rows(
            rows, update_ref, lambda row, h: memory_ref[row, h * DK : (h + 1) * DK, :], final_buf
        )
        for row in rows:
            save(row).start()
        return carry

    lax.fori_loop(0, ROWS // GROUP, group, 0)
    for copy in tails:
        copy.wait()
    for row in range(ROWS):
        save(row).wait()


VMEM = pl.BlockSpec(memory_space=pltpu.VMEM)
SMEM = pl.BlockSpec(memory_space=pltpu.SMEM)
HBM = pl.BlockSpec(memory_space=pltpu.HBM)
PARAMS = pltpu.CompilerParams(vmem_limit_bytes=VMEM_BYTES)


def in_hbm(array):
    return pltpu.with_memory_space_constraint(array, pltpu.HBM)


def shape(dims, kind):
    return jax.ShapeDtypeStruct(dims, kind)


def buffer(array):
    return pltpu.VMEM(array.shape, array.dtype)


def work_buffers():
    return [
        pltpu.VMEM((ROWS, 4 * HEADS, DV), f32),
        pltpu.VMEM((2, ROWS, HEADS, DV), f32),
        pltpu.VMEM((ROWS, 4 * HEADS, DV), f32),
        pltpu.VMEM((2 * ROWS * HEADS, DV), f32),
    ]


def first_half(arrays):
    rows = arrays[0].shape[0]
    half = rows // 2
    window = pltpu.VMEM(((TAPS - 1) * ROWS * HEADS + rows * HEADS, DV), f32)
    wide = pltpu.VMEM((rows * HEADS, DV), f32)
    return pl.pallas_call(
        first_kernel,
        in_specs=[HBM] * len(arrays),
        out_specs=[VMEM] * 13,
        out_shape=(
            *[shape((half * HEADS, DV), bf16)] * 3,
            *[shape((half * HEADS, DV), f32)] * 4,
            shape((rows * HEADS, DV), f32),
            shape((half, SLIM * DV), bf16),
            shape((ROWS, (TAPS - 1) * SLIM, DV), bf16),
            shape((3, TAPS, HEADS, DV), f32),
            shape((ROWS, 4 * HEADS, DV), f32),
            shape((2, ROWS, HEADS, DV), f32),
        ),
        scratch_shapes=[
            *[buffer(array) for array in arrays[:-2]],
            *[pltpu.SMEM(array.shape, f32) for array in arrays[-2:]],
            window,
            window,
            window,
            wide,
            wide,
            pltpu.VMEM((ROWS * (TAPS - 1) * SLIM, DV), f32),
            pltpu.SemaphoreType.DMA((len(arrays) - 4,)),
            pltpu.SemaphoreType.DMA((4 * KEYS,)),
        ],
        compiler_params=PARAMS,
        name="first_half",
    )(*[in_hbm(array) for array in arrays])


def fill_slots(parents, early, tails, state):
    count = parents.shape[0]
    _, _, found, _ = work_buffers()
    return pl.pallas_call(
        send_kernel,
        in_specs=[VMEM] * 6 + [HBM],
        out_specs=[HBM, VMEM],
        out_shape=(
            shape((count, SLOT, DV), bf16),
            shape((2 * ROWS * HEADS, DV), f32),
        ),
        scratch_shapes=[
            buffer(state),
            pltpu.VMEM((ROWS, SLOT, DV), bf16),
            found,
            pltpu.VMEM((ROWS, 5 * HEADS, DV), f32),
            pltpu.VMEM((count, 1, DV), jnp.int32),
            pltpu.SMEM((count, 1, DV), jnp.int32),
            pltpu.SemaphoreType.DMA((1,)),
            pltpu.SemaphoreType.DMA((ROWS,)),
            pltpu.SemaphoreType.DMA((count,)),
        ],
        compiler_params=PARAMS,
        name="fill_slots",
    )(parents, *early, tails, in_hbm(state))


def second_half(parents, late, conv, early, slots, w_out):
    window = pltpu.VMEM(((TAPS - 1) * ROWS * HEADS, DV), f32)
    rows, width = 4 * ROWS, w_out.shape[1] // PARTS
    *sums, update, last, memory = pl.pallas_call(
        second_kernel,
        in_specs=[SMEM] + [VMEM] * 8 + [HBM] * 2,
        out_specs=[VMEM] * (PARTS + 3),
        out_shape=(
            shape((rows, width), f32),
            *[shape((rows, width), bf16)] * (PARTS - 1),
            shape((ROWS, 5 * HEADS, DV), f32),
            shape((ROWS, SLIM, DV), bf16),
            shape((ROWS, BODY, DV), bf16),
        ),
        scratch_shapes=[
            pltpu.VMEM((ROWS, SLOT - BODY, DV), bf16),
            window,
            window,
            window,
            *work_buffers(),
            pltpu.VMEM((PARTS, w_out.shape[0], width), bf16),
            pltpu.VMEM((rows, HEADS * DV), bf16),
            pltpu.SemaphoreType.DMA((ROWS,)),
            pltpu.SemaphoreType.DMA((ROWS,)),
            pltpu.SemaphoreType.DMA((PARTS,)),
        ],
        compiler_params=PARAMS,
        name="second_half",
    )(parents, *late, conv, early, in_hbm(slots), in_hbm(w_out))
    return sums, update, last, memory


def last_memory(update, last, raw, memory):
    tails = [shape((TAPS - 1, ROWS, width), bf16) for width in (KEYS * DK, KEYS * DK, HEADS * DV)]
    return pl.pallas_call(
        final_kernel,
        in_specs=[VMEM] * 4,
        out_specs=[HBM] * 4,
        out_shape=(shape((ROWS, BODY, DV), bf16), *tails),
        scratch_shapes=[
            buffer(memory),
            pltpu.VMEM((ROWS * SLIM, DV), f32),
            *[buffer(tail) for tail in tails],
            pltpu.SemaphoreType.DMA((ROWS,)),
            pltpu.SemaphoreType.DMA((3,)),
        ],
        compiler_params=PARAMS,
        name="last_memory",
    )(update, last, raw, memory)


def sum_heads(blocks):
    total = blocks[0]
    for shift in (1, 3, 2):
        pairs = [(i, (i + shift) % PARTS) for i in range(PARTS)]
        total = total + lax.ppermute(blocks[shift], "tensor", pairs).astype(f32)
    return total.astype(bf16)


def per_device(
    inputs,
    w_query,
    w_key,
    w_value,
    w_gate_z,
    w_beta,
    w_decay,
    conv_query,
    conv_key,
    conv_value,
    decay_log,
    dt_bias,
    norm_gain,
    w_out,
    state,
    tail_query,
    tail_key,
    tail_value,
    parents,
):
    groups = lax.axis_size("branch")
    asked = jnp.broadcast_to(parents[None, None, :], (groups, 1, ROWS))
    asked = lax.all_to_all(asked, "branch", split_axis=0, concat_axis=0, tiled=True)

    flat_state = state.reshape(ROWS, BODY, DV)
    (
        late_query, late_key, late_value, *scales, raw, stored_tails, conv, vectors, values
    ) = first_half(
        (
            inputs.reshape(-1, inputs.shape[-1]),
            norm_gain[None],
            tail_query.transpose(1, 0, 2),
            tail_key.transpose(1, 0, 2),
            tail_value.transpose(1, 0, 2),
            conv_query,
            conv_key,
            conv_value,
            w_query,
            w_key,
            w_value,
            w_gate_z,
            w_beta.T,
            w_decay.T,
            decay_log,
            dt_bias,
        )
    )
    shipped, early = fill_slots(asked, (vectors, values, *scales[:2]), stored_tails, flat_state)
    arrived = lax.all_to_all(shipped, "branch", split_axis=0, concat_axis=0, tiled=True)
    late = (late_query, late_key, late_value, *scales[2:])
    sums, update, last, memory = second_half(
        parents, late, conv, early, arrived, w_out
    )
    out_rows = sum_heads(sums).reshape(inputs.shape[0], ROWS, -1)
    final_state, *final_tails = last_memory(update, last, raw, memory)
    return (
        out_rows,
        final_state.reshape(state.shape),
        *[tail.transpose(1, 0, 2) for tail in final_tails],
    )


def solution(mesh):
    return jax.shard_map(
        per_device,
        mesh=mesh,
        in_specs=(
            P(None, "branch", None),
            P(None, "tensor"),
            P(None, "tensor"),
            P(None, "tensor"),
            P(None, "tensor"),
            P(None, "tensor"),
            P(None, "tensor"),
            P(None, "tensor"),
            P(None, "tensor"),
            P(None, "tensor"),
            P("tensor"),
            P("tensor"),
            P(),
            P("tensor", None),
            P("branch", "tensor", None, None),
            P("branch", None, "tensor"),
            P("branch", None, "tensor"),
            P("branch", None, "tensor"),
            P("branch"),
        ),
        out_specs=(
            P(None, "branch", "tensor"),
            P("branch", "tensor", None, None),
            P("branch", None, "tensor"),
            P("branch", None, "tensor"),
            P("branch", None, "tensor"),
        ),
        check_vma=False,
    )
```

```python
import jax
import jax.numpy as jnp
from jax import lax
from jax.experimental import pallas as pl
from jax.experimental.pallas import tpu as pltpu
from jax.sharding import PartitionSpec as P

DK = 128
DV = 128
HEADS = 8
KEYS = 4
ROWS = 16
TAPS = 4
WIDE = 3 * HEADS
SLIM = 2 * KEYS + HEADS
BODY = HEADS * DK
SLOT = BODY + (TAPS - 1) * SLIM
VMEM_BYTES = 48 * 1024 * 1024
CHUNK = 4
PARTS = 4
GROUP = 8
LATE = 16
AHEAD = 2
SHIP = 4
f32 = jnp.float32
bf16 = jnp.bfloat16


def split(value):
    high = value.astype(bf16).astype(f32)
    return high, value - high


def dot(left, right):
    return jnp.dot(left, right, preferred_element_type=f32)


def inner(left, right):
    return jnp.sum(left * right, axis=-1, keepdims=True)


def widening():
    row = lax.broadcasted_iota(jnp.int32, ((TAPS - 1) * WIDE, (TAPS - 1) * SLIM), 0)
    column = lax.broadcasted_iota(jnp.int32, ((TAPS - 1) * WIDE, (TAPS - 1) * SLIM), 1)
    tap, place = row // WIDE, row % WIDE
    origin = tap * SLIM + jnp.where(place < 2 * HEADS, place // 2, place - HEADS)
    return jnp.where(origin == column, 1.0, 0.0).astype(bf16)


def spread(target, start, h, block):
    target[pl.ds(start * HEADS + h, block.shape[0], stride=HEADS), :] = block


def part_of(ref, index, first, count):
    return ref[pl.ds(index * ROWS * HEADS + first * HEADS, count * HEADS), :]


def find_vectors(window, conv_ref, vector_buf, value_buf):
    for first in range(0, ROWS, CHUNK):
        there = slice(first, first + CHUNK)
        for step in range(2):
            for kind in range(3):
                mixed = 0.0
                for tap in range(TAPS):
                    rows = window(kind, step + tap, first).reshape(CHUNK, HEADS, DV)
                    mixed = mixed + rows * conv_ref[kind, tap][None]
                mixed = mixed * jax.nn.sigmoid(mixed)
                if kind == 2:
                    value_buf[step, there] = mixed
                    continue
                unit = mixed * lax.rsqrt(inner(mixed, mixed) + 1e-06)
                if kind == 0:
                    unit = unit * DK ** (-0.5)
                place = 2 * step + 1 - kind
                vector_buf[there, place * HEADS : (place + 1) * HEADS, :] = unit


def recall(rows, memory, vector_buf, found_buf):
    head = lax.broadcasted_iota(jnp.int32, (HEADS, DV), 0)
    for row in rows:
        high, low = split(vector_buf[row])
        left = jnp.concatenate([high, low], axis=0).astype(bf16)
        found = [jnp.zeros((HEADS, DV), f32)] * 4
        for h in range(0, HEADS, 2):
            pair = jnp.concatenate([memory(row, h), memory(row, h + 1)], axis=1)
            product = dot(left, pair)
            product = product[: 4 * HEADS] + product[4 * HEADS :]
            for i in range(4):
                block = product[i * HEADS : (i + 1) * HEADS]
                found[i] = jnp.where(head == h, block[:, :DV], found[i])
                found[i] = jnp.where(head == h + 1, block[:, DV:], found[i])
        found_buf[row] = jnp.concatenate(found, axis=0)


def finish(first, strengths, decays, vector_buf, value_buf, found_buf, normed_buf, update_buf):
    there = slice(first, first + CHUNK)

    def piece(ref, i):
        return ref[there, i * HEADS : (i + 1) * HEADS, :]

    def steps(ref):
        return [part_of(ref, step, first, CHUNK).reshape(CHUNK, HEADS, DV) for step in range(2)]

    key0, query0, key1, query1 = [piece(vector_buf, i) for i in range(4)]
    found0, found1, found2, found3 = [piece(found_buf, i) for i in range(4)]
    strength0, strength1 = steps(strengths)
    decay0, decay1 = steps(decays)
    change0 = (value_buf[0, there] - decay0 * found0) * strength0
    read0 = decay0 * found1 + inner(query0, key0) * change0
    kept = decay0 * found2 + inner(key1, key0) * change0
    change1 = (value_buf[1, there] - decay1 * kept) * strength1
    kept = decay0 * found3 + inner(query1, key0) * change0
    read1 = decay1 * kept + inner(query1, key1) * change1
    for step, read in enumerate((read0, read1)):
        scale = lax.rsqrt(jnp.mean(read * read, axis=-1, keepdims=True) + 1e-06)
        start = (step * ROWS + first) * HEADS
        normed_buf[start : start + CHUNK * HEADS, :] = (read * scale).reshape(CHUNK * HEADS, DV)
    for i, value in enumerate((key0, key1, decay1 * change0, change1, decay0 * decay1)):
        update_buf[there, i * HEADS : (i + 1) * HEADS, :] = value


def flatten_heads(normed_buf, gate_buf, first, normed_ref):
    for h in range(HEADS):
        normed = normed_buf[pl.ds(h, 2 * ROWS, stride=HEADS), :]
        gate = gate_buf[pl.ds(first * HEADS + h, 2 * ROWS, stride=HEADS), :]
        normed_ref[first : first + 2 * ROWS, h * DV : (h + 1) * DV] = (normed * gate).astype(bf16)


def write_row(update, memory, store):
    key0, key1, change0, change1, decay = [
        update[i * HEADS : (i + 1) * HEADS] for i in range(5)
    ]
    (key0h, key0l), (key1h, key1l) = split(key0), split(key1)
    (change0h, change0l), (change1h, change1l) = split(change0), split(change1)
    left = jnp.concatenate([key0h, key0l, key0h, key1h, key1l, key1h], axis=0)
    left = left.T.astype(bf16)
    right = jnp.concatenate([change0h, change0h, change0l, change1h, change1h, change1l], axis=0)
    head = lax.broadcasted_iota(jnp.int32, right.shape, 0) % HEADS
    for h in range(0, HEADS, 2):
        pair = [jnp.where(head == h + i, right, 0.0).astype(bf16) for i in range(2)]
        added = dot(left, jnp.concatenate(pair, axis=1))
        for i in range(2):
            kept = memory(h + i).astype(f32) * decay[h + i : h + i + 1]
            store(h + i, (kept + added[:, i * DV : (i + 1) * DV]).astype(bf16))


def write_rows(rows, update_buf, memory, target_ref):
    for row in rows:

        def store(h, value, row=row):
            target_ref[row, h * DK : (h + 1) * DK, :] = value

        write_row(update_buf[row], lambda h, row=row: memory(row, h), store)


def first_kernel(
    x, gain, tail_query, tail_key, tail_value, conv_query, conv_key, conv_value,
    w_query, w_key, w_value, w_gate, w_beta, w_decay, decay_log, dt_bias,
    late_query_ref, late_key_ref, late_value_ref,
    early_strength_ref, early_forget_ref, late_strength_ref, late_forget_ref,
    gate_ref, raw_ref, stored_ref, conv_ref, vector_ref, value_ref,
    x_buf, gain_buf, tail_query_buf, tail_key_buf, tail_value_buf,
    conv_query_buf, conv_key_buf, conv_value_buf,
    query_buf, key_buf, value_buf, gate_buf, beta_buf, decay_buf, decay_ref, bias_ref,
    window_query, window_key, window_value, strength_all, forget_all, stored_buf,
    small_sem, weight_sem,
):
    rows = x_buf.shape[0]
    small = [
        pltpu.make_async_copy(source, target, small_sem.at[i])
        for i, (source, target) in enumerate(
            (
                (x, x_buf),
                (w_beta, beta_buf),
                (w_decay, decay_buf),
                (gain, gain_buf),
                (tail_query, tail_query_buf),
                (tail_key, tail_key_buf),
                (tail_value, tail_value_buf),
                (conv_query, conv_query_buf),
                (conv_key, conv_key_buf),
                (conv_value, conv_value_buf),
                (decay_log, decay_ref),
                (dt_bias, bias_ref),
            )
        )
    ]
    for copy in small:
        copy.start()

    def weights(j):
        pieces = (
            (w_query, query_buf, DK),
            (w_key, key_buf, DK),
            (w_value, value_buf, 2 * DV),
            (w_gate, gate_buf, 2 * DV),
        )
        copies = []
        for i, (hbm, buf, width) in enumerate(pieces):
            part = pl.ds(j * width, width)
            copies.append(
                pltpu.make_async_copy(hbm.at[:, part], buf.at[:, part], weight_sem.at[4 * j + i])
            )
        return copies

    def begin(j):
        for copy in weights(j):
            copy.start()

    for j in range(AHEAD):
        begin(j)

    for copy in small:
        copy.wait()
    head = lax.broadcasted_iota(jnp.int32, (HEADS, DV), 0)
    rate, bias = jnp.zeros((HEADS, DV), f32), jnp.zeros((HEADS, DV), f32)
    for h in range(HEADS):
        rate = jnp.where(head == h, decay_ref[h], rate)
        bias = jnp.where(head == h, bias_ref[h], bias)
    rate = -jnp.exp(rate)
    x_all = x_buf[...]

    across = (((1,), (1,)), ((), ()))
    beta = lax.dot_general(x_all, beta_buf[...], across, preferred_element_type=f32)
    decay = lax.dot_general(x_all, decay_buf[...], across, preferred_element_type=f32)
    for h in range(HEADS):
        spread(strength_all, 0, h, jnp.broadcast_to(beta[:, h : h + 1], (rows, DV)))
        spread(forget_all, 0, h, jnp.broadcast_to(decay[:, h : h + 1], (rows, DV)))
    for first in range(0, rows, ROWS):
        there = slice(first * HEADS, (first + ROWS) * HEADS)
        strength_all[there] = jax.nn.sigmoid(strength_all[there])
        raised = forget_all[there].reshape(ROWS, HEADS, DV) + bias[None]
        forget = jnp.exp(rate[None] * jax.nn.softplus(raised))
        forget_all[there] = forget.reshape(ROWS * HEADS, DV)

    history = (TAPS - 1) * ROWS

    def place(window, h, before, fresh):
        spread(window, 0, h, before)
        spread(window, history, h, fresh)

    def keep(channel, before, fresh):
        after = jnp.concatenate([before[2 * ROWS :], fresh[: 2 * ROWS]], axis=0)
        for tap in range(TAPS - 1):
            stored_buf[pl.ds(tap * SLIM + channel, ROWS, stride=(TAPS - 1) * SLIM), :] = after[
                tap * ROWS : (tap + 1) * ROWS
            ]

    for kind, buf in enumerate((conv_query_buf, conv_key_buf, conv_value_buf)):
        wide = buf[...].astype(f32)
        for h in range(HEADS):
            channel = h if kind == 2 else h // 2
            taps = wide[:, channel * DV : (channel + 1) * DV]
            for tap in range(TAPS):
                conv_ref[kind, tap, h : h + 1, :] = taps[tap : tap + 1]

    for j in range(KEYS):
        for copy in weights(j):
            copy.wait()
        if j + AHEAD < KEYS:
            begin(j + AHEAD)
        one, two = slice(j * DK, (j + 1) * DK), slice(2 * j * DV, 2 * (j + 1) * DV)
        query = dot(x_all, query_buf[:, one]).astype(bf16)
        key = dot(x_all, key_buf[:, one]).astype(bf16)
        value = dot(x_all, value_buf[:, two]).astype(bf16)
        gate = dot(x_all, gate_buf[:, two])
        gate = gate * jax.nn.sigmoid(gate)
        raw_ref[:, j * DK : (j + 1) * DK] = query[2 * ROWS :]
        raw_ref[:, (KEYS + j) * DK : (KEYS + j + 1) * DK] = key[2 * ROWS :]
        raw_ref[:, 2 * (KEYS + j) * DK : 2 * (KEYS + j + 1) * DK] = value[2 * ROWS :]
        query, key, value = query.astype(f32), key.astype(f32), value.astype(f32)
        old_query = tail_query_buf[:, :, one].reshape(history, DK).astype(f32)
        old_key = tail_key_buf[:, :, one].reshape(history, DK).astype(f32)
        old_value = tail_value_buf[:, :, two].reshape(history, 2 * DV).astype(f32)
        keep(j, old_query, query)
        keep(KEYS + j, old_key, key)
        for i in range(2):
            h, half = 2 * j + i, slice(i * DV, (i + 1) * DV)
            place(window_query, h, old_query, query)
            place(window_key, h, old_key, key)
            place(window_value, h, old_value[:, half], value[:, half])
            keep(2 * KEYS + h, old_value[:, half], value[:, half])
            spread(gate_ref, 0, h, gate[:, half] * gain_buf[...])

    late = (history + 2 * ROWS) * HEADS
    late_query_ref[...] = window_query[late:, :].astype(bf16)
    late_key_ref[...] = window_key[late:, :].astype(bf16)
    late_value_ref[...] = window_value[late:, :].astype(bf16)
    half = 2 * ROWS * HEADS
    for value, early_ref, late_ref in (
        (strength_all, early_strength_ref, late_strength_ref),
        (forget_all, early_forget_ref, late_forget_ref),
    ):
        early_ref[...] = value[:half, :]
        late_ref[...] = value[half:, :]
    stored_ref[...] = stored_buf[...].reshape(stored_ref.shape).astype(bf16)
    windows = (window_query, window_key, window_value)
    find_vectors(
        lambda kind, tap, first: part_of(windows[kind], tap, first, CHUNK),
        conv_ref,
        vector_ref,
        value_ref,
    )


def send_kernel(
    parent_ref, vector_ref, value_ref, strength_ref, forget_ref, tails_ref, state,
    slots, normed_buf,
    state_buf, stored_buf, found_buf, update_buf, wanted_buf, wanted_ref,
    look_sem, state_sem, slot_sem,
):
    count = slots.shape[0]

    def load(row):
        return pltpu.make_async_copy(state.at[row], state_buf.at[row], state_sem.at[row])

    for row in range(2 * SHIP):
        load(row).start()
    parent = parent_ref[...]
    mine = parent // ROWS == lax.axis_index("branch")
    wanted = jnp.max(jnp.where(mine, parent % ROWS, -1).astype(f32), axis=-1, keepdims=True)
    wanted_buf[...] = jnp.broadcast_to(wanted.astype(jnp.int32), wanted_buf.shape)
    look = pltpu.make_async_copy(wanted_buf, wanted_ref, look_sem.at[0])
    look.start()
    for row in range(ROWS):
        stored_buf[row, BODY:, :] = tails_ref[row]

    def ship(slot, row):
        return pltpu.make_async_copy(stored_buf.at[row], slots.at[slot], slot_sem.at[slot])

    def memory(row, h):
        return state_buf[row, h * DK : (h + 1) * DK, :]

    for start in range(0, ROWS, SHIP):
        rows = range(start, start + SHIP)
        for row in rows:
            load(row).wait()
        for row in range(start + 2 * SHIP, min(start + 3 * SHIP, ROWS)):
            load(row).start()
        recall(rows, memory, vector_ref, found_buf)
        for first in range(start, start + SHIP, CHUNK):
            finish(
                first, strength_ref, forget_ref,
                vector_ref, value_ref, found_buf, normed_buf, update_buf,
            )
        write_rows(rows, update_buf, memory, stored_buf)

        if start == 0:
            look.wait()

        def begin(slot, carry, start=start):
            row = wanted_ref[slot, 0, 0]

            @pl.when((row >= start) & (row < start + SHIP))
            def _():
                ship(slot, row).start()

            return carry

        lax.fori_loop(0, count, begin, 0, unroll=count)
    def end(slot, carry):
        @pl.when(wanted_ref[slot, 0, 0] >= 0)
        def _():
            ship(slot, 0).wait()

        return carry

    lax.fori_loop(0, count, end, 0, unroll=count)


def second_kernel(
    parent_ref, late_query, late_key, late_value, late_strength, late_forget, gate_ref, conv_ref,
    early_ref, slots, w_out,
    *refs,
):
    sums = refs[:PARTS]
    (
        update_ref, last_ref, memory_buf,
        tail_buf, window_query, window_key, window_value,
        vector_buf, value_buf, found_buf, normed_buf, out_buf, normed_ref,
        tail_sem, memory_sem, out_sem,
    ) = refs[PARTS:]
    def load_tail(row):
        return pltpu.make_async_copy(
            slots.at[parent_ref[row] // ROWS, pl.ds(BODY, SLOT - BODY)], tail_buf.at[row], tail_sem.at[row]
        )

    def load(row):
        return pltpu.make_async_copy(
            slots.at[parent_ref[row] // ROWS, pl.ds(0, BODY)], memory_buf.at[row], memory_sem.at[row]
        )

    for row in range(ROWS):
        load_tail(row).start()
    for row in range(ROWS):
        load(row).start()
    width = out_buf.shape[2]
    place = lax.axis_index("tensor")

    def load_out(shift):
        start = pl.multiple_of((place + shift) % PARTS * width, width)
        return pltpu.make_async_copy(
            w_out.at[:, pl.ds(start, width)], out_buf.at[shift], out_sem.at[shift]
        )

    wide = widening()
    flatten_heads(early_ref, gate_ref, 0, normed_ref)
    for row in range(ROWS):
        load_tail(row).wait()
    for row in range(ROWS):
        tails = tail_buf[row]
        last_ref[row] = tails[2 * SLIM :]
        spaced = dot(wide, tails)
        for tap in range(TAPS - 1):
            for kind, window in enumerate((window_query, window_key, window_value)):
                start = tap * WIDE + kind * HEADS
                window[(tap * ROWS + row) * HEADS : (tap * ROWS + row + 1) * HEADS, :] = spaced[
                    start : start + HEADS
                ]
    windows = (window_query, window_key, window_value)
    fresh = (late_query, late_key, late_value)

    def window(kind, tap, first):
        if tap < TAPS - 1:
            return part_of(windows[kind], tap, first, CHUNK)
        return part_of(fresh[kind], tap - (TAPS - 1), first, CHUNK).astype(f32)

    find_vectors(window, conv_ref, vector_buf, value_buf)
    for shift in range(PARTS):
        load_out(shift).start()

    def group(index, carry):
        rows = [index * LATE + i for i in range(LATE)]
        for row in rows:
            load(row).wait()
        recall(rows, lambda row, h: memory_buf[row, h * DK : (h + 1) * DK, :], vector_buf, found_buf)
        return carry

    lax.fori_loop(0, ROWS // LATE, group, 0)
    for first in range(0, ROWS, CHUNK):
        finish(
            first, late_strength, late_forget,
            vector_buf, value_buf, found_buf, normed_buf, update_ref,
        )
    flatten_heads(normed_buf, gate_ref, 2 * ROWS, normed_ref)
    for shift in range(PARTS):
        load_out(shift).wait()
    normed = normed_ref[...]
    for shift in range(PARTS):
        sums[shift][...] = dot(normed, out_buf[shift]).astype(sums[shift].dtype)


def final_kernel(
    update_ref, last_ref, raw_ref, memory_ref,
    final, query, key, value,
    final_buf, last_buf, query_buf, key_buf, value_buf, final_sem, tail_sem,
):
    def save(row):
        return pltpu.make_async_copy(final_buf.at[row], final.at[row], final_sem.at[row])

    start = 0
    last_buf[...] = last_ref[...].astype(f32).reshape(ROWS * SLIM, DV)
    tails = []
    for i, (ref, target) in enumerate(((query_buf, query), (key_buf, key), (value_buf, value))):
        width = ref.shape[2]
        for channel in range(width // DV):
            block = last_buf[pl.ds(start // DV + channel, ROWS, stride=SLIM), :]
            ref[0, :, channel * DV : (channel + 1) * DV] = block.astype(bf16)
        for step in range(2):
            ref[1 + step] = raw_ref[step * ROWS : (step + 1) * ROWS, start : start + width]
        start += width
        tails.append(pltpu.make_async_copy(ref, target, tail_sem.at[i]))
        tails[i].start()

    def group(index, carry):
        rows = [index * GROUP + i for i in range(GROUP)]
        write_rows(
            rows, update_ref, lambda row, h: memory_ref[row, h * DK : (h + 1) * DK, :], final_buf
        )
        for row in rows:
            save(row).start()
        return carry

    lax.fori_loop(0, ROWS // GROUP, group, 0)
    for copy in tails:
        copy.wait()
    for row in range(ROWS):
        save(row).wait()


VMEM = pl.BlockSpec(memory_space=pltpu.VMEM)
SMEM = pl.BlockSpec(memory_space=pltpu.SMEM)
HBM = pl.BlockSpec(memory_space=pltpu.HBM)
PARAMS = pltpu.CompilerParams(vmem_limit_bytes=VMEM_BYTES)


def in_hbm(array):
    return pltpu.with_memory_space_constraint(array, pltpu.HBM)


def shape(dims, kind):
    return jax.ShapeDtypeStruct(dims, kind)


def buffer(array):
    return pltpu.VMEM(array.shape, array.dtype)


def work_buffers():
    return [
        pltpu.VMEM((ROWS, 4 * HEADS, DV), f32),
        pltpu.VMEM((2, ROWS, HEADS, DV), f32),
        pltpu.VMEM((ROWS, 4 * HEADS, DV), f32),
        pltpu.VMEM((2 * ROWS * HEADS, DV), f32),
    ]


def first_half(arrays):
    rows = arrays[0].shape[0]
    half = rows // 2
    window = pltpu.VMEM(((TAPS - 1) * ROWS * HEADS + rows * HEADS, DV), f32)
    wide = pltpu.VMEM((rows * HEADS, DV), f32)
    return pl.pallas_call(
        first_kernel,
        in_specs=[HBM] * len(arrays),
        out_specs=[VMEM] * 13,
        out_shape=(
            *[shape((half * HEADS, DV), bf16)] * 3,
            *[shape((half * HEADS, DV), f32)] * 4,
            shape((rows * HEADS, DV), f32),
            shape((half, SLIM * DV), bf16),
            shape((ROWS, (TAPS - 1) * SLIM, DV), bf16),
            shape((3, TAPS, HEADS, DV), f32),
            shape((ROWS, 4 * HEADS, DV), f32),
            shape((2, ROWS, HEADS, DV), f32),
        ),
        scratch_shapes=[
            *[buffer(array) for array in arrays[:-2]],
            *[pltpu.SMEM(array.shape, f32) for array in arrays[-2:]],
            window,
            window,
            window,
            wide,
            wide,
            pltpu.VMEM((ROWS * (TAPS - 1) * SLIM, DV), f32),
            pltpu.SemaphoreType.DMA((len(arrays) - 4,)),
            pltpu.SemaphoreType.DMA((4 * KEYS,)),
        ],
        compiler_params=PARAMS,
        name="first_half",
    )(*[in_hbm(array) for array in arrays])


def fill_slots(parents, early, tails, state):
    count = parents.shape[0]
    _, _, found, _ = work_buffers()
    return pl.pallas_call(
        send_kernel,
        in_specs=[VMEM] * 6 + [HBM],
        out_specs=[HBM, VMEM],
        out_shape=(
            shape((count, SLOT, DV), bf16),
            shape((2 * ROWS * HEADS, DV), f32),
        ),
        scratch_shapes=[
            buffer(state),
            pltpu.VMEM((ROWS, SLOT, DV), bf16),
            found,
            pltpu.VMEM((ROWS, 5 * HEADS, DV), f32),
            pltpu.VMEM((count, 1, DV), jnp.int32),
            pltpu.SMEM((count, 1, DV), jnp.int32),
            pltpu.SemaphoreType.DMA((1,)),
            pltpu.SemaphoreType.DMA((ROWS,)),
            pltpu.SemaphoreType.DMA((count,)),
        ],
        compiler_params=PARAMS,
        name="fill_slots",
    )(parents, *early, tails, in_hbm(state))


def second_half(parents, late, conv, early, slots, w_out):
    window = pltpu.VMEM(((TAPS - 1) * ROWS * HEADS, DV), f32)
    rows, width = 4 * ROWS, w_out.shape[1] // PARTS
    *sums, update, last, memory = pl.pallas_call(
        second_kernel,
        in_specs=[SMEM] + [VMEM] * 8 + [HBM] * 2,
        out_specs=[VMEM] * (PARTS + 3),
        out_shape=(
            shape((rows, width), f32),
            *[shape((rows, width), bf16)] * (PARTS - 1),
            shape((ROWS, 5 * HEADS, DV), f32),
            shape((ROWS, SLIM, DV), bf16),
            shape((ROWS, BODY, DV), bf16),
        ),
        scratch_shapes=[
            pltpu.VMEM((ROWS, SLOT - BODY, DV), bf16),
            window,
            window,
            window,
            *work_buffers(),
            pltpu.VMEM((PARTS, w_out.shape[0], width), bf16),
            pltpu.VMEM((rows, HEADS * DV), bf16),
            pltpu.SemaphoreType.DMA((ROWS,)),
            pltpu.SemaphoreType.DMA((ROWS,)),
            pltpu.SemaphoreType.DMA((PARTS,)),
        ],
        compiler_params=PARAMS,
        name="second_half",
    )(parents, *late, conv, early, in_hbm(slots), in_hbm(w_out))
    return sums, update, last, memory


def last_memory(update, last, raw, memory):
    tails = [shape((TAPS - 1, ROWS, width), bf16) for width in (KEYS * DK, KEYS * DK, HEADS * DV)]
    return pl.pallas_call(
        final_kernel,
        in_specs=[VMEM] * 4,
        out_specs=[HBM] * 4,
        out_shape=(shape((ROWS, BODY, DV), bf16), *tails),
        scratch_shapes=[
            buffer(memory),
            pltpu.VMEM((ROWS * SLIM, DV), f32),
            *[buffer(tail) for tail in tails],
            pltpu.SemaphoreType.DMA((ROWS,)),
            pltpu.SemaphoreType.DMA((3,)),
        ],
        compiler_params=PARAMS,
        name="last_memory",
    )(update, last, raw, memory)


def sum_heads(blocks):
    total = blocks[0]
    for shift in (1, 3, 2):
        pairs = [(i, (i + shift) % PARTS) for i in range(PARTS)]
        total = total + lax.ppermute(blocks[shift], "tensor", pairs).astype(f32)
    return total.astype(bf16)


def per_device(
    inputs,
    w_query,
    w_key,
    w_value,
    w_gate_z,
    w_beta,
    w_decay,
    conv_query,
    conv_key,
    conv_value,
    decay_log,
    dt_bias,
    norm_gain,
    w_out,
    state,
    tail_query,
    tail_key,
    tail_value,
    parents,
):
    groups = lax.axis_size("branch")
    asked = jnp.broadcast_to(parents[None, None, :], (groups, 1, ROWS))
    asked = lax.all_to_all(asked, "branch", split_axis=0, concat_axis=0, tiled=True)

    flat_state = state.reshape(ROWS, BODY, DV)
    (
        late_query, late_key, late_value, *scales, raw, stored_tails, conv, vectors, values
    ) = first_half(
        (
            inputs.reshape(-1, inputs.shape[-1]),
            norm_gain[None],
            tail_query.transpose(1, 0, 2),
            tail_key.transpose(1, 0, 2),
            tail_value.transpose(1, 0, 2),
            conv_query,
            conv_key,
            conv_value,
            w_query,
            w_key,
            w_value,
            w_gate_z,
            w_beta.T,
            w_decay.T,
            decay_log,
            dt_bias,
        )
    )
    shipped, early = fill_slots(asked, (vectors, values, *scales[:2]), stored_tails, flat_state)
    arrived = lax.all_to_all(shipped, "branch", split_axis=0, concat_axis=0, tiled=True)
    late = (late_query, late_key, late_value, *scales[2:])
    sums, update, last, memory = second_half(
        parents, late, conv, early, arrived, w_out
    )
    out_rows = sum_heads(sums).reshape(inputs.shape[0], ROWS, -1)
    final_state, *final_tails = last_memory(update, last, raw, memory)
    return (
        out_rows,
        final_state.reshape(state.shape),
        *[tail.transpose(1, 0, 2) for tail in final_tails],
    )


def solution(mesh):
    return jax.shard_map(
        per_device,
        mesh=mesh,
        in_specs=(
            P(None, "branch", None),
            P(None, "tensor"),
            P(None, "tensor"),
            P(None, "tensor"),
            P(None, "tensor"),
            P(None, "tensor"),
            P(None, "tensor"),
            P(None, "tensor"),
            P(None, "tensor"),
            P(None, "tensor"),
            P("tensor"),
            P("tensor"),
            P(),
            P("tensor", None),
            P("branch", "tensor", None, None),
            P("branch", None, "tensor"),
            P("branch", None, "tensor"),
            P("branch", None, "tensor"),
            P("branch"),
        ),
        out_specs=(
            P(None, "branch", "tensor"),
            P("branch", "tensor", None, None),
            P("branch", None, "tensor"),
            P("branch", None, "tensor"),
            P("branch", None, "tensor"),
        ),
        check_vma=False,
    )
```
